128 devices in a mesh: img: 32 (over y, x, core), ch: 4 (over z).
Axes of the slice: x: 4, y: 4, z: 4, core: 2. Of those that a mesh axis runs over, the one named last changes fastest.
Arguments:
- canvas: bfloat16 [1024, 32, 1536], P('img', None, 'ch'), may hold values from -6 to 6
- screen_size: int32 [32, 2], P('img'), may hold values from 8 to 32, as said below
- tile_counts: int32 [32], replicated, may hold values from 1 to 32, 512 in all
- tile_offsets: int32 [1024, 2], P('img'), may hold values from 0 to 28, as said below
- cotangent: bfloat16 [1024, 4, 4, 1536], P('img', None, None, 'ch'), may hold values from -6 to 6
- dw_kernel: bfloat16 [49, 1536], P(None, 'ch'), may hold values from -0.875 to 0.875
- dw_bias: float32 [1536], P('ch'), may hold values from -3 to 3
- ln_gain: float32 [1536], replicated, may hold values from 0.5 to 1.5
- ln_bias: float32 [1536], replicated, may hold values from -0.5 to 0.5
- w_in: bfloat16 [1536, 6144], P(None, 'ch'), may hold values from -0.15625 to 0.15625
- b_in: float32 [6144], P('ch'), may hold values from -1 to 1
- w_out: bfloat16 [6144, 1536], P('ch'), may hold values from -0.078125 to 0.078125
- layer_scale: float32 [1536], replicated, may hold values from 0.25 to 2
Outputs:
- grad_canvas: float32 [1024, 32, 1536], P('img', None, 'ch')
The draws below stay inside these ranges and needn't reach their ends.
Inputs may be any that keep to these rules, and one draw needn't show every extreme that they name: `tile_counts`: the counts sum to 512 and the largest is exactly 32. `screen_size`: some screenshot is 32 by 32 cells. `tile_offsets`: every slot's interior lies inside its screenshot.
All inputs are finite; a program needn't handle non-finite values.
Results may differ from the reference program's by a relative error of at most 0.0031.
Values may be sent and summed in bfloat16 or wider, within the bound.
No kernel may reach another device: no remote copies, remote signals or barrier semaphores. Data moves between devices by JAX's collectives and lax.ppermute only.
A program may use at most 128 MiB of HBM per device.

```python
import math
import jax
import jax.numpy as jnp
import numpy as np
from jax import lax

C = 1536
HID = 6144
TS = 4
CANVAS = 32
MOST = 32
TILES_DEV = 16
N_IMG = 32


def screen_table(key):
    screens = jax.random.randint(jax.random.fold_in(key, 11), (N_IMG, 2), 2 * TS, CANVAS + 1)
    biggest = jax.random.randint(jax.random.fold_in(key, 12), (), 0, N_IMG)
    owner_index = jnp.arange(N_IMG)[:, None]
    return jnp.where(owner_index == biggest, CANVAS, screens).astype(jnp.int32)


def draw_screen_size(key, part):
    return screen_table(key)


def draw_tile_offsets(key, part):
    screens = screen_table(key)
    upper_bound = screens - TS + 1
    row_start = jax.random.randint(jax.random.fold_in(key, 13), (N_IMG, MOST), 0, upper_bound[:, 0:1])
    col_start = jax.random.randint(jax.random.fold_in(key, 14), (N_IMG, MOST), 0, upper_bound[:, 1:2])
    return jnp.stack([row_start, col_start], axis=2).reshape(N_IMG * MOST, 2).astype(jnp.int32)


def level_of(rng, dims, pieces, smallest, top_value):
    level, own = 1.0, jax.random.fold_in(rng, 6)
    for position, shards_of in pieces:
        heights = jnp.exp(jax.random.uniform(jax.random.fold_in(own, position), (shards_of,), jnp.float32, smallest / len(pieces), top_value / len(pieces)))
        level = level * jnp.repeat(heights, dims[position] // shards_of).reshape([-1 if axis == position else 1 for axis in range(len(dims))])
    return level


def profile(amount, total, limit, skew):
    portions = [(1 << 20) // math.isqrt(standing ** skew) + 1 for standing in range(2, amount + 1)]
    spare, holding = total - limit - (amount - 1), [1] * (amount - 1)
    while spare > 0:
        movable = [i for i in range(amount - 1) if holding[i] < limit]
        whole, left = sum([portions[i] for i in movable]), spare
        for i in movable:
            extra = min(limit - holding[i], max(1, left * portions[i] // whole), spare)
            holding[i] = holding[i] + extra
            spare = spare - extra
    return np.array([limit] + holding)


def uneven(stream_key, count, total, bound, lean):
    if count == 2:
        one = jax.random.randint(stream_key, (), max(1, total - bound), min(bound, total - 1) + 1)
        return jnp.stack([one, total - one])
    lengths = jnp.asarray(profile(count, total, bound, lean), jnp.int32)
    twos = (count - 1) // 2
    source_of, receiver = lengths[1:1 + 2 * twos:2], lengths[2:2 + 2 * twos:2]
    room = jnp.minimum(source_of - 1, bound - receiver)
    shifted = jax.random.randint(jax.random.fold_in(stream_key, 1), (twos,), 0, 1 << 20) % (room + 1)
    lengths = lengths.at[1:1 + 2 * twos:2].set(source_of - shifted).at[2:2 + 2 * twos:2].set(receiver + shifted)
    return lengths[jax.random.permutation(jax.random.fold_in(stream_key, 2), count)]


def scatter_about(key, shape, deviation, limit, cuts=(), kind=jnp.bfloat16):
    level = level_of(key, shape, cuts, -0.22, 0.18) if cuts else 1.0
    drawn = jax.random.normal(key, shape, jnp.float32) * deviation * level
    return jnp.minimum(jnp.maximum(drawn, -limit), limit).astype(kind)


def setup_inputs(seed: int = 0) -> dict:
    keys = jax.random.split(jax.random.key(seed), 14)
    return {
        "canvas": scatter_about(keys[0], (N_IMG * CANVAS, CANVAS, C), 1.0, 6.0, ((0, 32), (2, 4))),
        "screen_size": draw_screen_size(jax.random.fold_in(keys[13], 71), 0),
        "tile_counts": uneven(keys[2], N_IMG, TILES_DEV * N_IMG, MOST, 2).astype(jnp.int32),
        "tile_offsets": draw_tile_offsets(jax.random.fold_in(keys[13], 71), 0),
        "cotangent": scatter_about(keys[4], (N_IMG * MOST, TS, TS, C), 1.0, 6.0, ((0, 32), (3, 4))),
        "dw_kernel": scatter_about(keys[5], (49, C), 49 ** -0.5, 0.875, ((1, 4),)),
        "dw_bias": scatter_about(keys[6], (C,), 0.5, 3.0, ((0, 4),), jnp.float32),
        "ln_gain": jnp.clip(1.0 + 0.1 * jax.random.normal(keys[7], (C,), jnp.float32), 0.5, 1.5),
        "ln_bias": jnp.clip(jax.random.uniform(keys[8], (C,), jnp.float32, -0.5, 0.5), -0.5, 0.5),
        "w_in": scatter_about(keys[9], (C, HID), C ** -0.5, 0.15625, ((1, 4),)),
        "b_in": jnp.clip(jax.random.uniform(keys[10], (HID,), jnp.float32, -1.0, 1.0) * level_of(keys[10], (HID,), ((0, 4),), -0.4, 0.0), -1.0, 1.0),
        "w_out": scatter_about(keys[11], (HID, C), HID ** -0.5, 0.078125, ((0, 4),)),
        "layer_scale": jnp.clip(jnp.exp(jax.random.uniform(keys[12], (C,), jnp.float32, math.log(0.25), math.log(2.0))), 0.25, 2.0),
    }


slope_coef = 0.7978845608
cubic_coef = 0.044715
norm_eps = 1e-06

def gelu_slope(pre_act):
    inner_arg = slope_coef * (pre_act + cubic_coef * pre_act * pre_act * pre_act)
    tangent = jnp.tanh(inner_arg)
    return 0.5 * (1.0 + tangent) + 0.5 * pre_act * (1.0 - tangent * tangent) * slope_coef * (1.0 + 3.0 * cubic_coef * pre_act * pre_act)

def depthwise(patches, kernel, bias):
    result = jnp.zeros((patches.shape[0], TS, TS, patches.shape[3]), jnp.float32) + bias.astype(jnp.float32)
    for offset_r in range(7):
        for offset_c in range(7):
            result = result + patches[:, offset_r:offset_r + TS, offset_c:offset_c + TS, :].astype(jnp.float32) * kernel[offset_r * 7 + offset_c].astype(jnp.float32)
    return result

def depthwise_back(upstream, kernel):
    result = jnp.zeros((upstream.shape[0], TS + 6, TS + 6, upstream.shape[3]), jnp.float32)
    for offset_r in range(7):
        for offset_c in range(7):
            result = result.at[:, offset_r:offset_r + TS, offset_c:offset_c + TS, :].add(upstream * kernel[offset_r * 7 + offset_c].astype(jnp.float32))
    return result

def tile_gradients(patches, cot_tiles, dw_kernel, dw_bias, ln_gain, ln_bias, w_in, b_in, w_out, layer_scale):
    count_tiles = patches.shape[0]
    row_count = count_tiles * TS * TS
    mixed = depthwise(patches, dw_kernel, dw_bias).astype(jnp.bfloat16)
    values = mixed.astype(jnp.float32)
    center = lax.optimization_barrier(jnp.mean(values, axis=3, keepdims=True))
    spread = lax.optimization_barrier(jnp.mean(jnp.square(values - center), axis=3, keepdims=True))
    inv_std = lax.rsqrt(spread + norm_eps)
    normed = (values - center) * inv_std
    scaled = (normed * ln_gain + ln_bias).astype(jnp.bfloat16)
    pre_act = jnp.dot(scaled.reshape(row_count, C), w_in, preferred_element_type=jnp.float32) + b_in
    out_grad = (layer_scale * cot_tiles.astype(jnp.float32)).astype(jnp.bfloat16).reshape(row_count, C)
    hidden_grad = lax.dot_general(out_grad, w_out, (((1,), (1,)), ((), ())), preferred_element_type=jnp.float32)
    act_grad = (hidden_grad * gelu_slope(pre_act)).astype(jnp.bfloat16)
    norm_grad = lax.dot_general(act_grad, w_in, (((1,), (1,)), ((), ())), preferred_element_type=jnp.float32)
    weighted = norm_grad.reshape(count_tiles, TS, TS, C) * ln_gain
    upstream = inv_std * (weighted - lax.optimization_barrier(jnp.mean(weighted, axis=3, keepdims=True)) - normed * lax.optimization_barrier(jnp.mean(weighted * normed, axis=3, keepdims=True)))
    tile_grad = depthwise_back(upstream, dw_kernel)
    return tile_grad.at[:, 3:3 + TS, 3:3 + TS, :].add(cot_tiles.astype(jnp.float32))

def reference(canvas, screen_size, tile_counts, tile_offsets, cotangent, dw_kernel, dw_bias, ln_gain, ln_bias, w_in, b_in, w_out, layer_scale):
    canvases = canvas.reshape(N_IMG, CANVAS, CANVAS, C)
    offsets_all = tile_offsets.reshape(N_IMG, MOST, 2)
    cot_all = cotangent.reshape(N_IMG, MOST, TS, TS, C)

    def one_screen(packed):
        sheet, extent, corners, cot_tiles, listed = packed
        lines = jnp.arange(CANVAS, dtype=jnp.int32)
        inside = (lines[:, None] < extent[0]) & (lines[None, :] < extent[1])
        masked = jnp.where(inside[:, :, None], sheet, jnp.zeros_like(sheet))
        framed = jnp.pad(masked, ((3, 3), (3, 3), (0, 0)))
        patches = jax.vmap(lambda corner: lax.dynamic_slice(framed, (corner[0], corner[1], jnp.int32(0)), (TS + 6, TS + 6, C)))(corners)
        grads = tile_gradients(patches, cot_tiles, dw_kernel, dw_bias, ln_gain, ln_bias, w_in, b_in, w_out, layer_scale)
        listed_mask = (jnp.arange(MOST, dtype=jnp.int32) < listed).astype(jnp.float32)
        grads = grads * listed_mask[:, None, None, None]
        span = jnp.arange(TS + 6, dtype=jnp.int32)
        row_index = corners[:, 0][:, None, None] + span[None, :, None]
        col_index = corners[:, 1][:, None, None] + span[None, None, :]
        total = jnp.zeros((CANVAS + 6, CANVAS + 6, C), jnp.float32).at[row_index, col_index].add(grads)
        cropped = total[3:3 + CANVAS, 3:3 + CANVAS, :]
        return jnp.where(inside[:, :, None], cropped, jnp.zeros_like(cropped))
    result = lax.map(one_screen, (canvases, screen_size, offsets_all, cot_all, tile_counts))
    return result.reshape(N_IMG * CANVAS, CANVAS, C)
```

```python
import functools

import jax
import jax.numpy as jnp
from jax import lax
from jax.experimental import pallas as pl
from jax.experimental.pallas import tpu as pltpu
from jax.sharding import PartitionSpec as P

TS = 4
SIDE = 32
PAD_ROWS = 38
PAD_COLS = 48
LEFT = 8

slope_coef = 0.7978845608
cubic_coef = 0.044715
norm_eps = 1e-06

VMEM = pl.BlockSpec(memory_space=pltpu.VMEM)
SMEM = pl.BlockSpec(memory_space=pltpu.SMEM)
LIMIT = 56 * 1024 * 1024


def call(kernel, out_shape, in_specs, scratch=()):
    many = isinstance(out_shape, (list, tuple))
    return pl.pallas_call(
        kernel,
        out_shape=out_shape,
        in_specs=in_specs,
        out_specs=[VMEM] * len(out_shape) if many else VMEM,
        scratch_shapes=list(scratch),
        compiler_params=pltpu.CompilerParams(vmem_limit_bytes=LIMIT),
    )


def inside_of(rows, row, height, width):
    column = lax.broadcasted_iota(jnp.int32, (rows, 128), 0)
    return (column < width) & (row < height)


def depthwise_kernel(offsets, screen, canvas, dwk, bias, mixed, framed, taps):
    lanes = canvas.shape[2] // 128
    height, width = screen[0, 0], screen[0, 1]
    low = lax.broadcasted_iota(jnp.int32, (8, 128), 0) < 4
    for b in range(lanes):
        cut = slice(b * 128, (b + 1) * 128)
        blank = jnp.zeros((PAD_COLS, 128), jnp.float32)
        for y in (0, 1, 2, SIDE + 3, SIDE + 4, SIDE + 5):
            framed[b, y] = blank

        def fill(y, carry):
            framed[b, y + 3, 0:LEFT, :] = blank[:LEFT]
            framed[b, y + 3, LEFT + SIDE : PAD_COLS, :] = blank[: PAD_COLS - LEFT - SIDE]
            row = canvas[y, :, cut].astype(jnp.float32)
            framed[b, y + 3, LEFT : LEFT + SIDE, :] = jnp.where(
                inside_of(SIDE, y, height, width), row, 0.0
            )
            return carry

        lax.fori_loop(0, SIDE, fill, 0, unroll=2)
        kern = dwk[:, cut].astype(jnp.float32)
        for i in range(7):
            for j in range(4):
                first = jnp.broadcast_to(kern[7 * i + j][None], (8, 128))
                if j < 3:
                    second = jnp.broadcast_to(kern[7 * i + j + 4][None], (8, 128))
                else:
                    second = jnp.zeros((8, 128), jnp.float32)
                taps[i * 4 + j] = jnp.where(low, first, second)
        start = jnp.broadcast_to(bias[:, cut], (8, 128))

        def tile(t, carry):
            r, q = offsets[t, 0], offsets[t, 1]
            sums = [None] * 4
            for p in range(10):
                for j in range(4):
                    seen = framed[b, r + p, pl.ds(q + (LEFT - 3 + j), 8), :]
                    for y in range(max(0, p - 6), min(3, p) + 1):
                        term = seen * taps[(p - y) * 4 + j]
                        sums[y] = term if sums[y] is None else sums[y] + term
            folded = [s + pltpu.roll(s, 4, 0) + start for s in sums]
            pair = [jnp.where(low, folded[y], folded[y + 1]) for y in (0, 2)]
            rows = pl.ds(pl.multiple_of(t * 16, 16), 16)
            mixed[rows, cut] = jnp.concatenate(pair, 0).astype(jnp.bfloat16)
            return carry

        lax.fori_loop(0, offsets.shape[0], tile, 0)


def assemble(full, place, blocks, change):
    own, left, right, opp_a, opp_b = blocks
    share = own.shape[1]
    half = opp_a.shape[0]
    rows = own.shape[0]
    for ref, shift, span in (
        (own, 0, (0, rows)),
        (left, 3, (0, rows)),
        (right, 1, (0, rows)),
        (opp_a, 2, (0, half)),
        (opp_b, 2, (half, rows)),
    ):
        begin = pl.multiple_of(lax.rem(place + shift, 4) * share, 128)
        full[span[0] : span[1], pl.ds(begin, share)] = change(ref[...], begin, share)


def hidden_kernel(place, own, left, right, opp_a, opp_b, scale, w_out, hidden, full):
    def scaled(block, begin, share):
        return (scale[:, pl.ds(begin, share)] * block.astype(jnp.float32)).astype(jnp.bfloat16)

    assemble(full, place[0], (own, left, right, opp_a, opp_b), scaled)
    step = 512
    for n in range(0, hidden.shape[1], step):
        hidden[:, n : n + step] = lax.dot_general(
            full[...],
            w_out[n : n + step, :],
            (((1,), (1,)), ((), ())),
            preferred_element_type=jnp.float32,
        )


def gelu_slope(v):
    square = v * v
    t = jnp.tanh(slope_coef * (v + cubic_coef * square * v))
    return 0.5 * (1.0 + t) + 0.5 * v * (1.0 - t * t) * slope_coef * (1.0 + 3.0 * cubic_coef * square)


def as_rows(column):
    count = column.shape[0] // 128
    eye = lax.broadcasted_iota(jnp.int32, (128, 128), 0) == lax.broadcasted_iota(jnp.int32, (128, 128), 1)
    return jnp.concatenate(
        [
            jnp.sum(jnp.where(eye, column[g * 128 : (g + 1) * 128], 0.0), axis=0, keepdims=True)
            for g in range(count)
        ],
        0,
    )


def as_column(rows):
    eye = lax.broadcasted_iota(jnp.int32, (128, 128), 0) == lax.broadcasted_iota(jnp.int32, (128, 128), 1)
    return jnp.concatenate(
        [
            jnp.sum(jnp.where(eye, rows[g : g + 1], 0.0), axis=1, keepdims=True)
            for g in range(rows.shape[0])
        ],
        0,
    )


def block_kernel(
    place, own, left, right, opp_a, opp_b, gain, bias, w_in, b_in, hidden,
    to_right, to_left, next_right, next_left, mine, centers, inverses, full, scaled, act,
):
    rows, width = full.shape
    share = own.shape[1]
    half = rows // 2
    assemble(full, place[0], (own, left, right, opp_a, opp_b), lambda block, begin, share: block)
    step = 64
    for m in range(0, rows, step):
        values = full[m : m + step, :].astype(jnp.float32)
        center = jnp.mean(values, axis=1, keepdims=True)
        apart = values - center
        inverse = lax.rsqrt(jnp.mean(apart * apart, axis=1, keepdims=True) + norm_eps)
        centers[m : m + step, :] = center
        inverses[m : m + step, :] = inverse
        scaled[m : m + step, :] = (apart * inverse * gain[...] + bias[...]).astype(jnp.bfloat16)
    step = 512
    for n in range(0, width, step):
        pre = jnp.dot(scaled[...], w_in[:, n : n + step], preferred_element_type=jnp.float32)
        pre = pre + b_in[:, n : n + step]
        act[:, n : n + step] = (hidden[:, n : n + step] * gelu_slope(pre)).astype(jnp.bfloat16)
    first = jnp.zeros((rows, 1), jnp.float32)
    second = jnp.zeros((rows, 1), jnp.float32)
    for shift in (2, 1, 3, 0):
        begin = pl.multiple_of(lax.rem(place[0] + shift, 4) * share, 128)
        part = lax.dot_general(
            act[...],
            w_in[pl.ds(begin, share), :],
            (((1,), (1,)), ((), ())),
            preferred_element_type=jnp.float32,
        )
        if shift == 2:
            to_right[:half, :] = part[:half].astype(jnp.bfloat16)
            to_left[:half, :] = part[half:].astype(jnp.bfloat16)
        elif shift == 1:
            next_right[...] = part.astype(jnp.bfloat16)
        elif shift == 3:
            next_left[...] = part.astype(jnp.bfloat16)
        else:
            mine[...] = part
        weighted = part * gain[:, pl.ds(begin, share)]
        normed = (full[:, pl.ds(begin, share)].astype(jnp.float32) - centers[...]) * inverses[...]
        first = first + jnp.sum(weighted, axis=1, keepdims=True)
        second = second + jnp.sum(weighted * normed, axis=1, keepdims=True)
    packed = []
    for column in (first, second):
        line = as_rows(column)
        high = line.astype(jnp.bfloat16).astype(jnp.float32)
        packed += [high, line - high]
    sums = jnp.concatenate(packed, 0).astype(jnp.bfloat16)
    for out in (to_right, to_left):
        out[half : half + 16, :] = jnp.zeros((16, share), jnp.bfloat16)
        out[half : half + 16, :128] = sums


def middle_kernel(from_left, from_right, next_right, next_left, go_right, go_left):
    rows = next_right.shape[0]
    half = rows // 2

    def add(a, b):
        return (a.astype(jnp.float32) + b.astype(jnp.float32)).astype(jnp.bfloat16)

    go_right[:half, :] = add(next_right[:half, :], from_left[:half, :])
    go_right[half:rows, :] = next_right[half:, :]
    go_right[rows : rows + 16, :] = from_left[half : half + 16, :]
    go_left[:half, :] = next_left[:half, :]
    go_left[half:, :] = add(next_left[half:, :], from_right[:half, :])


def canvas_kernel(
    place, offsets, screen, counts,
    mine, got_left, got_right, from_left, from_right, to_right, mixed, centers, inverses, gain, cot, dwk,
    grad, upstream, grown, taken, taps,
):
    rows, share = mixed.shape
    half = rows // 2
    lanes = share // 128
    total = gain.shape[1]
    height, width = screen[0, 0], screen[0, 1]
    listed = counts[0, place[1]]
    begin = pl.multiple_of(place[0] * share, 128)
    packed = (
        to_right[half : half + 16, :128].astype(jnp.float32)
        + from_left[half : half + 16, :128].astype(jnp.float32)
        + from_right[half : half + 16, :128].astype(jnp.float32)
        + got_left[rows : rows + 16, :128].astype(jnp.float32)
    )
    first = as_column((packed[0:4] + packed[4:8]) * (1.0 / total))
    second = as_column((packed[8:12] + packed[12:16]) * (1.0 / total))
    step = 64
    for m in range(0, rows, step):
        span = slice(m, m + step)
        norm_grad = (
            mine[span, :]
            + got_left[span, :].astype(jnp.float32)
            + got_right[span, :].astype(jnp.float32)
        )
        inverse = inverses[span, :]
        normed = (mixed[span, :].astype(jnp.float32) - centers[span, :]) * inverse
        weighted = norm_grad * gain[:, pl.ds(begin, share)]
        upstream[span, :] = inverse * (weighted - first[span] - normed * second[span])

    low = lax.broadcasted_iota(jnp.int32, (8, 128), 0) < 4
    grown[...] = jnp.zeros_like(grown)
    taken[...] = jnp.zeros_like(taken)

    def tile(t, carry):
        r, q = offsets[t, 0], offsets[t, 1]
        for b in range(lanes):
            cut = slice(b * 128, (b + 1) * 128)
            span = pl.ds(pl.multiple_of(t * 16, 16), 16)
            up = upstream[span, cut]
            direct = cot[span, cut].astype(jnp.float32)
            for values, canvas, top in ((up, grown, 3), (direct, taken, 0)):
                for y in range(4):
                    pair = values[8 * (y // 2) : 8 * (y // 2) + 8]
                    pair = pltpu.roll(pair, 4, 0) if y % 2 else pair
                    columns = pl.ds(q + LEFT, 8)
                    canvas[b, r + top + y, columns, :] += jnp.where(low, pair, 0.0)
        return carry

    lax.fori_loop(0, listed, tile, 0)
    pairs = 2
    for b in range(lanes):
        cut = slice(b * 128, (b + 1) * 128)
        kern = dwk[:, cut].astype(jnp.float32)
        for k in range(49):
            taps[k] = jnp.broadcast_to(kern[k][None], (8, 128))

        def line(step, carry):
            y = step * pairs
            sums = [[None] * 4 for _ in range(pairs)]
            for p in range(6 + pairs):
                for j in range(7):
                    seen = [
                        grown[b, y + p, LEFT + 3 - j + 8 * x : LEFT + 3 - j + 8 * x + 8, :]
                        for x in range(4)
                    ]
                    for d in range(pairs):
                        i = 6 + d - p
                        if 0 <= i < 7:
                            tap = taps[7 * i + j]
                            for x in range(4):
                                term = seen[x] * tap
                                sums[d][x] = term if sums[d][x] is None else sums[d][x] + term
            for d in range(pairs):
                whole = jnp.concatenate(sums[d], 0) + taken[b, y + d, LEFT : LEFT + SIDE, :]
                grad[y + d, :, cut] = jnp.where(inside_of(SIDE, y + d, height, width), whole, 0.0)
            return carry

        lax.fori_loop(0, SIDE // pairs, line, 0)


def shift(x, by):
    n = lax.axis_size("ch")
    return lax.ppermute(x, "ch", [(i, (i + by) % n) for i in range(n)])


def ring_gather(x):
    half = x.shape[0] // 2
    left, right = shift(x, 1), shift(x, -1)
    return x, left, right, shift(left[:half], 1), shift(right[half:], -1)


def shards(
    canvas,
    screen_size,
    tile_counts,
    tile_offsets,
    cotangent,
    dw_kernel,
    dw_bias,
    ln_gain,
    ln_bias,
    w_in,
    b_in,
    w_out,
    layer_scale,
):
    f32, bf16 = jnp.float32, jnp.bfloat16
    struct = jax.ShapeDtypeStruct
    slots = tile_offsets.shape[0]
    share = canvas.shape[2]
    width = ln_gain.shape[0]
    hid = w_in.shape[1]
    rows = slots * TS * TS
    half = rows // 2
    lanes = share // 128
    place = jnp.stack([lax.axis_index("ch"), lax.axis_index("img")]).astype(jnp.int32)
    line = lambda v: v.reshape(1, -1)

    cot = cotangent.reshape(rows, share)
    cots = ring_gather(cot)
    mixed = call(
        depthwise_kernel,
        struct((rows, share), bf16),
        [SMEM, SMEM, VMEM, VMEM, VMEM],
        [
            pltpu.VMEM((lanes, PAD_ROWS, PAD_COLS, 128), f32),
            pltpu.VMEM((28, 8, 128), f32),
        ],
    )(tile_offsets, screen_size, canvas, dw_kernel, line(dw_bias))
    mixes = ring_gather(mixed)
    hidden = call(
        hidden_kernel,
        struct((rows, hid), f32),
        [SMEM] + [VMEM] * 7,
        [pltpu.VMEM((rows, width), bf16)],
    )(place, *cots, line(layer_scale), w_out)
    to_right, to_left, next_right, next_left, mine, centers, inverses = call(
        block_kernel,
        [
            struct((half + 16, share), bf16),
            struct((half + 16, share), bf16),
            struct((rows, share), bf16),
            struct((rows, share), bf16),
            struct((rows, share), f32),
            struct((rows, 1), f32),
            struct((rows, 1), f32),
        ],
        [SMEM] + [VMEM] * 10,
        [
            pltpu.VMEM((rows, width), bf16),
            pltpu.VMEM((rows, width), bf16),
            pltpu.VMEM((rows, hid), bf16),
        ],
    )(place, *mixes, line(ln_gain), line(ln_bias), w_in, line(b_in), hidden)
    from_left, from_right = shift(to_right, 1), shift(to_left, -1)
    go_right, go_left = call(
        middle_kernel,
        [struct((rows + 16, share), bf16), struct((rows, share), bf16)],
        [VMEM] * 4,
    )(from_left, from_right, next_right, next_left)
    got_left, got_right = shift(go_right, 1), shift(go_left, -1)
    return call(
        canvas_kernel,
        struct(canvas.shape, f32),
        [SMEM] * 4 + [VMEM] * 12,
        [
            pltpu.VMEM((rows, share), f32),
            pltpu.VMEM((lanes, PAD_ROWS, PAD_COLS, 128), f32),
            pltpu.VMEM((lanes, SIDE, PAD_COLS, 128), f32),
            pltpu.VMEM((49, 8, 128), f32),
        ],
    )(
        place, tile_offsets, screen_size, line(tile_counts),
        mine, got_left, got_right, from_left, from_right, to_right, mixed, centers, inverses,
        line(ln_gain), cot, dw_kernel,
    )


def solution(mesh):
    return jax.shard_map(
        shards,
        mesh=mesh,
        in_specs=(
            P("img", None, "ch"),
            P("img", None),
            P(),
            P("img", None),
            P("img", None, None, "ch"),
            P(None, "ch"),
            P("ch"),
            P(),
            P(),
            P(None, "ch"),
            P("ch"),
            P("ch", None),
            P(),
        ),
        out_specs=P("img", None, "ch"),
        check_vma=False,
    )
```

```python
import functools

import jax
import jax.numpy as jnp
from jax import lax
from jax.experimental import pallas as pl
from jax.experimental.pallas import tpu as pltpu
from jax.sharding import PartitionSpec as P

TS = 4
SIDE = 32
PAD_ROWS = 38
PAD_COLS = 48
LEFT = 8

slope_coef = 0.7978845608
cubic_coef = 0.044715
norm_eps = 1e-06

VMEM = pl.BlockSpec(memory_space=pltpu.VMEM)
SMEM = pl.BlockSpec(memory_space=pltpu.SMEM)
HBM = pl.BlockSpec(memory_space=pltpu.HBM)


def call(kernel, out_shape, in_specs, scratch=(), limit=16, out_specs=None):
    run = pl.pallas_call(
        kernel,
        out_shape=out_shape,
        in_specs=in_specs,
        out_specs=out_specs or [VMEM] * len(out_shape),
        scratch_shapes=list(scratch),
        compiler_params=pltpu.CompilerParams(vmem_limit_bytes=limit << 20),
    )

    def held(*args):
        return run(
            *(
                pltpu.with_memory_space_constraint(a, pltpu.VMEM if spec is VMEM else pltpu.HBM)
                for spec, a in zip(in_specs, args, strict=True)
            )
        )

    return held


def inside_of(rows, row, height, width):
    column = lax.broadcasted_iota(jnp.int32, (rows, 128), 0)
    return (column < width) & (row < height)


def depthwise_kernel(
    offsets, screen, canvas, dwk, bias, w_in, w_out, mixed, near_in, near_out, framed, taps, sems
):
    fetches = [
        pltpu.make_async_copy(w_out, near_out, sems.at[0]),
        pltpu.make_async_copy(w_in, near_in, sems.at[1]),
    ]
    for fetch in fetches:
        fetch.start()
    lanes = canvas.shape[2] // 128
    height, width = screen[0, 0], screen[0, 1]
    low = lax.broadcasted_iota(jnp.int32, (8, 128), 0) < 4
    for b in range(lanes):
        cut = slice(b * 128, (b + 1) * 128)
        blank = jnp.zeros((PAD_COLS, 128), jnp.float32)
        for y in (0, 1, 2, SIDE + 3, SIDE + 4, SIDE + 5):
            framed[b, y] = blank

        def fill(y, carry):
            framed[b, y + 3, 0:LEFT, :] = blank[:LEFT]
            framed[b, y + 3, LEFT + SIDE : PAD_COLS, :] = blank[: PAD_COLS - LEFT - SIDE]
            row = canvas[y, :, cut].astype(jnp.float32)
            framed[b, y + 3, LEFT : LEFT + SIDE, :] = jnp.where(
                inside_of(SIDE, y, height, width), row, 0.0
            )
            return carry

        lax.fori_loop(0, SIDE, fill, 0, unroll=2)
        kern = dwk[:, cut].astype(jnp.float32)
        for i in range(7):
            for j in range(4):
                first = jnp.broadcast_to(kern[7 * i + j][None], (8, 128))
                if j < 3:
                    second = jnp.broadcast_to(kern[7 * i + j + 4][None], (8, 128))
                else:
                    second = jnp.zeros((8, 128), jnp.float32)
                taps[i * 4 + j] = jnp.where(low, first, second)
        start = jnp.broadcast_to(bias[cut][None], (8, 128))

        def tile(t, carry):
            r, q = offsets[0, t], offsets[1, t]
            sums = [None] * 4
            for p in range(10):
                for j in range(4):
                    seen = framed[b, r + p, pl.ds(q + (LEFT - 3 + j), 8), :]
                    for y in range(max(0, p - 6), min(3, p) + 1):
                        term = seen * taps[(p - y) * 4 + j]
                        sums[y] = term if sums[y] is None else sums[y] + term
            folded = [s + pltpu.roll(s, 4, 0) + start for s in sums]
            pair = [jnp.where(low, folded[y], folded[y + 1]) for y in (0, 2)]
            rows = pl.ds(pl.multiple_of(t * 16, 16), 16)
            mixed[rows, cut] = jnp.concatenate(pair, 0).astype(jnp.bfloat16)
            return carry

        lax.fori_loop(0, offsets.shape[1], tile, 0)
    for fetch in fetches:
        fetch.wait()


def assemble(full, blocks, change):
    own, left, right, opp_a, opp_b = blocks
    place = lax.axis_index("ch")
    share = own.shape[1]
    half = opp_a.shape[0]
    rows = own.shape[0]
    for ref, shift, span in (
        (own, 0, (0, rows)),
        (left, 3, (0, rows)),
        (right, 1, (0, rows)),
        (opp_a, 2, (0, half)),
        (opp_b, 2, (half, rows)),
    ):
        begin = pl.multiple_of(lax.rem(place + shift, 4) * share, 128)
        full[span[0] : span[1], pl.ds(begin, share)] = change(ref[...], begin, share)


def place_tiles(offsets, listed, values, canvas, top):
    low = lax.broadcasted_iota(jnp.int32, (8, 128), 0) < 4

    def tile(t, carry):
        r, q = offsets[0, t], offsets[1, t]
        columns = pl.ds(q + LEFT, 8)
        span = pl.ds(pl.multiple_of(t * 16, 16), 16)
        for b in range(values.shape[1] // 128):
            cells = values[span, b * 128 : (b + 1) * 128].astype(jnp.float32)
            for y in range(4):
                pair = cells[8 * (y // 2) : 8 * (y // 2) + 8]
                pair = pltpu.roll(pair, 4, 0) if y % 2 else pair
                canvas[b, r + top + y, columns, :] += jnp.where(low, pair, 0.0)
        return carry

    lax.fori_loop(0, listed, tile, 0)


def hidden_kernel(
    offsets, counts, own, left, right, opp_a, opp_b, scale, w_out, hidden, taken, full
):
    def scaled(block, begin, share):
        return (scale[pl.ds(begin, share)][None] * block.astype(jnp.float32)).astype(jnp.bfloat16)

    taken[...] = jnp.zeros_like(taken)
    place_tiles(offsets, counts[lax.axis_index("img")], own, taken, 0)
    assemble(full, (own, left, right, opp_a, opp_b), scaled)
    step = 512
    for n in range(0, hidden.shape[1], step):
        hidden[:, n : n + step] = lax.dot_general(
            full[...],
            w_out[n : n + step, :],
            (((1,), (1,)), ((), ())),
            preferred_element_type=jnp.float32,
        )


def gelu_slope(v):
    square = v * v
    t = jnp.tanh(slope_coef * (v + cubic_coef * square * v))
    return 0.5 * (1.0 + t) + 0.5 * v * (1.0 - t * t) * slope_coef * (1.0 + 3.0 * cubic_coef * square)


def as_rows(column):
    count = column.shape[0] // 128
    eye = lax.broadcasted_iota(jnp.int32, (128, 128), 0) == lax.broadcasted_iota(jnp.int32, (128, 128), 1)
    return jnp.concatenate(
        [
            jnp.sum(jnp.where(eye, column[g * 128 : (g + 1) * 128], 0.0), axis=0, keepdims=True)
            for g in range(count)
        ],
        0,
    )


def as_column(rows):
    eye = lax.broadcasted_iota(jnp.int32, (128, 128), 0) == lax.broadcasted_iota(jnp.int32, (128, 128), 1)
    return jnp.concatenate(
        [
            jnp.sum(jnp.where(eye, rows[g : g + 1], 0.0), axis=1, keepdims=True)
            for g in range(rows.shape[0])
        ],
        0,
    )


def block_kernel(
    own, left, right, opp_a, opp_b, gain, bias, w_in, b_in, hidden,
    to_right, to_left, next_right, next_left, mine, centers, inverses, full, scaled, act,
):
    rows, width = full.shape
    share = own.shape[1]
    place = lax.axis_index("ch")
    half = rows // 2
    assemble(full, (own, left, right, opp_a, opp_b), lambda block, begin, share: block)
    step = 64
    for m in range(0, rows, step):
        values = full[m : m + step, :].astype(jnp.float32)
        center = jnp.mean(values, axis=1, keepdims=True)
        apart = values - center
        inverse = lax.rsqrt(jnp.mean(apart * apart, axis=1, keepdims=True) + norm_eps)
        centers[m : m + step, :] = center
        inverses[m : m + step, :] = inverse
        scaled[m : m + step, :] = (apart * inverse * gain[...][None] + bias[...][None]).astype(jnp.bfloat16)
    step = 512
    for n in range(0, width, step):
        pre = jnp.dot(scaled[...], w_in[:, n : n + step], preferred_element_type=jnp.float32)
        pre = pre + b_in[n : n + step][None]
        act[:, n : n + step] = (hidden[:, n : n + step] * gelu_slope(pre)).astype(jnp.bfloat16)
    first = jnp.zeros((rows, 1), jnp.float32)
    second = jnp.zeros((rows, 1), jnp.float32)
    for shift in (2, 1, 3, 0):
        begin = pl.multiple_of(lax.rem(place + shift, 4) * share, 128)
        part = lax.dot_general(
            act[...],
            w_in[pl.ds(begin, share), :],
            (((1,), (1,)), ((), ())),
            preferred_element_type=jnp.float32,
        )
        if shift == 2:
            to_right[:half, :] = part[:half].astype(jnp.bfloat16)
            to_left[:half, :] = part[half:].astype(jnp.bfloat16)
        elif shift == 1:
            next_right[...] = part.astype(jnp.bfloat16)
        elif shift == 3:
            next_left[...] = part.astype(jnp.bfloat16)
        else:
            mine[...] = part
        weighted = part * gain[pl.ds(begin, share)][None]
        normed = (full[:, pl.ds(begin, share)].astype(jnp.float32) - centers[...]) * inverses[...]
        first = first + jnp.sum(weighted, axis=1, keepdims=True)
        second = second + jnp.sum(weighted * normed, axis=1, keepdims=True)
    packed = []
    for column in (first, second):
        line = as_rows(column)
        high = line.astype(jnp.bfloat16).astype(jnp.float32)
        packed += [high, line - high]
    sums = jnp.concatenate(packed, 0).astype(jnp.bfloat16)
    for out in (to_right, to_left):
        out[half : half + 16, :] = jnp.zeros((16, share), jnp.bfloat16)
        out[half : half + 16, :128] = sums


def middle_kernel(from_left, from_right, next_right, next_left, go_right, go_left):
    rows = next_right.shape[0]
    half = rows // 2

    def add(a, b):
        return (a.astype(jnp.float32) + b.astype(jnp.float32)).astype(jnp.bfloat16)

    go_right[:half, :] = add(next_right[:half, :], from_left[:half, :])
    go_right[half:rows, :] = next_right[half:, :]
    go_right[rows : rows + 16, :] = from_left[half : half + 16, :]
    go_left[:half, :] = next_left[:half, :]
    go_left[half:, :] = add(next_left[half:, :], from_right[:half, :])


def canvas_kernel(
    offsets, screen, counts,
    mine, got_left, got_right, from_left, from_right, to_right, mixed, centers, inverses, gain, taken, dwk,
    grad, upstream, grown, taps, stage, sems,
):
    rows, share = mixed.shape
    half = rows // 2
    lanes = share // 128
    total = gain.shape[0]
    height, width = screen[0, 0], screen[0, 1]
    begin = pl.multiple_of(lax.axis_index("ch") * share, 128)
    packed = (
        to_right[half : half + 16, :128].astype(jnp.float32)
        + from_left[half : half + 16, :128].astype(jnp.float32)
        + from_right[half : half + 16, :128].astype(jnp.float32)
        + got_left[rows : rows + 16, :128].astype(jnp.float32)
    )
    first = as_column((packed[0:4] + packed[4:8]) * (1.0 / total))
    second = as_column((packed[8:12] + packed[12:16]) * (1.0 / total))
    step = 64
    for m in range(0, rows, step):
        span = slice(m, m + step)
        norm_grad = (
            mine[span, :]
            + got_left[span, :].astype(jnp.float32)
            + got_right[span, :].astype(jnp.float32)
        )
        inverse = inverses[span, :]
        normed = (mixed[span, :].astype(jnp.float32) - centers[span, :]) * inverse
        weighted = norm_grad * gain[pl.ds(begin, share)][None]
        upstream[span, :] = inverse * (weighted - first[span] - normed * second[span])

    grown[...] = jnp.zeros_like(grown)
    place_tiles(offsets, counts[lax.axis_index("img")], upstream, grown, 3)
    stores = []
    pairs = 2
    for b in range(lanes):
        cut = slice(b * 128, (b + 1) * 128)
        kern = dwk[:, cut].astype(jnp.float32)
        for k in range(49):
            taps[k] = jnp.broadcast_to(kern[k][None], (8, 128))

        def line(step, carry):
            y = step * pairs
            sums = [[None] * 4 for _ in range(pairs)]
            for p in range(6 + pairs):
                for j in range(7):
                    seen = [
                        grown[b, y + p, LEFT + 3 - j + 8 * x : LEFT + 3 - j + 8 * x + 8, :]
                        for x in range(4)
                    ]
                    for d in range(pairs):
                        i = 6 + d - p
                        if 0 <= i < 7:
                            tap = taps[7 * i + j]
                            for x in range(4):
                                term = seen[x] * tap
                                sums[d][x] = term if sums[d][x] is None else sums[d][x] + term
            for d in range(pairs):
                whole = jnp.concatenate(sums[d], 0) + taken[b, y + d, LEFT : LEFT + SIDE, :]
                stage[y + d, :, cut] = jnp.where(inside_of(SIDE, y + d, height, width), whole, 0.0)
            return carry

        lax.fori_loop(0, SIDE // pairs, line, 0)
        store = pltpu.make_async_copy(stage.at[:, :, cut], grad.at[:, :, cut], sems.at[b])
        store.start()
        stores.append(store)
    for store in stores:
        store.wait()


def shift(x, by):
    n = lax.axis_size("ch")
    return lax.ppermute(x, "ch", [(i, (i + by) % n) for i in range(n)])


def ring_gather(x):
    half = x.shape[0] // 2
    left, right = shift(x, 1), shift(x, -1)
    return x, left, right, shift(left[:half], 1), shift(right[half:], -1)


def shards(
    canvas,
    screen_size,
    tile_counts,
    tile_offsets,
    cotangent,
    dw_kernel,
    dw_bias,
    ln_gain,
    ln_bias,
    w_in,
    b_in,
    w_out,
    layer_scale,
):
    f32, bf16 = jnp.float32, jnp.bfloat16
    struct = pltpu.VMEM
    slots = tile_offsets.shape[0]
    share = canvas.shape[2]
    width = ln_gain.shape[0]
    hid = w_in.shape[1]
    rows = slots * TS * TS
    half = rows // 2
    lanes = share // 128
    offsets = tile_offsets.T
    cot = cotangent.reshape(rows, share)
    cots = ring_gather(cot)
    mixed, near_in, near_out = call(
        depthwise_kernel,
        [struct((rows, share), bf16), struct(w_in.shape, bf16), struct(w_out.shape, bf16)],
        [SMEM, SMEM, VMEM, VMEM, VMEM, HBM, HBM],
        [
            pltpu.VMEM((lanes, PAD_ROWS, PAD_COLS, 128), f32),
            pltpu.VMEM((28, 8, 128), f32),
            pltpu.SemaphoreType.DMA((2,)),
        ],
    )(offsets, screen_size, canvas, dw_kernel, dw_bias, w_in, w_out)
    mixes = ring_gather(mixed)
    hidden, taken = call(
        hidden_kernel,
        [struct((rows, hid), f32), struct((lanes, SIDE, PAD_COLS, 128), f32)],
        [SMEM] * 2 + [VMEM] * 7,
        [pltpu.VMEM((rows, width), bf16)],
    )(offsets, tile_counts, *cots, layer_scale, near_out)
    to_right, to_left, next_right, next_left, mine, centers, inverses = call(
        block_kernel,
        [
            struct((half + 16, share), bf16),
            struct((half + 16, share), bf16),
            struct((rows, share), bf16),
            struct((rows, share), bf16),
            struct((rows, share), f32),
            struct((rows, 1), f32),
            struct((rows, 1), f32),
        ],
        [VMEM] * 10,
        [
            pltpu.VMEM((rows, width), bf16),
            pltpu.VMEM((rows, width), bf16),
            pltpu.VMEM((rows, hid), bf16),
        ],
        limit=24,
    )(*mixes, ln_gain, ln_bias, near_in, b_in, hidden)
    from_left, from_right = shift(to_right, 1), shift(to_left, -1)
    go_right, go_left = call(
        middle_kernel,
        [struct((rows + 16, share), bf16), struct((rows, share), bf16)],
        [VMEM] * 4,
    )(from_left, from_right, next_right, next_left)
    got_left, got_right = shift(go_right, 1), shift(go_left, -1)
    return call(
        canvas_kernel,
        jax.ShapeDtypeStruct(canvas.shape, f32),
        [SMEM] * 3 + [VMEM] * 12,
        [
            pltpu.VMEM((rows, share), f32),
            pltpu.VMEM((lanes, PAD_ROWS, PAD_COLS, 128), f32),
            pltpu.VMEM((49, 8, 128), f32),
            pltpu.VMEM(canvas.shape, f32),
            pltpu.SemaphoreType.DMA((lanes,)),
        ],
        out_specs=HBM,
    )(
        offsets, screen_size, tile_counts,
        mine, got_left, got_right, from_left, from_right, to_right, mixed, centers, inverses,
        ln_gain, taken, dw_kernel,
    )


def solution(mesh):
    return jax.shard_map(
        shards,
        mesh=mesh,
        in_specs=(
            P("img", None, "ch"),
            P("img", None),
            P(),
            P("img", None),
            P("img", None, None, "ch"),
            P(None, "ch"),
            P("ch"),
            P(),
            P(),
            P(None, "ch"),
            P("ch"),
            P("ch", None),
            P(),
        ),
        out_specs=P("img", None, "ch"),
        check_vma=False,
    )
```

```python
import functools

import jax
import jax.numpy as jnp
from jax import lax
from jax.experimental import pallas as pl
from jax.experimental.pallas import tpu as pltpu
from jax.sharding import PartitionSpec as P

TS = 4
SIDE = 32
PAD_ROWS = 38
PAD_COLS = 48
LEFT = 8

slope_coef = 0.7978845608
cubic_coef = 0.044715
norm_eps = 1e-06

VMEM = pl.BlockSpec(memory_space=pltpu.VMEM)
SMEM = pl.BlockSpec(memory_space=pltpu.SMEM)
HBM = pl.BlockSpec(memory_space=pltpu.HBM)


def call(kernel, out_shape, in_specs, scratch=(), limit=16, out_specs=None):
    run = pl.pallas_call(
        kernel,
        out_shape=out_shape,
        in_specs=in_specs,
        out_specs=out_specs or [VMEM] * len(out_shape),
        scratch_shapes=list(scratch),
        compiler_params=pltpu.CompilerParams(vmem_limit_bytes=limit << 20),
    )

    def held(*args):
        return run(
            *(
                pltpu.with_memory_space_constraint(a, pltpu.VMEM if spec is VMEM else pltpu.HBM)
                for spec, a in zip(in_specs, args, strict=True)
            )
        )

    return held


def inside_of(rows, row, height, width):
    column = lax.broadcasted_iota(jnp.int32, (rows, 128), 0)
    return (column < width) & (row < height)


def depthwise_kernel(
    offsets, screen, canvas, dwk, bias, w_out, mixed_a, mixed_b, near_out, here, framed, taps, kern_bf, bias_row, sems
):
    lanes = canvas.shape[2] // 128
    parts = 4
    deep = SIDE // parts
    height, width = screen[0, 0], screen[0, 1]
    small = [
        pltpu.make_async_copy(dwk, kern_bf, sems.at[parts]),
        pltpu.make_async_copy(bias, bias_row, sems.at[parts + 1]),
    ]
    rows_in = [
        pltpu.make_async_copy(
            canvas.at[pl.ds(g * deep, deep)], here.at[pl.ds(g * deep, deep)], sems.at[g]
        )
        for g in range(parts)
    ]
    weights = pltpu.make_async_copy(w_out, near_out, sems.at[parts + 2])
    for fetch in (*small, *rows_in, weights):
        fetch.start()
    low = lax.broadcasted_iota(jnp.int32, (8, 128), 0) < 4
    blank = jnp.zeros((PAD_COLS, 128), jnp.float32)
    for b in range(lanes):
        for y in (0, 1, 2, SIDE + 3, SIDE + 4, SIDE + 5):
            framed[b, y] = blank
    for fetch in small:
        fetch.wait()
    for b in range(lanes):
        kern = kern_bf[:, b * 128 : (b + 1) * 128].astype(jnp.float32)
        for i in range(7):
            for j in range(4):
                first = jnp.broadcast_to(kern[7 * i + j][None], (8, 128))
                if j < 3:
                    second = jnp.broadcast_to(kern[7 * i + j + 4][None], (8, 128))
                else:
                    second = jnp.zeros((8, 128), jnp.float32)
                taps[b, i * 4 + j] = jnp.where(low, first, second)

    def fill(y, carry):
        seen = inside_of(SIDE, y, height, width)
        for b in range(lanes):
            framed[b, y + 3, 0:LEFT, :] = blank[:LEFT]
            framed[b, y + 3, LEFT + SIDE : PAD_COLS, :] = blank[: PAD_COLS - LEFT - SIDE]
            row = here[y, :, b * 128 : (b + 1) * 128].astype(jnp.float32)
            framed[b, y + 3, LEFT : LEFT + SIDE, :] = jnp.where(seen, row, 0.0)
        return carry

    for g in range(parts):
        rows_in[g].wait()
        lax.fori_loop(g * deep, (g + 1) * deep, fill, 0, unroll=4)
    count = mixed_a.shape[0] // 16
    for b in range(lanes):
        cut = slice(b * 128, (b + 1) * 128)
        start = jnp.broadcast_to(bias_row[cut][None], (8, 128))
        for mixed, base in ((mixed_a, 0), (mixed_b, count)):

            def tile(t, carry):
                r, q = offsets[0, base + t], offsets[1, base + t]
                sums = [None] * 4
                for p in range(10):
                    for j in range(4):
                        seen = framed[b, r + p, pl.ds(q + (LEFT - 3 + j), 8), :]
                        for y in range(max(0, p - 6), min(3, p) + 1):
                            term = seen * taps[b, (p - y) * 4 + j]
                            sums[y] = term if sums[y] is None else sums[y] + term
                folded = [s + pltpu.roll(s, 4, 0) + start for s in sums]
                pair = [jnp.where(low, folded[y], folded[y + 1]) for y in (0, 2)]
                rows = pl.ds(pl.multiple_of(t * 16, 16), 16)
                mixed[rows, cut] = jnp.concatenate(pair, 0).astype(jnp.bfloat16)
                return carry

            lax.fori_loop(0, count, tile, 0, unroll=2)
    weights.wait()


def assemble(full, blocks, change):
    place = lax.axis_index("ch")
    for ref, ahead, row in blocks:
        rows, share = ref.shape
        begin = pl.multiple_of(lax.rem(place + ahead, 4) * share, 128)
        full[row : row + rows, pl.ds(begin, share)] = change(ref[...], begin, share)


def place_tiles(offsets, listed, values, canvas, top):
    low = lax.broadcasted_iota(jnp.int32, (8, 128), 0) < 4

    def tile(t, carry):
        r, q = offsets[0, t], offsets[1, t]
        columns = pl.ds(q + LEFT, 8)
        span = pl.ds(pl.multiple_of(t * 16, 16), 16)
        for b in range(values.shape[1] // 128):
            cells = values[span, b * 128 : (b + 1) * 128].astype(jnp.float32)
            for y in range(4):
                pair = cells[8 * (y // 2) : 8 * (y // 2) + 8]
                pair = pltpu.roll(pair, 4, 0) if y % 2 else pair
                canvas[b, r + top + y, columns, :] += jnp.where(low, pair, 0.0)
        return carry

    lax.fori_loop(0, listed, tile, 0)


def two_parts(row):
    high = row.astype(jnp.bfloat16).astype(jnp.float32)
    return [high, row - high]


def hidden_kernel(
    offsets, counts, own, left, right, opp_a, opp_b, scale, gain, bias, b_in, w_out, w_in,
    hidden, taken, near_in, sides, full, sem,
):
    fetch = pltpu.make_async_copy(w_in, near_in, sem)
    fetch.start()

    def scaled(block, begin, share):
        return (scale[pl.ds(begin, share)][None] * block.astype(jnp.float32)).astype(jnp.bfloat16)

    taken[...] = jnp.zeros_like(taken)
    place_tiles(offsets, counts[lax.axis_index("img")], own, taken, 0)
    half = opp_a.shape[0]
    blocks = ((own, 0, 0), (left, 3, 0), (right, 1, 0), (opp_a, 2, 0), (opp_b, 2, half))
    assemble(full, blocks, scaled)
    step = 512
    for n in range(0, hidden.shape[1], step):
        hidden[:, n : n + step] = lax.dot_general(
            full[...],
            w_out[n : n + step, :],
            (((1,), (1,)), ((), ())),
            preferred_element_type=jnp.float32,
        )
    width = gain.shape[0]
    lines = two_parts(gain[...][None]) + two_parts(bias[...][None])
    lines = jnp.concatenate(lines + [jnp.zeros((12, width), jnp.float32)], 0).astype(jnp.bfloat16)
    fetch.wait()
    both = jnp.dot(lines, near_in[...], preferred_element_type=jnp.float32)
    sides[0:1, :] = both[0:1] + both[1:2]
    sides[1:2, :] = both[2:3] + both[3:4] + b_in[...][None]


def gelu_slope(v):
    square = v * v
    t = jnp.tanh(slope_coef * (v + cubic_coef * square * v))
    return 0.5 * (1.0 + t) + 0.5 * v * (1.0 - t * t) * slope_coef * (1.0 + 3.0 * cubic_coef * square)


def as_rows(column):
    count = column.shape[0] // 128
    eye = lax.broadcasted_iota(jnp.int32, (128, 128), 0) == lax.broadcasted_iota(jnp.int32, (128, 128), 1)
    return jnp.concatenate(
        [
            jnp.sum(jnp.where(eye, column[g * 128 : (g + 1) * 128], 0.0), axis=0, keepdims=True)
            for g in range(count)
        ],
        0,
    )


def as_column(rows):
    eye = lax.broadcasted_iota(jnp.int32, (128, 128), 0) == lax.broadcasted_iota(jnp.int32, (128, 128), 1)
    return jnp.concatenate(
        [
            jnp.sum(jnp.where(eye, rows[g : g + 1], 0.0), axis=1, keepdims=True)
            for g in range(rows.shape[0])
        ],
        0,
    )


def part_of(act, w_in, ahead):
    share = w_in.shape[0] // 4
    begin = pl.multiple_of(lax.rem(lax.axis_index("ch") + ahead, 4) * share, 128)
    return lax.dot_general(
        act[...],
        w_in[pl.ds(begin, share), :],
        (((1,), (1,)), ((), ())),
        preferred_element_type=jnp.float32,
    )


def block_kernel(
    own_a, own_b, left_a, left_b, right_a, right_b, opp_a, opp_b, gain, bias, w_in, b_in, hidden, sides,
    to_right, to_left, act, centers, inverses, full, scaled,
):
    rows, width = full.shape
    half, share = own_a.shape
    pairs = ((own_a, own_b, 0), (left_a, left_b, 3), (right_a, right_b, 1), (opp_a, opp_b, 2))
    blocks = [(ref, ahead, row) for a, b, ahead in pairs for ref, row in ((a, 0), (b, half))]
    assemble(full, blocks, lambda block, begin, share: block)
    step = 64
    for m in range(0, rows, step):
        values = full[m : m + step, :].astype(jnp.float32)
        center = jnp.mean(values, axis=1, keepdims=True)
        apart = values - center
        inverse = lax.rsqrt(jnp.mean(apart * apart, axis=1, keepdims=True) + norm_eps)
        centers[m : m + step, :] = center
        inverses[m : m + step, :] = inverse
        scaled[m : m + step, :] = (apart * inverse * gain[...][None] + bias[...][None]).astype(
            jnp.bfloat16
        )
    step = 512
    first = jnp.zeros((rows, 128), jnp.float32)
    second = jnp.zeros((rows, 128), jnp.float32)
    for n in range(0, width, step):
        span = slice(n, n + step)
        product = jnp.dot(scaled[...], w_in[:, span], preferred_element_type=jnp.float32)
        pre = product + b_in[span][None]
        rounded = (hidden[:, span] * gelu_slope(pre)).astype(jnp.bfloat16)
        act[:, span] = rounded
        value = rounded.astype(jnp.float32)
        one = value * sides[0:1, span]
        two = value * (pre - sides[1:2, span])
        for k in range(0, step, 128):
            first = first + one[:, k : k + 128]
            second = second + two[:, k : k + 128]
    part = part_of(act, w_in, 2)
    to_right[:half, :] = part[:half].astype(jnp.bfloat16)
    to_left[:half, :] = part[half:].astype(jnp.bfloat16)
    packed = []
    for sums in (first, second):
        packed += two_parts(as_rows(jnp.sum(sums, axis=1, keepdims=True)))
    sums = jnp.concatenate(packed, 0).astype(jnp.bfloat16)
    for out in (to_right, to_left):
        out[half : half + 16, :] = jnp.zeros((16, share), jnp.bfloat16)
        out[half : half + 16, :128] = sums


def parts_kernel(act, w_in, next_right, next_left, mine):
    next_right[...] = part_of(act, w_in, 1).astype(jnp.bfloat16)
    next_left[...] = part_of(act, w_in, 3).astype(jnp.bfloat16)
    mine[...] = part_of(act, w_in, 0)


def middle_kernel(from_left, from_right, next_right, next_left, go_right, go_left):
    rows = next_right.shape[0]
    half = rows // 2

    def add(a, b):
        return (a.astype(jnp.float32) + b.astype(jnp.float32)).astype(jnp.bfloat16)

    go_right[:half, :] = add(next_right[:half, :], from_left[:half, :])
    go_right[half:rows, :] = next_right[half:, :]
    go_right[rows : rows + 16, :] = from_left[half : half + 16, :]
    go_left[:half, :] = next_left[:half, :]
    go_left[half:, :] = add(next_left[half:, :], from_right[:half, :])


def canvas_kernel(
    offsets, screen, counts,
    mine, got_left, got_right, from_left, from_right, to_right, mixed_a, mixed_b, centers, inverses, gain, taken, dwk,
    grad, upstream, grown, taps, stage, sems,
):
    half, share = mixed_a.shape
    rows = 2 * half
    lanes = share // 128
    total = gain.shape[0]
    height, width = screen[0, 0], screen[0, 1]
    begin = pl.multiple_of(lax.axis_index("ch") * share, 128)
    packed = (
        to_right[half : half + 16, :128].astype(jnp.float32)
        + from_left[half : half + 16, :128].astype(jnp.float32)
        + from_right[half : half + 16, :128].astype(jnp.float32)
        + got_left[rows : rows + 16, :128].astype(jnp.float32)
    )
    first = as_column((packed[0:4] + packed[4:8]) * (1.0 / total))
    second = as_column((packed[8:12] + packed[12:16]) * (1.0 / total))
    step = 64
    for m in range(0, rows, step):
        span = slice(m, m + step)
        norm_grad = (
            mine[span, :]
            + got_left[span, :].astype(jnp.float32)
            + got_right[span, :].astype(jnp.float32)
        )
        inverse = inverses[span, :]
        mixed = mixed_a[span, :] if m < half else mixed_b[m - half : m - half + step, :]
        normed = (mixed.astype(jnp.float32) - centers[span, :]) * inverse
        weighted = norm_grad * gain[pl.ds(begin, share)][None]
        upstream[span, :] = inverse * (weighted - first[span] - normed * second[span])

    grown[...] = jnp.zeros_like(grown)
    place_tiles(offsets, counts[lax.axis_index("img")], upstream, grown, 3)
    stores = []
    pairs = 4
    for b in range(lanes):
        cut = slice(b * 128, (b + 1) * 128)
        kern = dwk[:, cut].astype(jnp.float32)
        for k in range(49):
            taps[k] = jnp.broadcast_to(kern[k][None], (8, 128))

        def line(step, carry):
            y = step * pairs
            sums = [[None] * 4 for _ in range(pairs)]
            for p in range(6 + pairs):
                for j in range(7):
                    seen = [
                        grown[b, y + p, LEFT + 3 - j + 8 * x : LEFT + 3 - j + 8 * x + 8, :]
                        for x in range(4)
                    ]
                    for d in range(pairs):
                        i = 6 + d - p
                        if 0 <= i < 7:
                            tap = taps[7 * i + j]
                            for x in range(4):
                                term = seen[x] * tap
                                sums[d][x] = term if sums[d][x] is None else sums[d][x] + term
            for d in range(pairs):
                whole = jnp.concatenate(sums[d], 0) + taken[b, y + d, LEFT : LEFT + SIDE, :]
                stage[y + d, :, cut] = jnp.where(inside_of(SIDE, y + d, height, width), whole, 0.0)
            return carry

        lax.fori_loop(0, SIDE // pairs, line, 0)
        store = pltpu.make_async_copy(stage.at[:, :, cut], grad.at[:, :, cut], sems.at[b])
        store.start()
        stores.append(store)
    for store in stores:
        store.wait()


def shift(x, by):
    n = lax.axis_size("ch")
    return lax.ppermute(x, "ch", [(i, (i + by) % n) for i in range(n)])


def ring_gather(x):
    half = x.shape[0] // 2
    left, right = shift(x, 1), shift(x, -1)
    return x, left, right, shift(left[:half], 1), shift(right[half:], -1)


def shards(
    canvas,
    screen_size,
    tile_counts,
    tile_offsets,
    cotangent,
    dw_kernel,
    dw_bias,
    ln_gain,
    ln_bias,
    w_in,
    b_in,
    w_out,
    layer_scale,
):
    f32, bf16 = jnp.float32, jnp.bfloat16
    struct = pltpu.VMEM
    slots = tile_offsets.shape[0]
    share = canvas.shape[2]
    width = ln_gain.shape[0]
    hid = w_in.shape[1]
    rows = slots * TS * TS
    half = rows // 2
    lanes = share // 128
    offsets = tile_offsets.T
    cot = cotangent.reshape(rows, share)
    cots = ring_gather(cot)
    mixed_a, mixed_b, near_out = call(
        depthwise_kernel,
        [struct((half, share), bf16), struct((half, share), bf16), struct(w_out.shape, bf16)],
        [SMEM, SMEM, HBM, HBM, HBM, HBM],
        [
            pltpu.VMEM(canvas.shape, bf16),
            pltpu.VMEM((lanes, PAD_ROWS, PAD_COLS, 128), f32),
            pltpu.VMEM((lanes, 28, 8, 128), f32),
            pltpu.VMEM(dw_kernel.shape, bf16),
            pltpu.VMEM(dw_bias.shape, f32),
            pltpu.SemaphoreType.DMA((7,)),
        ],
    )(offsets, screen_size, canvas, dw_kernel, dw_bias, w_out)
    left_a, right_b = shift(mixed_a, 1), shift(mixed_b, -1)
    left_b, right_a = shift(mixed_b, 1), shift(mixed_a, -1)
    opp_a, opp_b = shift(left_a, 1), shift(right_b, -1)
    hidden, taken, near_in, sides = call(
        hidden_kernel,
        [
            struct((rows, hid), f32),
            struct((lanes, SIDE, PAD_COLS, 128), f32),
            struct(w_in.shape, bf16),
            struct((8, hid), f32),
        ],
        [SMEM] * 2 + [VMEM] * 10 + [HBM],
        [pltpu.VMEM((rows, width), bf16), pltpu.SemaphoreType.DMA(())],
    )(offsets, tile_counts, *cots, layer_scale, ln_gain, ln_bias, b_in, near_out, w_in)
    to_right, to_left, act, centers, inverses = call(
        block_kernel,
        [
            struct((half + 16, share), bf16),
            struct((half + 16, share), bf16),
            struct((rows, hid), bf16),
            struct((rows, 1), f32),
            struct((rows, 1), f32),
        ],
        [VMEM] * 14,
        [pltpu.VMEM((rows, width), bf16), pltpu.VMEM((rows, width), bf16)],
        limit=24,
    )(
        mixed_a, mixed_b, left_a, left_b, right_a, right_b, opp_a, opp_b,
        ln_gain, ln_bias, near_in, b_in, hidden, sides,
    )
    from_left, from_right = shift(to_right, 1), shift(to_left, -1)
    next_right, next_left, mine = call(
        parts_kernel,
        [struct((rows, share), bf16), struct((rows, share), bf16), struct((rows, share), f32)],
        [VMEM] * 2,
    )(act, near_in)
    go_right, go_left = call(
        middle_kernel,
        [struct((rows + 16, share), bf16), struct((rows, share), bf16)],
        [VMEM] * 4,
    )(from_left, from_right, next_right, next_left)
    got_left, got_right = shift(go_right, 1), shift(go_left, -1)
    return call(
        canvas_kernel,
        jax.ShapeDtypeStruct(canvas.shape, f32),
        [SMEM] * 3 + [VMEM] * 13,
        [
            pltpu.VMEM((rows, share), f32),
            pltpu.VMEM((lanes, PAD_ROWS, PAD_COLS, 128), f32),
            pltpu.VMEM((49, 8, 128), f32),
            pltpu.VMEM(canvas.shape, f32),
            pltpu.SemaphoreType.DMA((lanes,)),
        ],
        out_specs=HBM,
    )(
        offsets, screen_size, tile_counts,
        mine, got_left, got_right, from_left, from_right, to_right, mixed_a, mixed_b, centers, inverses,
        ln_gain, taken, dw_kernel,
    )


def solution(mesh):
    return jax.shard_map(
        shards,
        mesh=mesh,
        in_specs=(
            P("img", None, "ch"),
            P("img", None),
            P(),
            P("img", None),
            P("img", None, None, "ch"),
            P(None, "ch"),
            P("ch"),
            P(),
            P(),
            P(None, "ch"),
            P("ch"),
            P("ch", None),
            P(),
        ),
        out_specs=P("img", None, "ch"),
        check_vma=False,
    )
```

```python
import functools

import jax
import jax.numpy as jnp
from jax import lax
from jax.experimental import pallas as pl
from jax.experimental.pallas import tpu as pltpu
from jax.sharding import PartitionSpec as P

TS = 4
SIDE = 32
PAD_ROWS = 38
PAD_COLS = 48
LEFT = 8

slope_coef = 0.7978845608
cubic_coef = 0.044715
norm_eps = 1e-06

VMEM = pl.BlockSpec(memory_space=pltpu.VMEM)
SMEM = pl.BlockSpec(memory_space=pltpu.SMEM)
HBM = pl.BlockSpec(memory_space=pltpu.HBM)


def call(kernel, out_shape, in_specs, scratch=(), limit=16, out_specs=None):
    run = pl.pallas_call(
        kernel,
        out_shape=out_shape,
        in_specs=in_specs,
        out_specs=out_specs or [VMEM] * len(out_shape),
        scratch_shapes=list(scratch),
        compiler_params=pltpu.CompilerParams(vmem_limit_bytes=limit << 20),
    )

    def held(*args):
        return run(
            *(
                pltpu.with_memory_space_constraint(a, pltpu.VMEM if spec is VMEM else pltpu.HBM)
                for spec, a in zip(in_specs, args, strict=True)
            )
        )

    return held


def inside_of(rows, row, height, width):
    column = lax.broadcasted_iota(jnp.int32, (rows, 128), 0)
    return (column < width) & (row < height)


def depthwise_kernel(
    offsets, screen, canvas, dwk, bias, w_out, mixed_a, mixed_b, near_out, taps, here, framed, kern_bf, bias_row, sems
):
    lanes = canvas.shape[2] // 128
    parts = 4
    deep = SIDE // parts
    height, width = screen[0, 0], screen[0, 1]
    small = [
        pltpu.make_async_copy(dwk, kern_bf, sems.at[parts]),
        pltpu.make_async_copy(bias, bias_row, sems.at[parts + 1]),
    ]
    rows_in = [
        pltpu.make_async_copy(
            canvas.at[pl.ds(g * deep, deep)], here.at[pl.ds(g * deep, deep)], sems.at[g]
        )
        for g in range(parts)
    ]
    weights = pltpu.make_async_copy(w_out, near_out, sems.at[parts + 2])
    for fetch in (*small, *rows_in, weights):
        fetch.start()
    low = lax.broadcasted_iota(jnp.int32, (8, 128), 0) < 4
    blank = jnp.zeros((PAD_COLS, 128), jnp.float32)
    for b in range(lanes):
        for y in (0, 1, 2, SIDE + 3, SIDE + 4, SIDE + 5):
            framed[b, y] = blank
    for fetch in small:
        fetch.wait()
    for b in range(lanes):
        kern = kern_bf[:, b * 128 : (b + 1) * 128].astype(jnp.float32)
        for i in range(7):
            for j in range(4):
                first = jnp.broadcast_to(kern[7 * i + j][None], (8, 128))
                if j < 3:
                    second = jnp.broadcast_to(kern[7 * i + j + 4][None], (8, 128))
                else:
                    second = jnp.zeros((8, 128), jnp.float32)
                taps[b, i * 4 + j] = jnp.where(low, first, second)

    def fill(y, carry):
        seen = inside_of(SIDE, y, height, width)
        for b in range(lanes):
            framed[b, y + 3, 0:LEFT, :] = blank[:LEFT]
            framed[b, y + 3, LEFT + SIDE : PAD_COLS, :] = blank[: PAD_COLS - LEFT - SIDE]
            row = here[y, :, b * 128 : (b + 1) * 128].astype(jnp.float32)
            framed[b, y + 3, LEFT : LEFT + SIDE, :] = jnp.where(seen, row, 0.0)
        return carry

    for g in range(parts):
        rows_in[g].wait()
        lax.fori_loop(g * deep, (g + 1) * deep, fill, 0, unroll=4)
    count = mixed_a.shape[0] // 16
    for b in range(lanes):
        cut = slice(b * 128, (b + 1) * 128)
        start = jnp.broadcast_to(bias_row[cut][None], (8, 128))
        for mixed, base in ((mixed_a, 0), (mixed_b, count)):

            def tile(t, carry):
                r, q = offsets[0, base + t], offsets[1, base + t]
                sums = [None] * 4
                for p in range(10):
                    for j in range(4):
                        seen = framed[b, r + p, pl.ds(q + (LEFT - 3 + j), 8), :]
                        for y in range(max(0, p - 6), min(3, p) + 1):
                            term = seen * taps[b, (p - y) * 4 + j]
                            sums[y] = term if sums[y] is None else sums[y] + term
                folded = [s + pltpu.roll(s, 4, 0) + start for s in sums]
                pair = [jnp.where(low, folded[y], folded[y + 1]) for y in (0, 2)]
                rows = pl.ds(pl.multiple_of(t * 16, 16), 16)
                mixed[rows, cut] = jnp.concatenate(pair, 0).astype(jnp.bfloat16)
                return carry

            lax.fori_loop(0, count, tile, 0, unroll=2)
    weights.wait()


def two_parts(row):
    high = row.astype(jnp.bfloat16).astype(jnp.float32)
    return [high, row - high]


def scaled_rows(cells, scale, begin):
    share = cells.shape[3]
    flat = cells[...].astype(jnp.float32).reshape(cells.shape[0] * 16, share)
    return (scale[pl.ds(begin, share)][None] * flat).astype(jnp.bfloat16)


def channels_of(ahead, share):
    return pl.multiple_of(lax.rem(lax.axis_index("ch") + ahead, 4) * share, 128)


def hidden_kernel(
    offsets, counts, own, left, right, scale, gain, bias, b_in, w_out, w_in,
    hidden, taken, near_in, sides, flat, sem,
):
    fetch = pltpu.make_async_copy(w_in, near_in, sem)
    fetch.start()
    share = own.shape[3]
    taken[...] = jnp.zeros_like(taken)

    def tile(t, carry):
        r, q = offsets[0, t], offsets[1, t]
        for y in range(4):
            cells = own[t, y].astype(jnp.float32)
            for b in range(share // 128):
                taken[b, r + 3 + y, pl.ds(q + LEFT, 4), :] += cells[:, b * 128 : (b + 1) * 128]
        return carry

    lax.fori_loop(0, counts[lax.axis_index("img")], tile, 0)
    begins = []
    for k, (cells, ahead) in enumerate(((own, 0), (left, 3), (right, 1))):
        begins.append(channels_of(ahead, share))
        flat[k] = scaled_rows(cells, scale, begins[k])
    step = 512
    for n in range(0, hidden.shape[1], step):
        total = None
        for k, begin in enumerate(begins):
            product = lax.dot_general(
                flat[k],
                w_out[n : n + step, pl.ds(begin, share)],
                (((1,), (1,)), ((), ())),
                preferred_element_type=jnp.float32,
            )
            total = product if total is None else total + product
        hidden[:, n : n + step] = total
    width = gain.shape[0]
    lines = two_parts(gain[...][None]) + two_parts(bias[...][None])
    lines = jnp.concatenate(lines + [jnp.zeros((12, width), jnp.float32)], 0).astype(jnp.bfloat16)
    fetch.wait()
    both = jnp.dot(lines, near_in[...], preferred_element_type=jnp.float32)
    sides[0:1, :] = both[0:1] + both[1:2]
    sides[1:2, :] = both[2:3] + both[3:4] + b_in[...][None]


def gelu_slope(v):
    square = v * v
    t = jnp.tanh(slope_coef * (v + cubic_coef * square * v))
    return 0.5 * (1.0 + t) + 0.5 * v * (1.0 - t * t) * slope_coef * (1.0 + 3.0 * cubic_coef * square)


def as_rows(column):
    count = column.shape[0] // 128
    eye = lax.broadcasted_iota(jnp.int32, (128, 128), 0) == lax.broadcasted_iota(jnp.int32, (128, 128), 1)
    return jnp.concatenate(
        [
            jnp.sum(jnp.where(eye, column[g * 128 : (g + 1) * 128], 0.0), axis=0, keepdims=True)
            for g in range(count)
        ],
        0,
    )


def as_column(rows):
    eye = lax.broadcasted_iota(jnp.int32, (128, 128), 0) == lax.broadcasted_iota(jnp.int32, (128, 128), 1)
    return jnp.concatenate(
        [
            jnp.sum(jnp.where(eye, rows[g : g + 1], 0.0), axis=1, keepdims=True)
            for g in range(rows.shape[0])
        ],
        0,
    )


def part_of(act, w_in, ahead):
    share = w_in.shape[0] // 4
    return lax.dot_general(
        act[...],
        w_in[pl.ds(channels_of(ahead, share), share), :],
        (((1,), (1,)), ((), ())),
        preferred_element_type=jnp.float32,
    )


def block_kernel(
    own_a, own_b, left_a, left_b, right_a, right_b, opp_a, opp_b, cot_a, cot_b,
    gain, bias, scale, w_in, b_in, w_out, hidden, sides,
    to_right, to_left, act, centers, inverses, full, scaled, flat,
):
    rows, width = full.shape
    half, share = own_a.shape
    for a, b, ahead in ((own_a, own_b, 0), (left_a, left_b, 3), (right_a, right_b, 1), (opp_a, opp_b, 2)):
        columns = pl.ds(channels_of(ahead, share), share)
        full[:half, columns] = a[...]
        full[half:, columns] = b[...]
    opposite = channels_of(2, share)
    flat[:half, :] = scaled_rows(cot_a, scale, opposite)
    flat[half:, :] = scaled_rows(cot_b, scale, opposite)
    step = 64
    for m in range(0, rows, step):
        values = full[m : m + step, :].astype(jnp.float32)
        center = jnp.mean(values, axis=1, keepdims=True)
        apart = values - center
        inverse = lax.rsqrt(jnp.mean(apart * apart, axis=1, keepdims=True) + norm_eps)
        centers[m : m + step, :] = center
        inverses[m : m + step, :] = inverse
        scaled[m : m + step, :] = (apart * inverse * gain[...][None] + bias[...][None]).astype(
            jnp.bfloat16
        )
    step = 512
    first = jnp.zeros((rows, 128), jnp.float32)
    second = jnp.zeros((rows, 128), jnp.float32)
    for n in range(0, width, step):
        span = slice(n, n + step)
        product = jnp.dot(scaled[...], w_in[:, span], preferred_element_type=jnp.float32)
        pre = product + b_in[span][None]
        rest = lax.dot_general(
            flat[...],
            w_out[span, pl.ds(opposite, share)],
            (((1,), (1,)), ((), ())),
            preferred_element_type=jnp.float32,
        )
        rounded = ((hidden[:, span] + rest) * gelu_slope(pre)).astype(jnp.bfloat16)
        act[:, span] = rounded
        value = rounded.astype(jnp.float32)
        one = value * sides[0:1, span]
        two = value * (pre - sides[1:2, span])
        for k in range(0, step, 128):
            first = first + one[:, k : k + 128]
            second = second + two[:, k : k + 128]
    part = part_of(act, w_in, 2)
    to_right[:half, :] = part[:half].astype(jnp.bfloat16)
    to_left[:half, :] = part[half:].astype(jnp.bfloat16)
    packed = []
    for sums in (first, second):
        packed += two_parts(as_rows(jnp.sum(sums, axis=1, keepdims=True)))
    sums = jnp.concatenate(packed, 0).astype(jnp.bfloat16)
    for out in (to_right, to_left):
        out[half : half + 16, :] = jnp.zeros((16, share), jnp.bfloat16)
        out[half : half + 16, :128] = sums


def parts_kernel(act, w_in, keep_right, own_right, own_left, keep_left):
    half = keep_right.shape[0]
    for ahead, top, bottom in ((1, keep_right, own_right), (3, own_left, keep_left)):
        part = part_of(act, w_in, ahead).astype(jnp.bfloat16)
        top[:half, :] = part[:half]
        bottom[:half, :] = part[half:]
    for own in (own_right, own_left):
        own[half:, :] = jnp.zeros_like(own[half:, :])


def mine_kernel(act, w_in, keep, mine):
    del keep
    mine[...] = part_of(act, w_in, 0)


def middle_kernel(from_left, from_right, keep_right, keep_left, mine, go_right, go_left):
    del mine
    half = keep_right.shape[0]

    def add(a, b):
        return (a.astype(jnp.float32) + b.astype(jnp.float32)).astype(jnp.bfloat16)

    go_right[:half, :] = add(keep_right[...], from_left[:half, :])
    go_right[half : half + 16, :] = from_left[half : half + 16, :]
    go_left[...] = add(keep_left[...], from_right[:half, :])


def canvas_kernel(
    offsets, screen, counts,
    own_right, own_left, sum_left, sum_right, mine, from_left, from_right, to_right,
    mixed_a, mixed_b, centers, inverses, gain, taken, taps,
    grad, upstream, grown, stage, sems,
):
    half, share = mixed_a.shape
    rows = 2 * half
    lanes = share // 128
    total = gain.shape[0]
    height, width = screen[0, 0], screen[0, 1]
    grown[...] = taken[...]
    packed = (
        to_right[half : half + 16, :128].astype(jnp.float32)
        + from_left[half : half + 16, :128].astype(jnp.float32)
        + from_right[half : half + 16, :128].astype(jnp.float32)
        + sum_left[half : half + 16, :128].astype(jnp.float32)
    )
    first = as_column((packed[0:4] + packed[4:8]) * (1.0 / total))
    second = as_column((packed[8:12] + packed[12:16]) * (1.0 / total))
    weight = gain[pl.ds(channels_of(0, share), share)][None]
    step = 64
    for m in range(0, rows, step):
        span = slice(m, m + step)
        if m < half:
            here = span
            mixed, one, two = mixed_a, sum_left, own_left
        else:
            here = slice(m - half, m - half + step)
            mixed, one, two = mixed_b, own_right, sum_right
        norm_grad = mine[span, :] + one[here, :].astype(jnp.float32) + two[here, :].astype(jnp.float32)
        inverse = inverses[span, :]
        normed = (mixed[here, :].astype(jnp.float32) - centers[span, :]) * inverse
        upstream[span, :] = inverse * (norm_grad * weight - first[span] - normed * second[span])

    low = lax.broadcasted_iota(jnp.int32, (8, 128), 0) < 4

    def tile(t, carry):
        r, q = offsets[0, t], offsets[1, t]
        for b in range(lanes):
            doubled = []
            for h in range(2):
                pair = upstream[pl.ds(pl.multiple_of(t * 16 + 8 * h, 8), 8), b * 128 : (b + 1) * 128]
                turned = pltpu.roll(pair, 4, 0)
                doubled += [jnp.where(low, pair, turned), jnp.where(low, turned, pair)]
            for j in range(4):
                columns = pl.ds(q + (LEFT - 3 + j), 8)
                for y in range(10):
                    seen = grown[b, r + y, columns, :]
                    for k in range(max(0, y - 6), min(3, y) + 1):
                        seen = seen + doubled[k] * taps[b, (y - k) * 4 + j]
                    grown[b, r + y, columns, :] = seen
        return carry

    lax.fori_loop(0, counts[lax.axis_index("img")], tile, 0)
    stores = []
    deep = SIDE // 4
    for g in range(4):

        def line(y, carry):
            seen = inside_of(SIDE, y, height, width)
            for b in range(lanes):
                whole = grown[b, y + 3, LEFT : LEFT + SIDE, :]
                stage[y, :, b * 128 : (b + 1) * 128] = jnp.where(seen, whole, 0.0)
            return carry

        lax.fori_loop(g * deep, (g + 1) * deep, line, 0, unroll=4)
        part = pl.ds(g * deep, deep)
        store = pltpu.make_async_copy(stage.at[part], grad.at[part], sems.at[g])
        store.start()
        stores.append(store)
    for store in stores:
        store.wait()


def shift(x, by):
    n = lax.axis_size("ch")
    return lax.ppermute(x, "ch", [(i, (i + by) % n) for i in range(n)])


def shards(
    canvas,
    screen_size,
    tile_counts,
    tile_offsets,
    cotangent,
    dw_kernel,
    dw_bias,
    ln_gain,
    ln_bias,
    w_in,
    b_in,
    w_out,
    layer_scale,
):
    f32, bf16 = jnp.float32, jnp.bfloat16
    struct = pltpu.VMEM
    slots = tile_offsets.shape[0]
    share = canvas.shape[2]
    width = ln_gain.shape[0]
    hid = w_in.shape[1]
    rows = slots * TS * TS
    half = rows // 2
    lanes = share // 128
    offsets = tile_offsets.T
    left, right = shift(cotangent, 1), shift(cotangent, -1)
    mixed_a, mixed_b, near_out, taps = call(
        depthwise_kernel,
        [
            struct((half, share), bf16),
            struct((half, share), bf16),
            struct(w_out.shape, bf16),
            struct((lanes, 28, 8, 128), f32),
        ],
        [SMEM, SMEM, HBM, HBM, HBM, HBM],
        [
            pltpu.VMEM(canvas.shape, bf16),
            pltpu.VMEM((lanes, PAD_ROWS, PAD_COLS, 128), f32),
            pltpu.VMEM(dw_kernel.shape, bf16),
            pltpu.VMEM(dw_bias.shape, f32),
            pltpu.SemaphoreType.DMA((7,)),
        ],
    )(offsets, screen_size, canvas, dw_kernel, dw_bias, w_out)
    left_a, right_b = shift(mixed_a, 1), shift(mixed_b, -1)
    cot_a, cot_b = shift(left[: slots // 2], 1), shift(right[slots // 2 :], -1)
    left_b, right_a = shift(mixed_b, 1), shift(mixed_a, -1)
    opp_a, opp_b = shift(left_a, 1), shift(right_b, -1)
    hidden, taken, near_in, sides = call(
        hidden_kernel,
        [
            struct((rows, hid), f32),
            struct((lanes, PAD_ROWS, PAD_COLS, 128), f32),
            struct(w_in.shape, bf16),
            struct((8, hid), f32),
        ],
        [SMEM] * 2 + [VMEM] * 8 + [HBM],
        [pltpu.VMEM((3, rows, share), bf16), pltpu.SemaphoreType.DMA(())],
    )(
        offsets, tile_counts, cotangent, left, right, layer_scale, ln_gain, ln_bias, b_in, near_out, w_in
    )
    to_right, to_left, act, centers, inverses = call(
        block_kernel,
        [
            struct((half + 16, share), bf16),
            struct((half + 16, share), bf16),
            struct((rows, hid), bf16),
            struct((rows, 1), f32),
            struct((rows, 1), f32),
        ],
        [VMEM] * 18,
        [
            pltpu.VMEM((rows, width), bf16),
            pltpu.VMEM((rows, width), bf16),
            pltpu.VMEM((rows, share), bf16),
        ],
        limit=24,
    )(
        mixed_a, mixed_b, left_a, left_b, right_a, right_b, opp_a, opp_b, cot_a, cot_b,
        ln_gain, ln_bias, layer_scale, near_in, b_in, near_out, hidden, sides,
    )
    from_left, from_right = shift(to_right, 1), shift(to_left, -1)
    keep_right, own_right, own_left, keep_left = call(
        parts_kernel,
        [struct((half + more, share), bf16) for more in (0, 16, 16, 0)],
        [VMEM] * 2,
    )(act, near_in)
    got_left, got_right = shift(own_right, 1), shift(own_left, -1)
    (mine,) = call(mine_kernel, [struct((rows, share), f32)], [VMEM] * 3)(act, near_in, keep_right)
    go_right, go_left = call(
        middle_kernel,
        [struct((half + 16, share), bf16), struct((half, share), bf16)],
        [VMEM] * 5,
    )(from_left, from_right, keep_right, keep_left, mine)
    sum_left, sum_right = shift(go_right, 1), shift(go_left, -1)
    return call(
        canvas_kernel,
        jax.ShapeDtypeStruct(canvas.shape, f32),
        [SMEM] * 3 + [VMEM] * 15,
        [
            pltpu.VMEM((rows, share), f32),
            pltpu.VMEM((lanes, PAD_ROWS, PAD_COLS, 128), f32),
            pltpu.VMEM(canvas.shape, f32),
            pltpu.SemaphoreType.DMA((4,)),
        ],
        out_specs=HBM,
    )(
        offsets, screen_size, tile_counts,
        got_left, got_right, sum_left, sum_right, mine, from_left, from_right, to_right,
        mixed_a, mixed_b, centers, inverses, ln_gain, taken, taps,
    )


def solution(mesh):
    return jax.shard_map(
        shards,
        mesh=mesh,
        in_specs=(
            P("img", None, "ch"),
            P("img", None),
            P(),
            P("img", None),
            P("img", None, None, "ch"),
            P(None, "ch"),
            P("ch"),
            P(),
            P(),
            P(None, "ch"),
            P("ch"),
            P("ch", None),
            P(),
        ),
        out_specs=P("img", None, "ch"),
        check_vma=False,
    )
```

```python
import functools

import jax
import jax.numpy as jnp
from jax import lax
from jax.experimental import pallas as pl
from jax.experimental.pallas import tpu as pltpu
from jax.sharding import PartitionSpec as P

TS = 4
SIDE = 32
PAD_ROWS = 38
PAD_COLS = 48
LEFT = 8

slope_coef = 0.7978845608
cubic_coef = 0.044715
norm_eps = 1e-06

VMEM = pl.BlockSpec(memory_space=pltpu.VMEM)
SMEM = pl.BlockSpec(memory_space=pltpu.SMEM)
HBM = pl.BlockSpec(memory_space=pltpu.HBM)


def call(kernel, out_shape, in_specs, scratch=(), limit=16, out_specs=None):
    run = pl.pallas_call(
        kernel,
        out_shape=out_shape,
        in_specs=in_specs,
        out_specs=out_specs or [VMEM] * len(out_shape),
        scratch_shapes=list(scratch),
        compiler_params=pltpu.CompilerParams(vmem_limit_bytes=limit << 20),
    )

    def held(*args):
        return run(
            *(
                pltpu.with_memory_space_constraint(a, pltpu.VMEM if spec is VMEM else pltpu.HBM)
                for spec, a in zip(in_specs, args, strict=True)
            )
        )

    return held


def inside_of(rows, row, height, width):
    column = lax.broadcasted_iota(jnp.int32, (rows, 128), 0)
    return (column < width) & (row < height)


def depthwise_kernel(
    offsets, screen, canvas, dwk, bias, w_out, mixed_a, mixed_b, near_out, taps, here, framed, kern_bf, bias_row, sems
):
    lanes = canvas.shape[2] // 128
    parts = 4
    deep = SIDE // parts
    height, width = screen[0, 0], screen[0, 1]
    small = [
        pltpu.make_async_copy(dwk, kern_bf, sems.at[parts]),
        pltpu.make_async_copy(bias, bias_row, sems.at[parts + 1]),
    ]
    rows_in = [
        pltpu.make_async_copy(
            canvas.at[pl.ds(g * deep, deep)], here.at[pl.ds(g * deep, deep)], sems.at[g]
        )
        for g in range(parts)
    ]
    weights = pltpu.make_async_copy(w_out, near_out, sems.at[parts + 2])
    for fetch in (*small, *rows_in, weights):
        fetch.start()
    low = lax.broadcasted_iota(jnp.int32, (8, 128), 0) < 4
    blank = jnp.zeros((PAD_COLS, 128), jnp.float32)
    for b in range(lanes):
        for y in (0, 1, 2, SIDE + 3, SIDE + 4, SIDE + 5):
            framed[b, y] = blank
    for fetch in small:
        fetch.wait()
    for b in range(lanes):
        kern = kern_bf[:, b * 128 : (b + 1) * 128].astype(jnp.float32)
        for i in range(7):
            for j in range(4):
                first = jnp.broadcast_to(kern[7 * i + j][None], (8, 128))
                if j < 3:
                    second = jnp.broadcast_to(kern[7 * i + j + 4][None], (8, 128))
                else:
                    second = jnp.zeros((8, 128), jnp.float32)
                taps[b, i * 4 + j] = jnp.where(low, first, second)

    def fill(y, carry):
        seen = inside_of(SIDE, y, height, width)
        for b in range(lanes):
            framed[b, y + 3, 0:LEFT, :] = blank[:LEFT]
            framed[b, y + 3, LEFT + SIDE : PAD_COLS, :] = blank[: PAD_COLS - LEFT - SIDE]
            row = here[y, :, b * 128 : (b + 1) * 128].astype(jnp.float32)
            framed[b, y + 3, LEFT : LEFT + SIDE, :] = jnp.where(seen, row, 0.0)
        return carry

    for g in range(parts):
        rows_in[g].wait()
        lax.fori_loop(g * deep, (g + 1) * deep, fill, 0, unroll=4)
    count = mixed_a.shape[0] // 16
    for b in range(lanes):
        cut = slice(b * 128, (b + 1) * 128)
        start = jnp.broadcast_to(bias_row[cut][None], (8, 128))
        for mixed, base in ((mixed_a, 0), (mixed_b, count)):

            def tile(t, carry):
                r, q = offsets[0, base + t], offsets[1, base + t]
                sums = [None] * 4
                for p in range(10):
                    for j in range(4):
                        seen = framed[b, r + p, pl.ds(q + (LEFT - 3 + j), 8), :]
                        for y in range(max(0, p - 6), min(3, p) + 1):
                            term = seen * taps[b, (p - y) * 4 + j]
                            sums[y] = term if sums[y] is None else sums[y] + term
                folded = [s + pltpu.roll(s, 4, 0) + start for s in sums]
                pair = [jnp.where(low, folded[y], folded[y + 1]) for y in (0, 2)]
                rows = pl.ds(pl.multiple_of(t * 16, 16), 16)
                mixed[rows, cut] = jnp.concatenate(pair, 0).astype(jnp.bfloat16)
                return carry

            lax.fori_loop(0, count, tile, 0, unroll=2)
    weights.wait()


def two_parts(row):
    high = row.astype(jnp.bfloat16).astype(jnp.float32)
    return [high, row - high]


def scaled_rows(cells, scale, begin):
    share = cells.shape[3]
    flat = cells[...].astype(jnp.float32).reshape(cells.shape[0] * 16, share)
    return (scale[pl.ds(begin, share)][None] * flat).astype(jnp.bfloat16)


def channels_of(ahead, share):
    return pl.multiple_of(lax.rem(lax.axis_index("ch") + ahead, 4) * share, 128)


def hidden_kernel(
    offsets, counts, own, left, right, cot_a, cot_b, scale, gain, bias, b_in, w_out, w_in,
    hidden_a, hidden_b, taken, near_in, sides, full, sem,
):
    fetch = pltpu.make_async_copy(w_in, near_in, sem)
    fetch.start()
    share = own.shape[3]
    half = hidden_a.shape[0]
    taken[...] = jnp.zeros_like(taken)

    def tile(t, carry):
        r, q = offsets[0, t], offsets[1, t]
        for y in range(4):
            cells = own[t, y].astype(jnp.float32)
            for b in range(share // 128):
                taken[b, r + 3 + y, pl.ds(q + LEFT, 4), :] += cells[:, b * 128 : (b + 1) * 128]
        return carry

    lax.fori_loop(0, counts[lax.axis_index("img")], tile, 0)
    for cells, ahead, row in ((own, 0, 0), (left, 3, 0), (right, 1, 0), (cot_a, 2, 0), (cot_b, 2, half)):
        begin = channels_of(ahead, share)
        full[row : row + 16 * cells.shape[0], pl.ds(begin, share)] = scaled_rows(cells, scale, begin)
    step = 512
    for n in range(0, hidden_a.shape[1], step):
        product = lax.dot_general(
            full[...],
            w_out[n : n + step, :],
            (((1,), (1,)), ((), ())),
            preferred_element_type=jnp.float32,
        )
        hidden_a[:, n : n + step] = product[:half]
        hidden_b[:, n : n + step] = product[half:]
    width = gain.shape[0]
    lines = two_parts(gain[...][None]) + two_parts(bias[...][None])
    lines = jnp.concatenate(lines + [jnp.zeros((12, width), jnp.float32)], 0).astype(jnp.bfloat16)
    fetch.wait()
    both = jnp.dot(lines, near_in[...], preferred_element_type=jnp.float32)
    sides[0:1, :] = both[0:1] + both[1:2]
    sides[1:2, :] = both[2:3] + both[3:4] + b_in[...][None]


def gelu_slope(v):
    square = v * v
    t = jnp.tanh(slope_coef * (v + cubic_coef * square * v))
    return 0.5 * (1.0 + t) + 0.5 * v * (1.0 - t * t) * slope_coef * (1.0 + 3.0 * cubic_coef * square)


def as_rows(column):
    count = column.shape[0] // 128
    eye = lax.broadcasted_iota(jnp.int32, (128, 128), 0) == lax.broadcasted_iota(jnp.int32, (128, 128), 1)
    return jnp.concatenate(
        [
            jnp.sum(jnp.where(eye, column[g * 128 : (g + 1) * 128], 0.0), axis=0, keepdims=True)
            for g in range(count)
        ],
        0,
    )


def as_column(rows):
    eye = lax.broadcasted_iota(jnp.int32, (128, 128), 0) == lax.broadcasted_iota(jnp.int32, (128, 128), 1)
    return jnp.concatenate(
        [
            jnp.sum(jnp.where(eye, rows[g : g + 1], 0.0), axis=1, keepdims=True)
            for g in range(rows.shape[0])
        ],
        0,
    )


def part_of(act, w_in, ahead):
    share = w_in.shape[0] // 4
    return lax.dot_general(
        act[...],
        w_in[pl.ds(channels_of(ahead, share), share), :],
        (((1,), (1,)), ((), ())),
        preferred_element_type=jnp.float32,
    )


def block_kernel(
    own, left, right, opp, gain, bias, w_in, b_in, hidden, sides, earlier,
    away, act, centers, inverses, full, scaled,
):
    del earlier
    rows, width = full.shape
    share = own.shape[1]
    for ref, ahead in ((own, 0), (left, 3), (right, 1), (opp, 2)):
        full[:, pl.ds(channels_of(ahead, share), share)] = ref[...]
    step = 64
    for m in range(0, rows, step):
        values = full[m : m + step, :].astype(jnp.float32)
        center = jnp.mean(values, axis=1, keepdims=True)
        apart = values - center
        inverse = lax.rsqrt(jnp.mean(apart * apart, axis=1, keepdims=True) + norm_eps)
        centers[m : m + step, :] = center
        inverses[m : m + step, :] = inverse
        scaled[m : m + step, :] = (apart * inverse * gain[...][None] + bias[...][None]).astype(
            jnp.bfloat16
        )
    step = 512
    first = jnp.zeros((rows, 128), jnp.float32)
    second = jnp.zeros((rows, 128), jnp.float32)
    for n in range(0, width, step):
        span = slice(n, n + step)
        product = jnp.dot(scaled[...], w_in[:, span], preferred_element_type=jnp.float32)
        pre = product + b_in[span][None]
        rounded = (hidden[:, span] * gelu_slope(pre)).astype(jnp.bfloat16)
        act[:, span] = rounded
        value = rounded.astype(jnp.float32)
        one = value * sides[0:1, span]
        two = value * (pre - sides[1:2, span])
        for k in range(0, step, 128):
            first = first + one[:, k : k + 128]
            second = second + two[:, k : k + 128]
    away[:rows, :] = part_of(act, w_in, 2).astype(jnp.bfloat16)
    packed = []
    for sums in (first, second):
        packed += two_parts(as_rows(jnp.sum(sums, axis=1, keepdims=True)))
    packed += [jnp.zeros((16 - 4 * (rows // 128), 128), jnp.float32)]
    away[rows : rows + 16, :] = jnp.zeros((16, share), jnp.bfloat16)
    away[rows : rows + 16, :128] = jnp.concatenate(packed, 0).astype(jnp.bfloat16)


def parts_kernel(keep_ahead, own_ahead, act, w_in, away, earlier, keep, own, mine):
    del earlier
    rows = act.shape[0]
    own[:rows, :] = part_of(act, w_in, own_ahead).astype(jnp.bfloat16)
    own[rows:, :] = away[rows:, :]
    keep[...] = part_of(act, w_in, keep_ahead).astype(jnp.bfloat16)
    mine[...] = part_of(act, w_in, 0)


def middle_kernel(come, keep, go):
    rows = keep.shape[0]
    total = keep[...].astype(jnp.float32) + come[:rows, :].astype(jnp.float32)
    go[:rows, :] = total.astype(jnp.bfloat16)
    go[rows:, :] = come[rows:, :]


def add_tiles(
    base, offsets, counts, mine, got, total, come, away, mixed, centers, inverses, gain, taps, upstream, grown
):
    rows, share = mixed.shape
    width = gain.shape[0]
    packed = None
    for ref in (away, come, got, total):
        lines = ref[rows : rows + 16, :128].astype(jnp.float32)
        packed = lines if packed is None else packed + lines
    n = rows // 128
    first = as_column((packed[0:n] + packed[n : 2 * n]) * (1.0 / width))
    second = as_column((packed[2 * n : 3 * n] + packed[3 * n : 4 * n]) * (1.0 / width))
    weight = gain[pl.ds(channels_of(0, share), share)][None]
    step = 64
    for m in range(0, rows, step):
        span = slice(m, m + step)
        norm_grad = mine[span, :] + got[span, :].astype(jnp.float32) + total[span, :].astype(jnp.float32)
        inverse = inverses[span, :]
        normed = (mixed[span, :].astype(jnp.float32) - centers[span, :]) * inverse
        upstream[span, :] = inverse * (norm_grad * weight - first[span] - normed * second[span])

    low = lax.broadcasted_iota(jnp.int32, (8, 128), 0) < 4

    def tile(t, carry):
        r, q = offsets[0, base + t], offsets[1, base + t]
        for b in range(share // 128):
            doubled = []
            for h in range(2):
                pair = upstream[pl.ds(pl.multiple_of(t * 16 + 8 * h, 8), 8), b * 128 : (b + 1) * 128]
                turned = pltpu.roll(pair, 4, 0)
                doubled += [jnp.where(low, pair, turned), jnp.where(low, turned, pair)]
            for j in range(4):
                columns = pl.ds(q + (LEFT - 3 + j), 8)
                for y in range(10):
                    more = None
                    for k in range(max(0, y - 6), min(3, y) + 1):
                        term = doubled[k] * taps[b, (y - k) * 4 + j]
                        more = term if more is None else more + term
                    grown[b, r + y, columns, :] += more
        return carry

    listed = counts[lax.axis_index("img")] - base
    lax.fori_loop(0, jnp.clip(listed, 0, rows // 16), tile, 0)


def first_tiles_kernel(
    offsets, counts, mine, got, total, come, away, mixed, centers, inverses, gain, taps, before,
    grown, upstream,
):
    grown[...] = before[...]
    add_tiles(
        0, offsets, counts, mine, got, total, come, away, mixed, centers, inverses, gain, taps, upstream, grown
    )


def last_tiles_kernel(
    offsets, counts, screen, mine, got, total, come, away, mixed, centers, inverses, gain, taps, before,
    grad, upstream, grown, stage, sems,
):
    grown[...] = before[...]
    add_tiles(
        mixed.shape[0] // 16,
        offsets, counts, mine, got, total, come, away, mixed, centers, inverses, gain, taps, upstream, grown,
    )
    height, width = screen[0, 0], screen[0, 1]
    stores = []
    deep = SIDE // 4
    for g in range(4):

        def line(y, carry):
            seen = inside_of(SIDE, y, height, width)
            for b in range(mixed.shape[1] // 128):
                whole = grown[b, y + 3, LEFT : LEFT + SIDE, :]
                stage[y, :, b * 128 : (b + 1) * 128] = jnp.where(seen, whole, 0.0)
            return carry

        lax.fori_loop(g * deep, (g + 1) * deep, line, 0, unroll=4)
        part = pl.ds(g * deep, deep)
        store = pltpu.make_async_copy(stage.at[part], grad.at[part], sems.at[g])
        store.start()
        stores.append(store)
    for store in stores:
        store.wait()


def shift(x, by):
    n = lax.axis_size("ch")
    return lax.ppermute(x, "ch", [(i, (i + by) % n) for i in range(n)])


def shards(
    canvas,
    screen_size,
    tile_counts,
    tile_offsets,
    cotangent,
    dw_kernel,
    dw_bias,
    ln_gain,
    ln_bias,
    w_in,
    b_in,
    w_out,
    layer_scale,
):
    f32, bf16 = jnp.float32, jnp.bfloat16
    struct = pltpu.VMEM
    slots = tile_offsets.shape[0]
    share = canvas.shape[2]
    width = ln_gain.shape[0]
    hid = w_in.shape[1]
    rows = slots * TS * TS
    half = rows // 2
    lanes = share // 128
    offsets = tile_offsets.T
    left, right = shift(cotangent, 1), shift(cotangent, -1)
    mixed_a, mixed_b, near_out, taps = call(
        depthwise_kernel,
        [
            struct((half, share), bf16),
            struct((half, share), bf16),
            struct(w_out.shape, bf16),
            struct((lanes, 28, 8, 128), f32),
        ],
        [SMEM, SMEM, HBM, HBM, HBM, HBM],
        [
            pltpu.VMEM(canvas.shape, bf16),
            pltpu.VMEM((lanes, PAD_ROWS, PAD_COLS, 128), f32),
            pltpu.VMEM(dw_kernel.shape, bf16),
            pltpu.VMEM(dw_bias.shape, f32),
            pltpu.SemaphoreType.DMA((7,)),
        ],
    )(offsets, screen_size, canvas, dw_kernel, dw_bias, w_out)
    left_a, right_a = shift(mixed_a, 1), shift(mixed_a, -1)
    cot_a, cot_b = shift(left[: slots // 2], 1), shift(right[slots // 2 :], -1)
    opp_a, right_b = shift(left_a, 1), shift(mixed_b, -1)
    left_b, opp_b = shift(mixed_b, 1), shift(right_b, -1)
    canvas_like = struct((lanes, PAD_ROWS, PAD_COLS, 128), f32)
    hidden_a, hidden_b, taken, near_in, sides = call(
        hidden_kernel,
        [
            struct((half, hid), f32),
            struct((half, hid), f32),
            canvas_like,
            struct(w_in.shape, bf16),
            struct((8, hid), f32),
        ],
        [SMEM] * 2 + [VMEM] * 10 + [HBM],
        [pltpu.VMEM((rows, width), bf16), pltpu.SemaphoreType.DMA(())],
    )(
        offsets, tile_counts, cotangent, left, right, cot_a, cot_b,
        layer_scale, ln_gain, ln_bias, b_in, near_out, w_in,
    )
    message = struct((half + 16, share), bf16)

    def block(blocks, hidden, earlier):
        return call(
            block_kernel,
            [message, struct((half, hid), bf16), struct((half, 1), f32), struct((half, 1), f32)],
            [VMEM] * 11,
            [pltpu.VMEM((half, width), bf16), pltpu.VMEM((half, width), bf16)],
        )(*blocks, ln_gain, ln_bias, near_in, b_in, hidden, sides, earlier)

    def parts(keep_ahead, own_ahead, act, away, earlier):
        return call(
            functools.partial(parts_kernel, keep_ahead, own_ahead),
            [struct((half, share), bf16), message, struct((half, share), f32)],
            [VMEM] * 4,
        )(act, near_in, away, earlier)

    def middle(come, keep):
        return call(middle_kernel, [message], [VMEM] * 2)(come, keep)[0]

    away_a, act_a, centers_a, inverses_a = block((mixed_a, left_a, right_a, opp_a), hidden_a, mixed_b)
    come_a = shift(away_a, 1)
    keep_a, own_a, mine_a = parts(1, 3, act_a, away_a, away_a)
    got_a = shift(own_a, -1)
    away_b, act_b, centers_b, inverses_b = block((mixed_b, left_b, right_b, opp_b), hidden_b, keep_a)
    come_b = shift(away_b, -1)
    keep_b, own_b, mine_b = parts(3, 1, act_b, away_b, got_a)
    got_b = shift(own_b, 1)
    total_a = shift(middle(come_a, keep_a), 1)
    total_b = shift(middle(come_b, keep_b), -1)
    grown = call(
        first_tiles_kernel,
        [canvas_like],
        [SMEM] * 2 + [VMEM] * 11,
        [pltpu.VMEM((half, share), f32)],
    )(
        offsets, tile_counts, mine_a, got_a, total_a, come_a, away_a, mixed_a, centers_a, inverses_a,
        ln_gain, taps, taken,
    )[0]
    return call(
        last_tiles_kernel,
        jax.ShapeDtypeStruct(canvas.shape, f32),
        [SMEM] * 3 + [VMEM] * 11,
        [
            pltpu.VMEM((half, share), f32),
            pltpu.VMEM((lanes, PAD_ROWS, PAD_COLS, 128), f32),
            pltpu.VMEM(canvas.shape, f32),
            pltpu.SemaphoreType.DMA((4,)),
        ],
        out_specs=HBM,
    )(
        offsets, tile_counts, screen_size, mine_b, got_b, total_b, come_b, away_b, mixed_b, centers_b, inverses_b,
        ln_gain, taps, grown,
    )


def solution(mesh):
    return jax.shard_map(
        shards,
        mesh=mesh,
        in_specs=(
            P("img", None, "ch"),
            P("img", None),
            P(),
            P("img", None),
            P("img", None, None, "ch"),
            P(None, "ch"),
            P("ch"),
            P(),
            P(),
            P(None, "ch"),
            P("ch"),
            P("ch", None),
            P(),
        ),
        out_specs=P("img", None, "ch"),
        check_vma=False,
    )
```

```python
import functools

import jax
import jax.numpy as jnp
from jax import lax
from jax.experimental import pallas as pl
from jax.experimental.pallas import tpu as pltpu
from jax.sharding import PartitionSpec as P

TS = 4
SIDE = 32
PAD_ROWS = 38
PAD_COLS = 48
LEFT = 8

slope_coef = 0.7978845608
cubic_coef = 0.044715
norm_eps = 1e-06

VMEM = pl.BlockSpec(memory_space=pltpu.VMEM)
SMEM = pl.BlockSpec(memory_space=pltpu.SMEM)
HBM = pl.BlockSpec(memory_space=pltpu.HBM)


def call(kernel, out_shape, in_specs, scratch=(), limit=16, out_specs=None):
    run = pl.pallas_call(
        kernel,
        out_shape=out_shape,
        in_specs=in_specs,
        out_specs=out_specs or [VMEM] * len(out_shape),
        scratch_shapes=list(scratch),
        compiler_params=pltpu.CompilerParams(vmem_limit_bytes=limit << 20),
    )

    def held(*args):
        return run(
            *(
                pltpu.with_memory_space_constraint(a, pltpu.VMEM if spec is VMEM else pltpu.HBM)
                for spec, a in zip(in_specs, args, strict=True)
            )
        )

    return held


def inside_of(rows, row, height, width):
    column = lax.broadcasted_iota(jnp.int32, (rows, 128), 0)
    return (column < width) & (row < height)


def depthwise_kernel(
    offsets, screen, canvas, dwk, bias, w_out, mixed_a, mixed_b, near_out, taps, here, framed, kern_bf, bias_row, sems
):
    lanes = canvas.shape[2] // 128
    parts = 4
    deep = SIDE // parts
    height, width = screen[0, 0], screen[0, 1]
    small = [
        pltpu.make_async_copy(dwk, kern_bf, sems.at[parts]),
        pltpu.make_async_copy(bias, bias_row, sems.at[parts + 1]),
    ]
    rows_in = [
        pltpu.make_async_copy(
            canvas.at[pl.ds(g * deep, deep)], here.at[pl.ds(g * deep, deep)], sems.at[g]
        )
        for g in range(parts)
    ]
    weights = pltpu.make_async_copy(w_out, near_out, sems.at[parts + 2])
    for fetch in (*small, *rows_in, weights):
        fetch.start()
    low = lax.broadcasted_iota(jnp.int32, (8, 128), 0) < 4
    blank = jnp.zeros((PAD_COLS, 128), jnp.float32)
    for b in range(lanes):
        for y in (0, 1, 2, SIDE + 3, SIDE + 4, SIDE + 5):
            framed[b, y] = blank
    for fetch in small:
        fetch.wait()
    for b in range(lanes):
        kern = kern_bf[:, b * 128 : (b + 1) * 128].astype(jnp.float32)
        for i in range(7):
            for j in range(4):
                first = jnp.broadcast_to(kern[7 * i + j][None], (8, 128))
                if j < 3:
                    second = jnp.broadcast_to(kern[7 * i + j + 4][None], (8, 128))
                else:
                    second = jnp.zeros((8, 128), jnp.float32)
                taps[b, i * 4 + j] = jnp.where(low, first, second)

    def fill(y, carry):
        seen = inside_of(SIDE, y, height, width)
        for b in range(lanes):
            framed[b, y + 3, 0:LEFT, :] = blank[:LEFT]
            framed[b, y + 3, LEFT + SIDE : PAD_COLS, :] = blank[: PAD_COLS - LEFT - SIDE]
            row = here[y, :, b * 128 : (b + 1) * 128].astype(jnp.float32)
            framed[b, y + 3, LEFT : LEFT + SIDE, :] = jnp.where(seen, row, 0.0)
        return carry

    for g in range(parts):
        rows_in[g].wait()
        lax.fori_loop(g * deep, (g + 1) * deep, fill, 0, unroll=4)
    count = mixed_a.shape[0] // 16
    for b in range(lanes):
        cut = slice(b * 128, (b + 1) * 128)
        start = jnp.broadcast_to(bias_row[cut][None], (8, 128))
        for mixed, base in ((mixed_a, 0), (mixed_b, count)):

            def tile(t, carry):
                r, q = offsets[0, base + t], offsets[1, base + t]
                sums = [None] * 4
                for p in range(10):
                    for j in range(4):
                        seen = framed[b, r + p, pl.ds(q + (LEFT - 3 + j), 8), :]
                        for y in range(max(0, p - 6), min(3, p) + 1):
                            term = seen * taps[b, (p - y) * 4 + j]
                            sums[y] = term if sums[y] is None else sums[y] + term
                folded = [s + pltpu.roll(s, 4, 0) + start for s in sums]
                pair = [jnp.where(low, folded[y], folded[y + 1]) for y in (0, 2)]
                rows = pl.ds(pl.multiple_of(t * 16, 16), 16)
                mixed[rows, cut] = jnp.concatenate(pair, 0).astype(jnp.bfloat16)
                return carry

            lax.fori_loop(0, count, tile, 0, unroll=2)
    weights.wait()


def two_parts(row):
    high = row.astype(jnp.bfloat16).astype(jnp.float32)
    return [high, row - high]


def scaled_rows(cells, scale, begin):
    share = cells.shape[3]
    flat = cells[...].astype(jnp.float32).reshape(cells.shape[0] * 16, share)
    return (scale[pl.ds(begin, share)][None] * flat).astype(jnp.bfloat16)


def channels_of(ahead, share):
    return pl.multiple_of(lax.rem(lax.axis_index("ch") + ahead, 4) * share, 128)


def hidden_kernel(
    offsets, counts, own, left, right, scale, gain, bias, b_in, w_out, w_in,
    hidden, taken, near_in, sides, flat, sem,
):
    fetch = pltpu.make_async_copy(w_in, near_in, sem)
    fetch.start()
    share = own.shape[3]
    taken[...] = jnp.zeros_like(taken)

    def tile(t, carry):
        r, q = offsets[0, t], offsets[1, t]
        for y in range(4):
            cells = own[t, y].astype(jnp.float32)
            for b in range(share // 128):
                taken[b, r + 3 + y, pl.ds(q + LEFT, 4), :] += cells[:, b * 128 : (b + 1) * 128]
        return carry

    lax.fori_loop(0, counts[lax.axis_index("img")], tile, 0)
    begins = []
    for k, (cells, ahead) in enumerate(((own, 0), (left, 3), (right, 1))):
        begins.append(channels_of(ahead, share))
        flat[k] = scaled_rows(cells, scale, begins[k])
    step = 512
    for n in range(0, hidden.shape[1], step):
        total = None
        for k, begin in enumerate(begins):
            product = lax.dot_general(
                flat[k],
                w_out[n : n + step, pl.ds(begin, share)],
                (((1,), (1,)), ((), ())),
                preferred_element_type=jnp.float32,
            )
            total = product if total is None else total + product
        hidden[:, n : n + step] = total
    width = gain.shape[0]
    lines = two_parts(gain[...][None]) + two_parts(bias[...][None])
    lines = jnp.concatenate(lines + [jnp.zeros((12, width), jnp.float32)], 0).astype(jnp.bfloat16)
    fetch.wait()
    both = jnp.dot(lines, near_in[...], preferred_element_type=jnp.float32)
    sides[0:1, :] = both[0:1] + both[1:2]
    sides[1:2, :] = both[2:3] + both[3:4] + b_in[...][None]


def opposite_kernel(before, cot_a, cot_b, scale, w_out, hidden_a, hidden_b, flat):
    rows, share = flat.shape
    half = rows // 2
    begin = channels_of(2, share)
    flat[:half, :] = scaled_rows(cot_a, scale, begin)
    flat[half:, :] = scaled_rows(cot_b, scale, begin)
    step = 512
    for n in range(0, before.shape[1], step):
        product = lax.dot_general(
            flat[...],
            w_out[n : n + step, pl.ds(begin, share)],
            (((1,), (1,)), ((), ())),
            preferred_element_type=jnp.float32,
        )
        hidden_a[:, n : n + step] = before[:half, n : n + step] + product[:half]
        hidden_b[:, n : n + step] = before[half:, n : n + step] + product[half:]


def gelu_slope(v):
    square = v * v
    t = jnp.tanh(slope_coef * (v + cubic_coef * square * v))
    return 0.5 * (1.0 + t) + 0.5 * v * (1.0 - t * t) * slope_coef * (1.0 + 3.0 * cubic_coef * square)


def as_rows(column):
    count = column.shape[0] // 128
    eye = lax.broadcasted_iota(jnp.int32, (128, 128), 0) == lax.broadcasted_iota(jnp.int32, (128, 128), 1)
    return jnp.concatenate(
        [
            jnp.sum(jnp.where(eye, column[g * 128 : (g + 1) * 128], 0.0), axis=0, keepdims=True)
            for g in range(count)
        ],
        0,
    )


def as_column(rows):
    eye = lax.broadcasted_iota(jnp.int32, (128, 128), 0) == lax.broadcasted_iota(jnp.int32, (128, 128), 1)
    return jnp.concatenate(
        [
            jnp.sum(jnp.where(eye, rows[g : g + 1], 0.0), axis=1, keepdims=True)
            for g in range(rows.shape[0])
        ],
        0,
    )


def part_of(act, w_in, ahead):
    share = w_in.shape[0] // 4
    return lax.dot_general(
        act[...],
        w_in[pl.ds(channels_of(ahead, share), share), :],
        (((1,), (1,)), ((), ())),
        preferred_element_type=jnp.float32,
    )


def block_kernel(
    own, left, right, opp, gain, bias, w_in, b_in, hidden, sides,
    away, act, centers, inverses, full, scaled,
):
    rows, width = full.shape
    share = own.shape[1]
    for ref, ahead in ((own, 0), (left, 3), (right, 1), (opp, 2)):
        full[:, pl.ds(channels_of(ahead, share), share)] = ref[...]
    step = 64
    for m in range(0, rows, step):
        values = full[m : m + step, :].astype(jnp.float32)
        center = jnp.mean(values, axis=1, keepdims=True)
        apart = values - center
        inverse = lax.rsqrt(jnp.mean(apart * apart, axis=1, keepdims=True) + norm_eps)
        centers[m : m + step, :] = center
        inverses[m : m + step, :] = inverse
        scaled[m : m + step, :] = (apart * inverse * gain[...][None] + bias[...][None]).astype(
            jnp.bfloat16
        )
    step = 512
    first = jnp.zeros((rows, 128), jnp.float32)
    second = jnp.zeros((rows, 128), jnp.float32)
    for n in range(0, width, step):
        span = slice(n, n + step)
        product = jnp.dot(scaled[...], w_in[:, span], preferred_element_type=jnp.float32)
        pre = product + b_in[span][None]
        rounded = (hidden[:, span] * gelu_slope(pre)).astype(jnp.bfloat16)
        act[:, span] = rounded
        value = rounded.astype(jnp.float32)
        one = value * sides[0:1, span]
        two = value * (pre - sides[1:2, span])
        for k in range(0, step, 128):
            first = first + one[:, k : k + 128]
            second = second + two[:, k : k + 128]
    away[:rows, :] = part_of(act, w_in, 2).astype(jnp.bfloat16)
    packed = []
    for sums in (first, second):
        packed += two_parts(as_rows(jnp.sum(sums, axis=1, keepdims=True)))
    packed += [jnp.zeros((16 - 4 * (rows // 128), 128), jnp.float32)]
    away[rows : rows + 16, :] = jnp.zeros((16, share), jnp.bfloat16)
    away[rows : rows + 16, :128] = jnp.concatenate(packed, 0).astype(jnp.bfloat16)


def parts_kernel(keep_ahead, own_ahead, act, w_in, away, keep, own, mine):
    rows = act.shape[0]
    own[:rows, :] = part_of(act, w_in, own_ahead).astype(jnp.bfloat16)
    own[rows:, :] = away[rows:, :]
    keep[...] = part_of(act, w_in, keep_ahead).astype(jnp.bfloat16)
    mine[...] = part_of(act, w_in, 0)


def middle_kernel(come, keep, go):
    rows = keep.shape[0]
    total = keep[...].astype(jnp.float32) + come[:rows, :].astype(jnp.float32)
    go[:rows, :] = total.astype(jnp.bfloat16)
    go[rows:, :] = come[rows:, :]


def add_tiles(
    base, offsets, counts, mine, got, total, come, away, mixed, centers, inverses, gain, taps, upstream, grown
):
    rows, share = mixed.shape
    width = gain.shape[0]
    packed = None
    for ref in (away, come, got, total):
        lines = ref[rows : rows + 16, :128].astype(jnp.float32)
        packed = lines if packed is None else packed + lines
    n = rows // 128
    first = as_column((packed[0:n] + packed[n : 2 * n]) * (1.0 / width))
    second = as_column((packed[2 * n : 3 * n] + packed[3 * n : 4 * n]) * (1.0 / width))
    weight = gain[pl.ds(channels_of(0, share), share)][None]
    step = 64
    for m in range(0, rows, step):
        span = slice(m, m + step)
        norm_grad = mine[span, :] + got[span, :].astype(jnp.float32) + total[span, :].astype(jnp.float32)
        inverse = inverses[span, :]
        normed = (mixed[span, :].astype(jnp.float32) - centers[span, :]) * inverse
        upstream[span, :] = inverse * (norm_grad * weight - first[span] - normed * second[span])

    low = lax.broadcasted_iota(jnp.int32, (8, 128), 0) < 4

    def tile(t, carry):
        r, q = offsets[0, base + t], offsets[1, base + t]
        for b in range(share // 128):
            doubled = []
            for h in range(2):
                pair = upstream[pl.ds(pl.multiple_of(t * 16 + 8 * h, 8), 8), b * 128 : (b + 1) * 128]
                turned = pltpu.roll(pair, 4, 0)
                doubled += [jnp.where(low, pair, turned), jnp.where(low, turned, pair)]
            for j in range(4):
                columns = pl.ds(q + (LEFT - 3 + j), 8)
                for y in range(10):
                    more = None
                    for k in range(max(0, y - 6), min(3, y) + 1):
                        term = doubled[k] * taps[b, (y - k) * 4 + j]
                        more = term if more is None else more + term
                    grown[b, r + y, columns, :] += more
        return carry

    listed = counts[lax.axis_index("img")] - base
    lax.fori_loop(0, jnp.clip(listed, 0, rows // 16), tile, 0)


def first_tiles_kernel(
    offsets, counts, mine, got, total, come, away, mixed, centers, inverses, gain, taps, before,
    grown, upstream,
):
    grown[...] = before[...]
    add_tiles(
        0, offsets, counts, mine, got, total, come, away, mixed, centers, inverses, gain, taps, upstream, grown
    )


def last_tiles_kernel(
    offsets, counts, screen, mine, got, total, come, away, mixed, centers, inverses, gain, taps, before,
    grad, upstream, grown, stage, sems,
):
    grown[...] = before[...]
    add_tiles(
        mixed.shape[0] // 16,
        offsets, counts, mine, got, total, come, away, mixed, centers, inverses, gain, taps, upstream, grown,
    )
    height, width = screen[0, 0], screen[0, 1]
    stores = []
    deep = SIDE // 4
    for g in range(4):

        def line(y, carry):
            seen = inside_of(SIDE, y, height, width)
            for b in range(mixed.shape[1] // 128):
                whole = grown[b, y + 3, LEFT : LEFT + SIDE, :]
                stage[y, :, b * 128 : (b + 1) * 128] = jnp.where(seen, whole, 0.0)
            return carry

        lax.fori_loop(g * deep, (g + 1) * deep, line, 0, unroll=4)
        part = pl.ds(g * deep, deep)
        store = pltpu.make_async_copy(stage.at[part], grad.at[part], sems.at[g])
        store.start()
        stores.append(store)
    for store in stores:
        store.wait()


def shift(x, by):
    n = lax.axis_size("ch")
    return lax.ppermute(x, "ch", [(i, (i + by) % n) for i in range(n)])


def shards(
    canvas,
    screen_size,
    tile_counts,
    tile_offsets,
    cotangent,
    dw_kernel,
    dw_bias,
    ln_gain,
    ln_bias,
    w_in,
    b_in,
    w_out,
    layer_scale,
):
    f32, bf16 = jnp.float32, jnp.bfloat16
    struct = pltpu.VMEM
    slots = tile_offsets.shape[0]
    share = canvas.shape[2]
    width = ln_gain.shape[0]
    hid = w_in.shape[1]
    rows = slots * TS * TS
    half = rows // 2
    lanes = share // 128
    offsets = tile_offsets.T
    left, right = shift(cotangent, 1), shift(cotangent, -1)
    mixed_a, mixed_b, near_out, taps = call(
        depthwise_kernel,
        [
            struct((half, share), bf16),
            struct((half, share), bf16),
            struct(w_out.shape, bf16),
            struct((lanes, 28, 8, 128), f32),
        ],
        [SMEM, SMEM, HBM, HBM, HBM, HBM],
        [
            pltpu.VMEM(canvas.shape, bf16),
            pltpu.VMEM((lanes, PAD_ROWS, PAD_COLS, 128), f32),
            pltpu.VMEM(dw_kernel.shape, bf16),
            pltpu.VMEM(dw_bias.shape, f32),
            pltpu.SemaphoreType.DMA((7,)),
        ],
    )(offsets, screen_size, canvas, dw_kernel, dw_bias, w_out)
    left_a, right_a = shift(mixed_a, 1), shift(mixed_a, -1)
    cot_a, cot_b = shift(left[: slots // 2], 1), shift(right[slots // 2 :], -1)
    right_b, left_b = shift(mixed_b, -1), shift(mixed_b, 1)
    canvas_like = struct((lanes, PAD_ROWS, PAD_COLS, 128), f32)
    hidden, taken, near_in, sides = call(
        hidden_kernel,
        [struct((rows, hid), f32), canvas_like, struct(w_in.shape, bf16), struct((8, hid), f32)],
        [SMEM] * 2 + [VMEM] * 8 + [HBM],
        [pltpu.VMEM((3, rows, share), bf16), pltpu.SemaphoreType.DMA(())],
    )(
        offsets, tile_counts, cotangent, left, right, layer_scale, ln_gain, ln_bias, b_in, near_out, w_in
    )
    forward_a, forward_b, sides = lax.optimization_barrier((left_a, right_b, sides))
    opp_a, opp_b = shift(forward_a, 1), shift(forward_b, -1)
    hidden_a, hidden_b = call(
        opposite_kernel,
        [struct((half, hid), f32)] * 2,
        [VMEM] * 5,
        [pltpu.VMEM((rows, share), bf16)],
    )(hidden, cot_a, cot_b, layer_scale, near_out)
    message = struct((half + 16, share), bf16)

    def block(blocks, hidden):
        return call(
            block_kernel,
            [message, struct((half, hid), bf16), struct((half, 1), f32), struct((half, 1), f32)],
            [VMEM] * 10,
            [pltpu.VMEM((half, width), bf16), pltpu.VMEM((half, width), bf16)],
        )(*blocks, ln_gain, ln_bias, near_in, b_in, hidden, sides)

    def parts(keep_ahead, own_ahead, act, away):
        return call(
            functools.partial(parts_kernel, keep_ahead, own_ahead),
            [struct((half, share), bf16), message, struct((half, share), f32)],
            [VMEM] * 3,
        )(act, near_in, away)

    def middle(come, keep):
        return call(middle_kernel, [message], [VMEM] * 2)(come, keep)[0]

    away_a, act_a, centers_a, inverses_a = block((mixed_a, left_a, right_a, opp_a), hidden_a)
    come_a = shift(away_a, 1)
    keep_a, own_a, mine_a = parts(1, 3, act_a, away_a)
    got_a = shift(own_a, -1)
    away_b, act_b, centers_b, inverses_b = block((mixed_b, left_b, right_b, opp_b), hidden_b)
    come_b = shift(away_b, -1)
    keep_b, own_b, mine_b = parts(3, 1, act_b, away_b)
    got_b = shift(own_b, 1)
    total_a = shift(middle(come_a, keep_a), 1)
    total_b = shift(middle(come_b, keep_b), -1)
    grown = call(
        first_tiles_kernel,
        [canvas_like],
        [SMEM] * 2 + [VMEM] * 11,
        [pltpu.VMEM((half, share), f32)],
    )(
        offsets, tile_counts, mine_a, got_a, total_a, come_a, away_a, mixed_a, centers_a, inverses_a,
        ln_gain, taps, taken,
    )[0]
    return call(
        last_tiles_kernel,
        jax.ShapeDtypeStruct(canvas.shape, f32),
        [SMEM] * 3 + [VMEM] * 11,
        [
            pltpu.VMEM((half, share), f32),
            pltpu.VMEM((lanes, PAD_ROWS, PAD_COLS, 128), f32),
            pltpu.VMEM(canvas.shape, f32),
            pltpu.SemaphoreType.DMA((4,)),
        ],
        out_specs=HBM,
    )(
        offsets, tile_counts, screen_size, mine_b, got_b, total_b, come_b, away_b, mixed_b, centers_b, inverses_b,
        ln_gain, taps, grown,
    )


def solution(mesh):
    return jax.shard_map(
        shards,
        mesh=mesh,
        in_specs=(
            P("img", None, "ch"),
            P("img", None),
            P(),
            P("img", None),
            P("img", None, None, "ch"),
            P(None, "ch"),
            P("ch"),
            P(),
            P(),
            P(None, "ch"),
            P("ch"),
            P("ch", None),
            P(),
        ),
        out_specs=P("img", None, "ch"),
        check_vma=False,
    )
```

```python
import functools

import jax
import jax.numpy as jnp
from jax import lax
from jax.experimental import pallas as pl
from jax.experimental.pallas import tpu as pltpu
from jax.sharding import PartitionSpec as P

TS = 4
SIDE = 32
PAD_ROWS = 38
PAD_COLS = 48
LEFT = 8

slope_coef = 0.7978845608
cubic_coef = 0.044715
norm_eps = 1e-06

VMEM = pl.BlockSpec(memory_space=pltpu.VMEM)
SMEM = pl.BlockSpec(memory_space=pltpu.SMEM)
HBM = pl.BlockSpec(memory_space=pltpu.HBM)


def call(kernel, out_shape, in_specs, scratch=(), limit=16, out_specs=None):
    run = pl.pallas_call(
        kernel,
        out_shape=out_shape,
        in_specs=in_specs,
        out_specs=out_specs or [VMEM] * len(out_shape),
        scratch_shapes=list(scratch),
        compiler_params=pltpu.CompilerParams(vmem_limit_bytes=limit << 20),
    )

    def held(*args):
        return run(
            *(
                pltpu.with_memory_space_constraint(a, pltpu.VMEM if spec is VMEM else pltpu.HBM)
                for spec, a in zip(in_specs, args, strict=True)
            )
        )

    return held


def inside_of(rows, row, height, width):
    column = lax.broadcasted_iota(jnp.int32, (rows, 128), 0)
    return (column < width) & (row < height)


def depthwise_kernel(
    offsets, screen, canvas, dwk, bias, w_out, mixed_a, mixed_b, near_out, taps, here, framed, kern_bf, bias_row, sems
):
    lanes = canvas.shape[2] // 128
    parts = 4
    deep = SIDE // parts
    height, width = screen[0, 0], screen[0, 1]
    small = [
        pltpu.make_async_copy(dwk, kern_bf, sems.at[parts]),
        pltpu.make_async_copy(bias, bias_row, sems.at[parts + 1]),
    ]
    rows_in = [
        pltpu.make_async_copy(
            canvas.at[pl.ds(g * deep, deep)], here.at[pl.ds(g * deep, deep)], sems.at[g]
        )
        for g in range(parts)
    ]
    weights = pltpu.make_async_copy(w_out, near_out, sems.at[parts + 2])
    for fetch in (*small, *rows_in, weights):
        fetch.start()
    low = lax.broadcasted_iota(jnp.int32, (8, 128), 0) < 4
    blank = jnp.zeros((PAD_COLS, 128), jnp.float32)
    for b in range(lanes):
        for y in (0, 1, 2, SIDE + 3, SIDE + 4, SIDE + 5):
            framed[b, y] = blank
    for fetch in small:
        fetch.wait()
    for b in range(lanes):
        kern = kern_bf[:, b * 128 : (b + 1) * 128].astype(jnp.float32)
        for i in range(7):
            for j in range(4):
                first = jnp.broadcast_to(kern[7 * i + j][None], (8, 128))
                if j < 3:
                    second = jnp.broadcast_to(kern[7 * i + j + 4][None], (8, 128))
                else:
                    second = jnp.zeros((8, 128), jnp.float32)
                taps[b, i * 4 + j] = jnp.where(low, first, second)

    def fill(y, carry):
        seen = inside_of(SIDE, y, height, width)
        for b in range(lanes):
            framed[b, y + 3, 0:LEFT, :] = blank[:LEFT]
            framed[b, y + 3, LEFT + SIDE : PAD_COLS, :] = blank[: PAD_COLS - LEFT - SIDE]
            row = here[y, :, b * 128 : (b + 1) * 128].astype(jnp.float32)
            framed[b, y + 3, LEFT : LEFT + SIDE, :] = jnp.where(seen, row, 0.0)
        return carry

    for g in range(parts):
        rows_in[g].wait()
        lax.fori_loop(g * deep, (g + 1) * deep, fill, 0, unroll=4)
    count = mixed_a.shape[0] // 16
    for b in range(lanes):
        cut = slice(b * 128, (b + 1) * 128)
        start = jnp.broadcast_to(bias_row[cut][None], (8, 128))
        for mixed, base in ((mixed_a, 0), (mixed_b, count)):

            def tile(t, carry):
                r, q = offsets[0, base + t], offsets[1, base + t]
                sums = [None] * 4
                for p in range(10):
                    for j in range(4):
                        seen = framed[b, r + p, pl.ds(q + (LEFT - 3 + j), 8), :]
                        for y in range(max(0, p - 6), min(3, p) + 1):
                            term = seen * taps[b, (p - y) * 4 + j]
                            sums[y] = term if sums[y] is None else sums[y] + term
                folded = [s + pltpu.roll(s, 4, 0) + start for s in sums]
                pair = [jnp.where(low, folded[y], folded[y + 1]) for y in (0, 2)]
                rows = pl.ds(pl.multiple_of(t * 16, 16), 16)
                mixed[rows, cut] = jnp.concatenate(pair, 0).astype(jnp.bfloat16)
                return carry

            lax.fori_loop(0, count, tile, 0, unroll=2)
    weights.wait()


def two_parts(row):
    high = row.astype(jnp.bfloat16).astype(jnp.float32)
    return [high, row - high]


def scaled_rows(cells, scale, begin):
    share = cells.shape[3]
    flat = cells[...].astype(jnp.float32).reshape(cells.shape[0] * 16, share)
    return (scale[pl.ds(begin, share)][None] * flat).astype(jnp.bfloat16)


def channels_of(ahead, share):
    return pl.multiple_of(lax.rem(lax.axis_index("ch") + ahead, 4) * share, 128)


def hidden_kernel(
    offsets, counts, own, left, right, scale, gain, bias, b_in, w_out, earlier, w_in,
    hidden_a, hidden_b, taken, near_in, sides, flat, sem,
):
    del earlier
    fetch = pltpu.make_async_copy(w_in, near_in, sem)
    fetch.start()
    share = own.shape[3]
    taken[...] = jnp.zeros_like(taken)

    def tile(t, carry):
        r, q = offsets[0, t], offsets[1, t]
        for y in range(4):
            cells = own[t, y].astype(jnp.float32)
            for b in range(share // 128):
                taken[b, r + 3 + y, pl.ds(q + LEFT, 4), :] += cells[:, b * 128 : (b + 1) * 128]
        return carry

    lax.fori_loop(0, counts[lax.axis_index("img")], tile, 0)
    begins = []
    for k, (cells, ahead) in enumerate(((own, 0), (left, 3), (right, 1))):
        begins.append(channels_of(ahead, share))
        flat[k] = scaled_rows(cells, scale, begins[k])
    step = 512
    for n in range(0, hidden_a.shape[1], step):
        total = None
        for k, begin in enumerate(begins):
            product = lax.dot_general(
                flat[k],
                w_out[n : n + step, pl.ds(begin, share)],
                (((1,), (1,)), ((), ())),
                preferred_element_type=jnp.float32,
            )
            total = product if total is None else total + product
        hidden_a[:, n : n + step] = total[: hidden_a.shape[0]]
        hidden_b[:, n : n + step] = total[hidden_a.shape[0] :]
    width = gain.shape[0]
    lines = two_parts(gain[...][None]) + two_parts(bias[...][None])
    lines = jnp.concatenate(lines + [jnp.zeros((12, width), jnp.float32)], 0).astype(jnp.bfloat16)
    fetch.wait()
    both = jnp.dot(lines, near_in[...], preferred_element_type=jnp.float32)
    sides[0:1, :] = both[0:1] + both[1:2]
    sides[1:2, :] = both[2:3] + both[3:4] + b_in[...][None]


def opposite_kernel(before, cot, scale, w_out, earlier, hidden, flat):
    del earlier
    share = flat.shape[1]
    begin = channels_of(2, share)
    flat[...] = scaled_rows(cot, scale, begin)
    step = 512
    for n in range(0, before.shape[1], step):
        hidden[:, n : n + step] = before[:, n : n + step] + lax.dot_general(
            flat[...],
            w_out[n : n + step, pl.ds(begin, share)],
            (((1,), (1,)), ((), ())),
            preferred_element_type=jnp.float32,
        )


def gelu_slope(v):
    square = v * v
    t = jnp.tanh(slope_coef * (v + cubic_coef * square * v))
    return 0.5 * (1.0 + t) + 0.5 * v * (1.0 - t * t) * slope_coef * (1.0 + 3.0 * cubic_coef * square)


def as_rows(column):
    count = column.shape[0] // 128
    eye = lax.broadcasted_iota(jnp.int32, (128, 128), 0) == lax.broadcasted_iota(jnp.int32, (128, 128), 1)
    return jnp.concatenate(
        [
            jnp.sum(jnp.where(eye, column[g * 128 : (g + 1) * 128], 0.0), axis=0, keepdims=True)
            for g in range(count)
        ],
        0,
    )


def as_column(rows):
    eye = lax.broadcasted_iota(jnp.int32, (128, 128), 0) == lax.broadcasted_iota(jnp.int32, (128, 128), 1)
    return jnp.concatenate(
        [
            jnp.sum(jnp.where(eye, rows[g : g + 1], 0.0), axis=1, keepdims=True)
            for g in range(rows.shape[0])
        ],
        0,
    )


def part_of(act, w_in, ahead):
    share = w_in.shape[0] // 4
    return lax.dot_general(
        act[...],
        w_in[pl.ds(channels_of(ahead, share), share), :],
        (((1,), (1,)), ((), ())),
        preferred_element_type=jnp.float32,
    )


def block_kernel(
    own, left, right, opp, gain, bias, w_in, b_in, hidden, sides,
    away, act, centers, inverses, full, scaled,
):
    rows, width = full.shape
    share = own.shape[1]
    for ref, ahead in ((own, 0), (left, 3), (right, 1), (opp, 2)):
        full[:, pl.ds(channels_of(ahead, share), share)] = ref[...]
    step = 64
    for m in range(0, rows, step):
        values = full[m : m + step, :].astype(jnp.float32)
        center = jnp.mean(values, axis=1, keepdims=True)
        apart = values - center
        inverse = lax.rsqrt(jnp.mean(apart * apart, axis=1, keepdims=True) + norm_eps)
        centers[m : m + step, :] = center
        inverses[m : m + step, :] = inverse
        scaled[m : m + step, :] = (apart * inverse * gain[...][None] + bias[...][None]).astype(
            jnp.bfloat16
        )
    step = 512
    first = jnp.zeros((rows, 128), jnp.float32)
    second = jnp.zeros((rows, 128), jnp.float32)
    for n in range(0, width, step):
        span = slice(n, n + step)
        product = jnp.dot(scaled[...], w_in[:, span], preferred_element_type=jnp.float32)
        pre = product + b_in[span][None]
        rounded = (hidden[:, span] * gelu_slope(pre)).astype(jnp.bfloat16)
        act[:, span] = rounded
        value = rounded.astype(jnp.float32)
        one = value * sides[0:1, span]
        two = value * (pre - sides[1:2, span])
        for k in range(0, step, 128):
            first = first + one[:, k : k + 128]
            second = second + two[:, k : k + 128]
    away[:rows, :] = part_of(act, w_in, 2).astype(jnp.bfloat16)
    packed = []
    for sums in (first, second):
        packed += two_parts(as_rows(jnp.sum(sums, axis=1, keepdims=True)))
    packed += [jnp.zeros((16 - 4 * (rows // 128), 128), jnp.float32)]
    away[rows : rows + 16, :] = jnp.zeros((16, share), jnp.bfloat16)
    away[rows : rows + 16, :128] = jnp.concatenate(packed, 0).astype(jnp.bfloat16)


def parts_kernel(keep_ahead, own_ahead, act, w_in, away, keep, own, mine):
    rows = act.shape[0]
    own[:rows, :] = part_of(act, w_in, own_ahead).astype(jnp.bfloat16)
    own[rows:, :] = away[rows:, :]
    keep[...] = part_of(act, w_in, keep_ahead).astype(jnp.bfloat16)
    mine[...] = part_of(act, w_in, 0)


def middle_kernel(come, keep, go):
    rows = keep.shape[0]
    total = keep[...].astype(jnp.float32) + come[:rows, :].astype(jnp.float32)
    go[:rows, :] = total.astype(jnp.bfloat16)
    go[rows:, :] = come[rows:, :]


def add_tiles(
    base, offsets, counts, mine, got, total, come, away, mixed, centers, inverses, gain, taps, upstream, grown
):
    rows, share = mixed.shape
    width = gain.shape[0]
    packed = None
    for ref in (away, come, got, total):
        lines = ref[rows : rows + 16, :128].astype(jnp.float32)
        packed = lines if packed is None else packed + lines
    n = rows // 128
    first = as_column((packed[0:n] + packed[n : 2 * n]) * (1.0 / width))
    second = as_column((packed[2 * n : 3 * n] + packed[3 * n : 4 * n]) * (1.0 / width))
    weight = gain[pl.ds(channels_of(0, share), share)][None]
    step = 64
    for m in range(0, rows, step):
        span = slice(m, m + step)
        norm_grad = mine[span, :] + got[span, :].astype(jnp.float32) + total[span, :].astype(jnp.float32)
        inverse = inverses[span, :]
        normed = (mixed[span, :].astype(jnp.float32) - centers[span, :]) * inverse
        upstream[span, :] = inverse * (norm_grad * weight - first[span] - normed * second[span])

    low = lax.broadcasted_iota(jnp.int32, (8, 128), 0) < 4

    def tile(t, carry):
        r, q = offsets[0, base + t], offsets[1, base + t]
        for b in range(share // 128):
            doubled = []
            for h in range(2):
                pair = upstream[pl.ds(pl.multiple_of(t * 16 + 8 * h, 8), 8), b * 128 : (b + 1) * 128]
                turned = pltpu.roll(pair, 4, 0)
                doubled += [jnp.where(low, pair, turned), jnp.where(low, turned, pair)]
            for j in range(4):
                columns = pl.ds(q + (LEFT - 3 + j), 8)
                for y in range(10):
                    more = None
                    for k in range(max(0, y - 6), min(3, y) + 1):
                        term = doubled[k] * taps[b, (y - k) * 4 + j]
                        more = term if more is None else more + term
                    grown[b, r + y, columns, :] += more
        return carry

    listed = counts[lax.axis_index("img")] - base
    lax.fori_loop(0, jnp.clip(listed, 0, rows // 16), tile, 0)


def first_tiles_kernel(
    offsets, counts, mine, got, total, come, away, mixed, centers, inverses, gain, taps, before,
    grown, upstream,
):
    grown[...] = before[...]
    add_tiles(
        0, offsets, counts, mine, got, total, come, away, mixed, centers, inverses, gain, taps, upstream, grown
    )


def last_tiles_kernel(
    offsets, counts, screen, mine, got, total, come, away, mixed, centers, inverses, gain, taps, before,
    grad, upstream, grown, stage, sems,
):
    grown[...] = before[...]
    add_tiles(
        mixed.shape[0] // 16,
        offsets, counts, mine, got, total, come, away, mixed, centers, inverses, gain, taps, upstream, grown,
    )
    height, width = screen[0, 0], screen[0, 1]
    stores = []
    deep = SIDE // 4
    for g in range(4):

        def line(y, carry):
            seen = inside_of(SIDE, y, height, width)
            for b in range(mixed.shape[1] // 128):
                whole = grown[b, y + 3, LEFT : LEFT + SIDE, :]
                stage[y, :, b * 128 : (b + 1) * 128] = jnp.where(seen, whole, 0.0)
            return carry

        lax.fori_loop(g * deep, (g + 1) * deep, line, 0, unroll=4)
        part = pl.ds(g * deep, deep)
        store = pltpu.make_async_copy(stage.at[part], grad.at[part], sems.at[g])
        store.start()
        stores.append(store)
    for store in stores:
        store.wait()


def shift(x, by):
    n = lax.axis_size("ch")
    return lax.ppermute(x, "ch", [(i, (i + by) % n) for i in range(n)])


def shards(
    canvas,
    screen_size,
    tile_counts,
    tile_offsets,
    cotangent,
    dw_kernel,
    dw_bias,
    ln_gain,
    ln_bias,
    w_in,
    b_in,
    w_out,
    layer_scale,
):
    f32, bf16 = jnp.float32, jnp.bfloat16
    struct = pltpu.VMEM
    slots = tile_offsets.shape[0]
    share = canvas.shape[2]
    width = ln_gain.shape[0]
    hid = w_in.shape[1]
    rows = slots * TS * TS
    half = rows // 2
    lanes = share // 128
    offsets = tile_offsets.T
    left, right = shift(cotangent, 1), shift(cotangent, -1)
    mixed_a, mixed_b, near_out, taps = call(
        depthwise_kernel,
        [
            struct((half, share), bf16),
            struct((half, share), bf16),
            struct(w_out.shape, bf16),
            struct((lanes, 28, 8, 128), f32),
        ],
        [SMEM, SMEM, HBM, HBM, HBM, HBM],
        [
            pltpu.VMEM(canvas.shape, bf16),
            pltpu.VMEM((lanes, PAD_ROWS, PAD_COLS, 128), f32),
            pltpu.VMEM(dw_kernel.shape, bf16),
            pltpu.VMEM(dw_bias.shape, f32),
            pltpu.SemaphoreType.DMA((7,)),
        ],
    )(offsets, screen_size, canvas, dw_kernel, dw_bias, w_out)
    left_a, right_a = shift(mixed_a, 1), shift(mixed_a, -1)
    cot_a = shift(right[: slots // 2], -1)
    second, right = lax.optimization_barrier((mixed_b, right))
    left_b, right_b = shift(second, 1), shift(second, -1)
    opp_a = shift(left_a, 1)
    canvas_like = struct((lanes, PAD_ROWS, PAD_COLS, 128), f32)
    hidden_a, hidden_b, taken, near_in, sides = call(
        hidden_kernel,
        [struct((half, hid), f32), struct((half, hid), f32), canvas_like, struct(w_in.shape, bf16), struct((8, hid), f32)],
        [SMEM] * 2 + [VMEM] * 9 + [HBM],
        [pltpu.VMEM((3, rows, share), bf16), pltpu.SemaphoreType.DMA(())],
    )(
        offsets, tile_counts, cotangent, left, right, layer_scale, ln_gain, ln_bias, b_in, near_out, right_a, w_in
    )
    forward_b, forward_cot, sides = lax.optimization_barrier((left_b, right, sides))
    cot_b = shift(forward_cot[slots // 2 :], -1)
    opp_b = shift(forward_b, 1)

    def with_opposite(hidden, cot):
        return call(
            opposite_kernel,
            [struct((half, hid), f32)],
            [VMEM] * 5,
            [pltpu.VMEM((half, share), bf16)],
        )(hidden, cot, layer_scale, near_out, right_b)[0]

    message = struct((half + 16, share), bf16)

    def block(blocks, hidden):
        return call(
            block_kernel,
            [message, struct((half, hid), bf16), struct((half, 1), f32), struct((half, 1), f32)],
            [VMEM] * 10,
            [pltpu.VMEM((half, width), bf16), pltpu.VMEM((half, width), bf16)],
        )(*blocks, ln_gain, ln_bias, near_in, b_in, hidden, sides)

    def parts(keep_ahead, own_ahead, act, away):
        return call(
            functools.partial(parts_kernel, keep_ahead, own_ahead),
            [struct((half, share), bf16), message, struct((half, share), f32)],
            [VMEM] * 3,
        )(act, near_in, away)

    def middle(come, keep):
        return call(middle_kernel, [message], [VMEM] * 2)(come, keep)[0]

    away_a, act_a, centers_a, inverses_a = block((mixed_a, left_a, right_a, opp_a), with_opposite(hidden_a, cot_a))
    come_a = shift(away_a, 1)
    keep_a, own_a, mine_a = parts(1, 3, act_a, away_a)
    got_a = shift(own_a, -1)
    away_b, act_b, centers_b, inverses_b = block((mixed_b, left_b, right_b, opp_b), with_opposite(hidden_b, cot_b))
    come_b = shift(away_b, -1)
    keep_b, own_b, mine_b = parts(3, 1, act_b, away_b)
    got_b = shift(own_b, 1)
    total_a = shift(middle(come_a, keep_a), 1)
    total_b = shift(middle(come_b, keep_b), -1)
    grown = call(
        first_tiles_kernel,
        [canvas_like],
        [SMEM] * 2 + [VMEM] * 11,
        [pltpu.VMEM((half, share), f32)],
    )(
        offsets, tile_counts, mine_a, got_a, total_a, come_a, away_a, mixed_a, centers_a, inverses_a,
        ln_gain, taps, taken,
    )[0]
    return call(
        last_tiles_kernel,
        jax.ShapeDtypeStruct(canvas.shape, f32),
        [SMEM] * 3 + [VMEM] * 11,
        [
            pltpu.VMEM((half, share), f32),
            pltpu.VMEM((lanes, PAD_ROWS, PAD_COLS, 128), f32),
            pltpu.VMEM(canvas.shape, f32),
            pltpu.SemaphoreType.DMA((4,)),
        ],
        out_specs=HBM,
    )(
        offsets, tile_counts, screen_size, mine_b, got_b, total_b, come_b, away_b, mixed_b, centers_b, inverses_b,
        ln_gain, taps, grown,
    )


def solution(mesh):
    return jax.shard_map(
        shards,
        mesh=mesh,
        in_specs=(
            P("img", None, "ch"),
            P("img", None),
            P(),
            P("img", None),
            P("img", None, None, "ch"),
            P(None, "ch"),
            P("ch"),
            P(),
            P(),
            P(None, "ch"),
            P("ch"),
            P("ch", None),
            P(),
        ),
        out_specs=P("img", None, "ch"),
        check_vma=False,
    )
```

```python
import functools

import jax
import jax.numpy as jnp
from jax import lax
from jax.experimental import pallas as pl
from jax.experimental.pallas import tpu as pltpu
from jax.sharding import PartitionSpec as P

TS = 4
SIDE = 32
PAD_ROWS = 38
PAD_COLS = 48
LEFT = 8

slope_coef = 0.7978845608
cubic_coef = 0.044715
norm_eps = 1e-06

VMEM = pl.BlockSpec(memory_space=pltpu.VMEM)
SMEM = pl.BlockSpec(memory_space=pltpu.SMEM)
HBM = pl.BlockSpec(memory_space=pltpu.HBM)


def call(kernel, out_shape, in_specs, scratch=(), limit=16, out_specs=None):
    run = pl.pallas_call(
        kernel,
        out_shape=out_shape,
        in_specs=in_specs,
        out_specs=out_specs or [VMEM] * len(out_shape),
        scratch_shapes=list(scratch),
        compiler_params=pltpu.CompilerParams(vmem_limit_bytes=limit << 20),
    )

    def held(*args):
        return run(
            *(
                pltpu.with_memory_space_constraint(a, pltpu.VMEM if spec is VMEM else pltpu.HBM)
                for spec, a in zip(in_specs, args, strict=True)
            )
        )

    return held


def inside_of(rows, row, height, width):
    column = lax.broadcasted_iota(jnp.int32, (rows, 128), 0)
    return (column < width) & (row < height)


def depthwise_kernel(
    offsets, screen, canvas, dwk, bias, w_out, mixed_a, mixed_b, near_out, taps, here, framed, kern_bf, bias_row, sems
):
    lanes = canvas.shape[2] // 128
    parts = 4
    deep = SIDE // parts
    height, width = screen[0, 0], screen[0, 1]
    small = [
        pltpu.make_async_copy(dwk, kern_bf, sems.at[parts]),
        pltpu.make_async_copy(bias, bias_row, sems.at[parts + 1]),
    ]
    rows_in = [
        pltpu.make_async_copy(
            canvas.at[pl.ds(g * deep, deep)], here.at[pl.ds(g * deep, deep)], sems.at[g]
        )
        for g in range(parts)
    ]
    weights = pltpu.make_async_copy(w_out, near_out, sems.at[parts + 2])
    for fetch in (*small, *rows_in, weights):
        fetch.start()
    low = lax.broadcasted_iota(jnp.int32, (8, 128), 0) < 4
    blank = jnp.zeros((PAD_COLS, 128), jnp.float32)
    for b in range(lanes):
        for y in (0, 1, 2, SIDE + 3, SIDE + 4, SIDE + 5):
            framed[b, y] = blank
    for fetch in small:
        fetch.wait()
    for b in range(lanes):
        kern = kern_bf[:, b * 128 : (b + 1) * 128].astype(jnp.float32)
        for i in range(7):
            for j in range(4):
                first = jnp.broadcast_to(kern[7 * i + j][None], (8, 128))
                if j < 3:
                    second = jnp.broadcast_to(kern[7 * i + j + 4][None], (8, 128))
                else:
                    second = jnp.zeros((8, 128), jnp.float32)
                taps[b, i * 4 + j] = jnp.where(low, first, second)

    def fill(y, carry):
        seen = inside_of(SIDE, y, height, width)
        for b in range(lanes):
            framed[b, y + 3, 0:LEFT, :] = blank[:LEFT]
            framed[b, y + 3, LEFT + SIDE : PAD_COLS, :] = blank[: PAD_COLS - LEFT - SIDE]
            row = here[y, :, b * 128 : (b + 1) * 128].astype(jnp.float32)
            framed[b, y + 3, LEFT : LEFT + SIDE, :] = jnp.where(seen, row, 0.0)
        return carry

    for g in range(parts):
        rows_in[g].wait()
        lax.fori_loop(g * deep, (g + 1) * deep, fill, 0, unroll=4)
    count = mixed_a.shape[0] // 16
    for b in range(lanes):
        cut = slice(b * 128, (b + 1) * 128)
        start = jnp.broadcast_to(bias_row[cut][None], (8, 128))
        for mixed, base in ((mixed_a, 0), (mixed_b, count)):

            def tile(t, carry):
                r, q = offsets[0, base + t], offsets[1, base + t]
                sums = [None] * 4
                for p in range(10):
                    for j in range(4):
                        seen = framed[b, r + p, pl.ds(q + (LEFT - 3 + j), 8), :]
                        for y in range(max(0, p - 6), min(3, p) + 1):
                            term = seen * taps[b, (p - y) * 4 + j]
                            sums[y] = term if sums[y] is None else sums[y] + term
                folded = [s + pltpu.roll(s, 4, 0) + start for s in sums]
                pair = [jnp.where(low, folded[y], folded[y + 1]) for y in (0, 2)]
                rows = pl.ds(pl.multiple_of(t * 16, 16), 16)
                mixed[rows, cut] = jnp.concatenate(pair, 0).astype(jnp.bfloat16)
                return carry

            lax.fori_loop(0, count, tile, 0, unroll=2)
    weights.wait()


def two_parts(row):
    high = row.astype(jnp.bfloat16).astype(jnp.float32)
    return [high, row - high]


def scaled_rows(cells, scale, begin):
    share = cells.shape[3]
    flat = cells[...].astype(jnp.float32).reshape(cells.shape[0] * 16, share)
    return (scale[pl.ds(begin, share)][None] * flat).astype(jnp.bfloat16)


def channels_of(ahead, share):
    return pl.multiple_of(lax.rem(lax.axis_index("ch") + ahead, 4) * share, 128)


def hidden_kernel(
    offsets, counts, own, left, right, scale, gain, bias, b_in, w_out, w_in,
    hidden_a, hidden_b, taken, near_in, sides, flat, sem,
):
    fetch = pltpu.make_async_copy(w_in, near_in, sem)
    fetch.start()
    share = own.shape[3]
    taken[...] = jnp.zeros_like(taken)

    def tile(t, carry):
        r, q = offsets[0, t], offsets[1, t]
        for y in range(4):
            cells = own[t, y].astype(jnp.float32)
            for b in range(share // 128):
                taken[b, r + 3 + y, pl.ds(q + LEFT, 4), :] += cells[:, b * 128 : (b + 1) * 128]
        return carry

    lax.fori_loop(0, counts[lax.axis_index("img")], tile, 0)
    begins = []
    for k, (cells, ahead) in enumerate(((own, 0), (left, 3), (right, 1))):
        begins.append(channels_of(ahead, share))
        flat[k] = scaled_rows(cells, scale, begins[k])
    step = 512
    half = hidden_a.shape[0]
    for n in range(0, hidden_a.shape[1], step):
        total = None
        for k, begin in enumerate(begins):
            product = lax.dot_general(
                flat[k],
                w_out[n : n + step, pl.ds(begin, share)],
                (((1,), (1,)), ((), ())),
                preferred_element_type=jnp.float32,
            )
            total = product if total is None else total + product
        hidden_a[:, n : n + step] = total[:half]
        hidden_b[:, n : n + step] = total[half:]
    width = gain.shape[0]
    lines = two_parts(gain[...][None]) + two_parts(bias[...][None])
    lines = jnp.concatenate(lines + [jnp.zeros((12, width), jnp.float32)], 0).astype(jnp.bfloat16)
    fetch.wait()
    both = jnp.dot(lines, near_in[...], preferred_element_type=jnp.float32)
    sides[0:1, :] = both[0:1] + both[1:2]
    sides[1:2, :] = both[2:3] + both[3:4] + b_in[...][None]


def opposite_kernel(before, cot, scale, w_out, hidden, flat):
    share = flat.shape[1]
    begin = channels_of(2, share)
    flat[...] = scaled_rows(cot, scale, begin)
    step = 512
    for n in range(0, before.shape[1], step):
        hidden[:, n : n + step] = before[:, n : n + step] + lax.dot_general(
            flat[...],
            w_out[n : n + step, pl.ds(begin, share)],
            (((1,), (1,)), ((), ())),
            preferred_element_type=jnp.float32,
        )


def gelu_slope(v):
    square = v * v
    t = jnp.tanh(slope_coef * (v + cubic_coef * square * v))
    return 0.5 * (1.0 + t) + 0.5 * v * (1.0 - t * t) * slope_coef * (1.0 + 3.0 * cubic_coef * square)


def as_rows(column):
    count = column.shape[0] // 128
    eye = lax.broadcasted_iota(jnp.int32, (128, 128), 0) == lax.broadcasted_iota(jnp.int32, (128, 128), 1)
    return jnp.concatenate(
        [
            jnp.sum(jnp.where(eye, column[g * 128 : (g + 1) * 128], 0.0), axis=0, keepdims=True)
            for g in range(count)
        ],
        0,
    )


def as_column(rows):
    eye = lax.broadcasted_iota(jnp.int32, (128, 128), 0) == lax.broadcasted_iota(jnp.int32, (128, 128), 1)
    return jnp.concatenate(
        [
            jnp.sum(jnp.where(eye, rows[g : g + 1], 0.0), axis=1, keepdims=True)
            for g in range(rows.shape[0])
        ],
        0,
    )


def part_of(act, w_in, ahead):
    share = w_in.shape[0] // 4
    return lax.dot_general(
        act[...],
        w_in[pl.ds(channels_of(ahead, share), share), :],
        (((1,), (1,)), ((), ())),
        preferred_element_type=jnp.float32,
    )


def block_kernel(
    own, left, right, opp, gain, bias, w_in, b_in, hidden, sides,
    away, act, centers, inverses, full, scaled,
):
    rows, width = full.shape
    share = own.shape[1]
    for ref, ahead in ((own, 0), (left, 3), (right, 1), (opp, 2)):
        full[:, pl.ds(channels_of(ahead, share), share)] = ref[...]
    step = 64
    for m in range(0, rows, step):
        values = full[m : m + step, :].astype(jnp.float32)
        center = jnp.mean(values, axis=1, keepdims=True)
        apart = values - center
        inverse = lax.rsqrt(jnp.mean(apart * apart, axis=1, keepdims=True) + norm_eps)
        centers[m : m + step, :] = center
        inverses[m : m + step, :] = inverse
        scaled[m : m + step, :] = (apart * inverse * gain[...][None] + bias[...][None]).astype(
            jnp.bfloat16
        )
    step = 512
    first = jnp.zeros((rows, 128), jnp.float32)
    second = jnp.zeros((rows, 128), jnp.float32)
    for n in range(0, width, step):
        span = slice(n, n + step)
        product = jnp.dot(scaled[...], w_in[:, span], preferred_element_type=jnp.float32)
        pre = product + b_in[span][None]
        rounded = (hidden[:, span] * gelu_slope(pre)).astype(jnp.bfloat16)
        act[:, span] = rounded
        value = rounded.astype(jnp.float32)
        one = value * sides[0:1, span]
        two = value * (pre - sides[1:2, span])
        for k in range(0, step, 128):
            first = first + one[:, k : k + 128]
            second = second + two[:, k : k + 128]
    away[:rows, :] = part_of(act, w_in, 2).astype(jnp.bfloat16)
    packed = []
    for sums in (first, second):
        packed += two_parts(as_rows(jnp.sum(sums, axis=1, keepdims=True)))
    packed += [jnp.zeros((16 - 4 * (rows // 128), 128), jnp.float32)]
    away[rows : rows + 16, :] = jnp.zeros((16, share), jnp.bfloat16)
    away[rows : rows + 16, :128] = jnp.concatenate(packed, 0).astype(jnp.bfloat16)


def parts_kernel(keep_ahead, own_ahead, act, w_in, away, keep, own, mine):
    rows = act.shape[0]
    own[:rows, :] = part_of(act, w_in, own_ahead).astype(jnp.bfloat16)
    own[rows:, :] = away[rows:, :]
    keep[...] = part_of(act, w_in, keep_ahead).astype(jnp.bfloat16)
    mine[...] = part_of(act, w_in, 0)


def middle_kernel(come, keep, go):
    rows = keep.shape[0]
    total = keep[...].astype(jnp.float32) + come[:rows, :].astype(jnp.float32)
    go[:rows, :] = total.astype(jnp.bfloat16)
    go[rows:, :] = come[rows:, :]


def add_tiles(
    base, offsets, counts, mine, got, total, come, away, mixed, centers, inverses, gain, taps, upstream, grown
):
    rows, share = mixed.shape
    width = gain.shape[0]
    packed = None
    for ref in (away, come, got, total):
        lines = ref[rows : rows + 16, :128].astype(jnp.float32)
        packed = lines if packed is None else packed + lines
    n = rows // 128
    first = as_column((packed[0:n] + packed[n : 2 * n]) * (1.0 / width))
    second = as_column((packed[2 * n : 3 * n] + packed[3 * n : 4 * n]) * (1.0 / width))
    weight = gain[pl.ds(channels_of(0, share), share)][None]
    step = 64
    for m in range(0, rows, step):
        span = slice(m, m + step)
        norm_grad = mine[span, :] + got[span, :].astype(jnp.float32) + total[span, :].astype(jnp.float32)
        inverse = inverses[span, :]
        normed = (mixed[span, :].astype(jnp.float32) - centers[span, :]) * inverse
        upstream[span, :] = inverse * (norm_grad * weight - first[span] - normed * second[span])

    low = lax.broadcasted_iota(jnp.int32, (8, 128), 0) < 4

    def tile(t, carry):
        r, q = offsets[0, base + t], offsets[1, base + t]
        doubled = []
        for b in range(share // 128):
            twice = []
            for h in range(2):
                pair = upstream[pl.ds(pl.multiple_of(t * 16 + 8 * h, 8), 8), b * 128 : (b + 1) * 128]
                turned = pltpu.roll(pair, 4, 0)
                twice += [jnp.where(low, pair, turned), jnp.where(low, turned, pair)]
            doubled.append(twice)
        for j in range(4):
            columns = pl.ds(q + (LEFT - 3 + j), 8)
            for b in range(share // 128):
                for y in range(10):
                    more = None
                    for k in range(max(0, y - 6), min(3, y) + 1):
                        term = doubled[b][k] * taps[b, (y - k) * 4 + j]
                        more = term if more is None else more + term
                    grown[b, r + y, columns, :] += more
        return carry

    listed = counts[lax.axis_index("img")] - base
    lax.fori_loop(0, jnp.clip(listed, 0, rows // 16), tile, 0)


def first_tiles_kernel(
    offsets, counts, mine, got, total, come, away, mixed, centers, inverses, gain, taps, before,
    grown, upstream,
):
    grown[...] = before[...]
    add_tiles(
        0, offsets, counts, mine, got, total, come, away, mixed, centers, inverses, gain, taps, upstream, grown
    )


def last_tiles_kernel(
    offsets, counts, screen, mine, got, total, come, away, mixed, centers, inverses, gain, taps, before,
    grad, upstream, grown, stage, sems,
):
    grown[...] = before[...]
    add_tiles(
        mixed.shape[0] // 16,
        offsets, counts, mine, got, total, come, away, mixed, centers, inverses, gain, taps, upstream, grown,
    )
    height, width = screen[0, 0], screen[0, 1]
    stores = []
    deep = SIDE // 4
    for g in range(4):

        def line(y, carry):
            seen = inside_of(SIDE, y, height, width)
            for b in range(mixed.shape[1] // 128):
                whole = grown[b, y + 3, LEFT : LEFT + SIDE, :]
                stage[y, :, b * 128 : (b + 1) * 128] = jnp.where(seen, whole, 0.0)
            return carry

        lax.fori_loop(g * deep, (g + 1) * deep, line, 0, unroll=4)
        part = pl.ds(g * deep, deep)
        store = pltpu.make_async_copy(stage.at[part], grad.at[part], sems.at[g])
        store.start()
        stores.append(store)
    for store in stores:
        store.wait()


def shift(x, by):
    n = lax.axis_size("ch")
    return lax.ppermute(x, "ch", [(i, (i + by) % n) for i in range(n)])


def shards(
    canvas,
    screen_size,
    tile_counts,
    tile_offsets,
    cotangent,
    dw_kernel,
    dw_bias,
    ln_gain,
    ln_bias,
    w_in,
    b_in,
    w_out,
    layer_scale,
):
    f32, bf16 = jnp.float32, jnp.bfloat16
    struct = pltpu.VMEM
    slots = tile_offsets.shape[0]
    share = canvas.shape[2]
    width = ln_gain.shape[0]
    hid = w_in.shape[1]
    rows = slots * TS * TS
    half = rows // 2
    lanes = share // 128
    offsets = tile_offsets.T
    left, right = shift(cotangent, 1), shift(cotangent, -1)
    mixed_a, mixed_b, near_out, taps = call(
        depthwise_kernel,
        [
            struct((half, share), bf16),
            struct((half, share), bf16),
            struct(w_out.shape, bf16),
            struct((lanes, 28, 8, 128), f32),
        ],
        [SMEM, SMEM, HBM, HBM, HBM, HBM],
        [
            pltpu.VMEM(canvas.shape, bf16),
            pltpu.VMEM((lanes, PAD_ROWS, PAD_COLS, 128), f32),
            pltpu.VMEM(dw_kernel.shape, bf16),
            pltpu.VMEM(dw_bias.shape, f32),
            pltpu.SemaphoreType.DMA((7,)),
        ],
    )(offsets, screen_size, canvas, dw_kernel, dw_bias, w_out)
    left_a, right_b = shift(mixed_a, 1), shift(mixed_b, -1)
    cot_a, right_a = shift(left[: slots // 2], 1), shift(mixed_a, -1)
    canvas_like = struct((lanes, PAD_ROWS, PAD_COLS, 128), f32)
    hidden_a, hidden_b, taken, near_in, sides = call(
        hidden_kernel,
        [struct((half, hid), f32), struct((half, hid), f32), canvas_like, struct(w_in.shape, bf16), struct((8, hid), f32)],
        [SMEM] * 2 + [VMEM] * 8 + [HBM],
        [pltpu.VMEM((3, rows, share), bf16), pltpu.SemaphoreType.DMA(())],
    )(
        offsets, tile_counts, cotangent, left, right, layer_scale, ln_gain, ln_bias, b_in, near_out, w_in
    )
    forward_a, forward_b, forward_cot, sides = lax.optimization_barrier(
        (left_a, right_b, right, sides)
    )
    opp_a, opp_b = shift(forward_a, 1), shift(forward_b, -1)
    cot_b = shift(forward_cot[slots // 2 :], -1)

    def with_opposite(hidden, cot):
        return call(
            opposite_kernel,
            [struct((half, hid), f32)],
            [VMEM] * 4,
            [pltpu.VMEM((half, share), bf16)],
        )(hidden, cot, layer_scale, near_out)[0]

    hidden_a, late_b = lax.optimization_barrier((with_opposite(hidden_a, cot_a), mixed_b))
    left_b = shift(late_b, 1)
    hidden_b = with_opposite(hidden_b, cot_b)
    message = struct((half + 16, share), bf16)

    def block(blocks, hidden):
        return call(
            block_kernel,
            [message, struct((half, hid), bf16), struct((half, 1), f32), struct((half, 1), f32)],
            [VMEM] * 10,
            [pltpu.VMEM((half, width), bf16), pltpu.VMEM((half, width), bf16)],
        )(*blocks, ln_gain, ln_bias, near_in, b_in, hidden, sides)

    def parts(keep_ahead, own_ahead, act, away):
        return call(
            functools.partial(parts_kernel, keep_ahead, own_ahead),
            [struct((half, share), bf16), message, struct((half, share), f32)],
            [VMEM] * 3,
        )(act, near_in, away)

    def middle(come, keep):
        return call(middle_kernel, [message], [VMEM] * 2)(come, keep)[0]

    away_a, act_a, centers_a, inverses_a = block((mixed_a, left_a, right_a, opp_a), hidden_a)
    come_a = shift(away_a, 1)
    keep_a, own_a, mine_a = parts(1, 3, act_a, away_a)
    got_a = shift(own_a, -1)
    away_b, act_b, centers_b, inverses_b = block((mixed_b, left_b, right_b, opp_b), hidden_b)
    come_b = shift(away_b, -1)
    keep_b, own_b, mine_b = parts(3, 1, act_b, away_b)
    got_b = shift(own_b, 1)
    total_a = shift(middle(come_a, keep_a), 1)
    total_b = shift(middle(come_b, keep_b), -1)
    grown = call(
        first_tiles_kernel,
        [canvas_like],
        [SMEM] * 2 + [VMEM] * 11,
        [pltpu.VMEM((half, share), f32)],
    )(
        offsets, tile_counts, mine_a, got_a, total_a, come_a, away_a, mixed_a, centers_a, inverses_a,
        ln_gain, taps, taken,
    )[0]
    return call(
        last_tiles_kernel,
        jax.ShapeDtypeStruct(canvas.shape, f32),
        [SMEM] * 3 + [VMEM] * 11,
        [
            pltpu.VMEM((half, share), f32),
            pltpu.VMEM((lanes, PAD_ROWS, PAD_COLS, 128), f32),
            pltpu.VMEM(canvas.shape, f32),
            pltpu.SemaphoreType.DMA((4,)),
        ],
        out_specs=HBM,
    )(
        offsets, tile_counts, screen_size, mine_b, got_b, total_b, come_b, away_b, mixed_b, centers_b, inverses_b,
        ln_gain, taps, grown,
    )


def solution(mesh):
    return jax.shard_map(
        shards,
        mesh=mesh,
        in_specs=(
            P("img", None, "ch"),
            P("img", None),
            P(),
            P("img", None),
            P("img", None, None, "ch"),
            P(None, "ch"),
            P("ch"),
            P(),
            P(),
            P(None, "ch"),
            P("ch"),
            P("ch", None),
            P(),
        ),
        out_specs=P("img", None, "ch"),
        check_vma=False,
    )
```

```python
import jax
import jax.numpy as jnp
from jax import lax
from jax.experimental import pallas as pl
from jax.experimental.pallas import tpu as pltpu
from jax.sharding import PartitionSpec as P

TS = 4
SIDE = 32
PAD_ROWS = 38
PAD_COLS = 48
LEFT = 8

slope_coef = 0.7978845608
cubic_coef = 0.044715
norm_eps = 1e-06

VMEM = pl.BlockSpec(memory_space=pltpu.VMEM)
SMEM = pl.BlockSpec(memory_space=pltpu.SMEM)
HBM = pl.BlockSpec(memory_space=pltpu.HBM)


def call(kernel, out_shape, in_specs, scratch=(), limit=16, out_specs=None):
    run = pl.pallas_call(
        kernel,
        out_shape=out_shape,
        in_specs=in_specs,
        out_specs=out_specs or [VMEM] * len(out_shape),
        scratch_shapes=list(scratch),
        compiler_params=pltpu.CompilerParams(vmem_limit_bytes=limit << 20),
    )

    def held(*args):
        return run(
            *(
                pltpu.with_memory_space_constraint(a, pltpu.VMEM if spec is VMEM else pltpu.HBM)
                for spec, a in zip(in_specs, args, strict=True)
            )
        )

    return held


def inside_of(rows, row, height, width):
    column = lax.broadcasted_iota(jnp.int32, (rows, 128), 0)
    return (column < width) & (row < height)


def depthwise_kernel(
    offsets, screen, canvas, dwk, bias, w_out, mixed_a, mixed_b, near_out, taps, here, framed, kern_bf, bias_row, sems
):
    lanes = canvas.shape[2] // 128
    parts = 4
    deep = SIDE // parts
    height, width = screen[0, 0], screen[0, 1]
    small = [
        pltpu.make_async_copy(dwk, kern_bf, sems.at[parts]),
        pltpu.make_async_copy(bias, bias_row, sems.at[parts + 1]),
    ]
    rows_in = [
        pltpu.make_async_copy(
            canvas.at[pl.ds(g * deep, deep)], here.at[pl.ds(g * deep, deep)], sems.at[g]
        )
        for g in range(parts)
    ]
    weights = pltpu.make_async_copy(w_out, near_out, sems.at[parts + 2])
    for fetch in (*small, *rows_in, weights):
        fetch.start()
    low = lax.broadcasted_iota(jnp.int32, (8, 128), 0) < 4
    blank = jnp.zeros((PAD_COLS, 128), jnp.float32)
    for b in range(lanes):
        for y in (0, 1, 2, SIDE + 3, SIDE + 4, SIDE + 5):
            framed[b, y] = blank
    for fetch in small:
        fetch.wait()
    for b in range(lanes):
        kern = kern_bf[:, b * 128 : (b + 1) * 128].astype(jnp.float32)
        for i in range(7):
            for j in range(4):
                first = jnp.broadcast_to(kern[7 * i + j][None], (8, 128))
                if j < 3:
                    second = jnp.broadcast_to(kern[7 * i + j + 4][None], (8, 128))
                else:
                    second = jnp.zeros((8, 128), jnp.float32)
                taps[b, i * 4 + j] = jnp.where(low, first, second)

    def fill(y, carry):
        seen = inside_of(SIDE, y, height, width)
        for b in range(lanes):
            framed[b, y + 3, 0:LEFT, :] = blank[:LEFT]
            framed[b, y + 3, LEFT + SIDE : PAD_COLS, :] = blank[: PAD_COLS - LEFT - SIDE]
            row = here[y, :, b * 128 : (b + 1) * 128].astype(jnp.float32)
            framed[b, y + 3, LEFT : LEFT + SIDE, :] = jnp.where(seen, row, 0.0)
        return carry

    for g in range(parts):
        rows_in[g].wait()
        lax.fori_loop(g * deep, (g + 1) * deep, fill, 0, unroll=4)
    count = mixed_a.shape[0] // 16
    for b in range(lanes):
        cut = slice(b * 128, (b + 1) * 128)
        start = jnp.broadcast_to(bias_row[cut][None], (8, 128))
        for mixed, base in ((mixed_a, 0), (mixed_b, count)):

            def tile(t, carry):
                r, q = offsets[0, base + t], offsets[1, base + t]
                sums = [None] * 4
                for p in range(10):
                    for j in range(4):
                        seen = framed[b, r + p, pl.ds(q + (LEFT - 3 + j), 8), :]
                        for y in range(max(0, p - 6), min(3, p) + 1):
                            term = seen * taps[b, (p - y) * 4 + j]
                            sums[y] = term if sums[y] is None else sums[y] + term
                folded = [s + pltpu.roll(s, 4, 0) + start for s in sums]
                pair = [jnp.where(low, folded[y], folded[y + 1]) for y in (0, 2)]
                rows = pl.ds(pl.multiple_of(t * 16, 16), 16)
                mixed[rows, cut] = jnp.concatenate(pair, 0).astype(jnp.bfloat16)
                return carry

            lax.fori_loop(0, count, tile, 0, unroll=2)
    weights.wait()


def two_parts(row):
    high = row.astype(jnp.bfloat16).astype(jnp.float32)
    return [high, row - high]


def scaled_rows(cells, scale, begin):
    share = cells.shape[3]
    flat = cells[...].astype(jnp.float32).reshape(cells.shape[0] * 16, share)
    return (scale[pl.ds(begin, share)][None] * flat).astype(jnp.bfloat16)


def channels_of(ahead, share):
    return pl.multiple_of(lax.rem(lax.axis_index("ch") + ahead, 4) * share, 128)


def cotangent_kernel(offsets, counts, own, earlier, taken):
    del earlier
    taken[...] = jnp.zeros_like(taken)

    def tile(t, carry):
        r, q = offsets[0, t], offsets[1, t]
        for y in range(4):
            cells = own[t, y].astype(jnp.float32)
            for b in range(own.shape[3] // 128):
                taken[b, r + 3 + y, pl.ds(q + LEFT, 4), :] += cells[:, b * 128 : (b + 1) * 128]
        return carry

    lax.fori_loop(0, counts[lax.axis_index("img")], tile, 0)


def hidden_kernel(
    own, left, right, scale, gain, bias, b_in, w_out, w_in,
    hidden_a, hidden_b, near_in, sides, flat, sem,
):
    fetch = pltpu.make_async_copy(w_in, near_in, sem)
    fetch.start()
    share = own.shape[3]
    begins = []
    for k, (cells, ahead) in enumerate(((own, 0), (left, 3), (right, 1))):
        begins.append(channels_of(ahead, share))
        flat[k] = scaled_rows(cells, scale, begins[k])
    step = 512
    half = hidden_a.shape[0]
    for n in range(0, hidden_a.shape[1], step):
        total = None
        for k, begin in enumerate(begins):
            product = lax.dot_general(
                flat[k],
                w_out[n : n + step, pl.ds(begin, share)],
                (((1,), (1,)), ((), ())),
                preferred_element_type=jnp.float32,
            )
            total = product if total is None else total + product
        hidden_a[:, n : n + step] = total[:half]
        hidden_b[:, n : n + step] = total[half:]
    width = gain.shape[0]
    lines = two_parts(gain[...][None]) + two_parts(bias[...][None])
    lines = jnp.concatenate(lines + [jnp.zeros((12, width), jnp.float32)], 0).astype(jnp.bfloat16)
    fetch.wait()
    both = jnp.dot(lines, near_in[...], preferred_element_type=jnp.float32)
    sides[0:1, :] = both[0:1] + both[1:2]
    sides[1:2, :] = both[2:3] + both[3:4] + b_in[...][None]


def opposite_kernel(before, cot, scale, w_out, hidden, flat):
    share = flat.shape[1]
    begin = channels_of(2, share)
    flat[...] = scaled_rows(cot, scale, begin)
    step = 512
    for n in range(0, before.shape[1], step):
        hidden[:, n : n + step] = before[:, n : n + step] + lax.dot_general(
            flat[...],
            w_out[n : n + step, pl.ds(begin, share)],
            (((1,), (1,)), ((), ())),
            preferred_element_type=jnp.float32,
        )


def gelu_slope(v):
    square = v * v
    t = jnp.tanh(v * (slope_coef + slope_coef * cubic_coef * square))
    w = v * (0.5 * slope_coef + 1.5 * slope_coef * cubic_coef * square)
    return (0.5 + 0.5 * t) + w * (1.0 - t * t)


def as_rows(column):
    count = column.shape[0] // 128
    eye = lax.broadcasted_iota(jnp.int32, (128, 128), 0) == lax.broadcasted_iota(jnp.int32, (128, 128), 1)
    return jnp.concatenate(
        [
            jnp.sum(jnp.where(eye, column[g * 128 : (g + 1) * 128], 0.0), axis=0, keepdims=True)
            for g in range(count)
        ],
        0,
    )


def as_column(rows):
    eye = lax.broadcasted_iota(jnp.int32, (128, 128), 0) == lax.broadcasted_iota(jnp.int32, (128, 128), 1)
    return jnp.concatenate(
        [
            jnp.sum(jnp.where(eye, rows[g : g + 1], 0.0), axis=1, keepdims=True)
            for g in range(rows.shape[0])
        ],
        0,
    )


def part_of(act, w_in, ahead):
    share = w_in.shape[0] // 4
    return lax.dot_general(
        act[...],
        w_in[pl.ds(channels_of(ahead, share), share), :],
        (((1,), (1,)), ((), ())),
        preferred_element_type=jnp.float32,
    )


def block_kernel(
    own, left, right, opp, gain, bias, w_in, b_in, hidden, sides,
    *outs,
):
    *own_part, away, act, centers, inverses, full, scaled = outs
    rows, width = full.shape
    share = own.shape[1]
    for ref, ahead in ((own, 0), (left, 3), (right, 1), (opp, 2)):
        full[:, pl.ds(channels_of(ahead, share), share)] = ref[...]
    step = 64
    for m in range(0, rows, step):
        values = full[m : m + step, :].astype(jnp.float32)
        center = jnp.mean(values, axis=1, keepdims=True)
        apart = values - center
        inverse = lax.rsqrt(jnp.mean(apart * apart, axis=1, keepdims=True) + norm_eps)
        centers[m : m + step, :] = center
        inverses[m : m + step, :] = inverse
        scaled[m : m + step, :] = (apart * inverse * gain[...][None] + bias[...][None]).astype(
            jnp.bfloat16
        )
    step = 512
    first = jnp.zeros((rows, 128), jnp.float32)
    second = jnp.zeros((rows, 128), jnp.float32)
    for n in range(0, width, step):
        span = slice(n, n + step)
        product = jnp.dot(scaled[...], w_in[:, span], preferred_element_type=jnp.float32)
        pre = product + b_in[span][None]
        rounded = (hidden[:, span] * gelu_slope(pre)).astype(jnp.bfloat16)
        act[:, span] = rounded
        value = rounded.astype(jnp.float32)
        one = value * sides[0:1, span]
        two = value * (pre - sides[1:2, span])
        for k in range(0, step, 128):
            first = first + one[:, k : k + 128]
            second = second + two[:, k : k + 128]
    away[:rows, :] = part_of(act, w_in, 2).astype(jnp.bfloat16)
    packed = []
    for sums in (first, second):
        packed += two_parts(as_rows(jnp.sum(sums, axis=1, keepdims=True)))
    packed += [jnp.zeros((16 - 4 * (rows // 128), 128), jnp.float32)]
    away[rows : rows + 16, :] = jnp.zeros((16, share), jnp.bfloat16)
    away[rows : rows + 16, :128] = jnp.concatenate(packed, 0).astype(jnp.bfloat16)
    for own_out in own_part:
        own_out[:rows, :] = part_of(act, w_in, 3).astype(jnp.bfloat16)
        own_out[rows:, :] = away[rows:, :]


def first_parts_kernel(act, w_in, earlier, keep, mine):
    del earlier
    keep[...] = part_of(act, w_in, 1).astype(jnp.bfloat16)
    mine[...] = part_of(act, w_in, 0)


def second_parts_kernel(act, w_in, away, keep, own, mine):
    rows = act.shape[0]
    own[:rows, :] = part_of(act, w_in, 1).astype(jnp.bfloat16)
    own[rows:, :] = away[rows:, :]
    keep[...] = part_of(act, w_in, 3).astype(jnp.bfloat16)
    mine[...] = part_of(act, w_in, 0)


def middle_kernel(come, keep, go):
    rows = keep.shape[0]
    total = keep[...].astype(jnp.float32) + come[:rows, :].astype(jnp.float32)
    go[:rows, :] = total.astype(jnp.bfloat16)
    go[rows:, :] = come[rows:, :]


def add_tiles(
    base, offsets, counts, mine, got, total, come, away, mixed, centers, inverses, gain, taps, upstream, grown
):
    rows, share = mixed.shape
    width = gain.shape[0]
    packed = None
    for ref in (away, come, got, total):
        lines = ref[rows : rows + 16, :128].astype(jnp.float32)
        packed = lines if packed is None else packed + lines
    n = rows // 128
    first = as_column((packed[0:n] + packed[n : 2 * n]) * (1.0 / width))
    second = as_column((packed[2 * n : 3 * n] + packed[3 * n : 4 * n]) * (1.0 / width))
    weight = gain[pl.ds(channels_of(0, share), share)][None]
    step = 64
    for m in range(0, rows, step):
        span = slice(m, m + step)
        norm_grad = mine[span, :] + got[span, :].astype(jnp.float32) + total[span, :].astype(jnp.float32)
        inverse = inverses[span, :]
        normed = (mixed[span, :].astype(jnp.float32) - centers[span, :]) * inverse
        upstream[span, :] = inverse * (norm_grad * weight - first[span] - normed * second[span])

    low = lax.broadcasted_iota(jnp.int32, (8, 128), 0) < 4

    def tile(t, carry):
        r, q = offsets[0, base + t], offsets[1, base + t]
        doubled = []
        for b in range(share // 128):
            twice = []
            for h in range(2):
                pair = upstream[pl.ds(pl.multiple_of(t * 16 + 8 * h, 8), 8), b * 128 : (b + 1) * 128]
                turned = pltpu.roll(pair, 4, 0)
                twice += [jnp.where(low, pair, turned), jnp.where(low, turned, pair)]
            doubled.append(twice)
        for j in range(4):
            columns = pl.ds(q + (LEFT - 3 + j), 8)
            for b in range(share // 128):
                for y in range(10):
                    more = None
                    for k in range(max(0, y - 6), min(3, y) + 1):
                        term = doubled[b][k] * taps[b, (y - k) * 4 + j]
                        more = term if more is None else more + term
                    grown[b, r + y, columns, :] += more
        return carry

    listed = counts[lax.axis_index("img")] - base
    lax.fori_loop(0, jnp.clip(listed, 0, rows // 16), tile, 0)


def first_tiles_kernel(
    offsets, counts, mine, got, total, come, away, mixed, centers, inverses, gain, taps, before,
    grown, upstream,
):
    grown[...] = before[...]
    add_tiles(
        0, offsets, counts, mine, got, total, come, away, mixed, centers, inverses, gain, taps, upstream, grown
    )


def last_tiles_kernel(
    offsets, counts, screen, mine, got, total, come, away, mixed, centers, inverses, gain, taps, before,
    grad, upstream, grown, stage, sems,
):
    grown[...] = before[...]
    add_tiles(
        mixed.shape[0] // 16,
        offsets, counts, mine, got, total, come, away, mixed, centers, inverses, gain, taps, upstream, grown,
    )
    height, width = screen[0, 0], screen[0, 1]
    stores = []
    deep = SIDE // 4
    for g in range(4):

        def line(y, carry):
            seen = inside_of(SIDE, y, height, width)
            for b in range(mixed.shape[1] // 128):
                whole = grown[b, y + 3, LEFT : LEFT + SIDE, :]
                stage[y, :, b * 128 : (b + 1) * 128] = jnp.where(seen, whole, 0.0)
            return carry

        lax.fori_loop(g * deep, (g + 1) * deep, line, 0, unroll=4)
        part = pl.ds(g * deep, deep)
        store = pltpu.make_async_copy(stage.at[part], grad.at[part], sems.at[g])
        store.start()
        stores.append(store)
    for store in stores:
        store.wait()


def shift(x, by):
    n = lax.axis_size("ch")
    return lax.ppermute(x, "ch", [(i, (i + by) % n) for i in range(n)])


def shards(
    canvas,
    screen_size,
    tile_counts,
    tile_offsets,
    cotangent,
    dw_kernel,
    dw_bias,
    ln_gain,
    ln_bias,
    w_in,
    b_in,
    w_out,
    layer_scale,
):
    f32, bf16 = jnp.float32, jnp.bfloat16
    struct = pltpu.VMEM
    slots = tile_offsets.shape[0]
    share = canvas.shape[2]
    width = ln_gain.shape[0]
    hid = w_in.shape[1]
    rows = slots * TS * TS
    half = rows // 2
    lanes = share // 128
    offsets = tile_offsets.T
    left, right = shift(cotangent, 1), shift(cotangent, -1)
    mixed_a, mixed_b, near_out, taps = call(
        depthwise_kernel,
        [
            struct((half, share), bf16),
            struct((half, share), bf16),
            struct(w_out.shape, bf16),
            struct((lanes, 28, 8, 128), f32),
        ],
        [SMEM, SMEM, HBM, HBM, HBM, HBM],
        [
            pltpu.VMEM(canvas.shape, bf16),
            pltpu.VMEM((lanes, PAD_ROWS, PAD_COLS, 128), f32),
            pltpu.VMEM(dw_kernel.shape, bf16),
            pltpu.VMEM(dw_bias.shape, f32),
            pltpu.SemaphoreType.DMA((7,)),
        ],
    )(offsets, screen_size, canvas, dw_kernel, dw_bias, w_out)
    left_a, right_b = shift(mixed_a, 1), shift(mixed_b, -1)
    canvas_like = struct((lanes, PAD_ROWS, PAD_COLS, 128), f32)
    taken = call(cotangent_kernel, [canvas_like], [SMEM] * 2 + [VMEM] * 2)(
        offsets, tile_counts, cotangent, mixed_a
    )[0]
    left, taken = lax.optimization_barrier((left, taken))
    cot_a, right_a = shift(left[: slots // 2], 1), shift(mixed_a, -1)
    hidden_a, hidden_b, near_in, sides = call(
        hidden_kernel,
        [struct((half, hid), f32), struct((half, hid), f32), struct(w_in.shape, bf16), struct((8, hid), f32)],
        [VMEM] * 8 + [HBM],
        [pltpu.VMEM((3, rows, share), bf16), pltpu.SemaphoreType.DMA(())],
    )(cotangent, left, right, layer_scale, ln_gain, ln_bias, b_in, near_out, w_in)
    forward_a, forward_b, forward_cot, sides = lax.optimization_barrier(
        (left_a, right_b, right, sides)
    )
    opp_a, opp_b = shift(forward_a, 1), shift(forward_b, -1)
    cot_b = shift(forward_cot[slots // 2 :], -1)

    def with_opposite(hidden, cot):
        return call(
            opposite_kernel,
            [struct((half, hid), f32)],
            [VMEM] * 4,
            [pltpu.VMEM((half, share), bf16)],
        )(hidden, cot, layer_scale, near_out)[0]

    hidden_a, late_b = lax.optimization_barrier((with_opposite(hidden_a, cot_a), mixed_b))
    left_b = shift(late_b, 1)
    hidden_b = with_opposite(hidden_b, cot_b)
    message = struct((half + 16, share), bf16)

    def block(own_parts, blocks, hidden):
        return call(
            block_kernel,
            [message] * (own_parts + 1)
            + [struct((half, hid), bf16), struct((half, 1), f32), struct((half, 1), f32)],
            [VMEM] * 10,
            [pltpu.VMEM((half, width), bf16), pltpu.VMEM((half, width), bf16)],
        )(*blocks, ln_gain, ln_bias, near_in, b_in, hidden, sides)

    def middle(come, keep):
        return call(middle_kernel, [message], [VMEM] * 2)(come, keep)[0]

    own_a, away_a, act_a, centers_a, inverses_a = block(1, (mixed_a, left_a, right_a, opp_a), hidden_a)
    come_a, got_a = shift(away_a, 1), shift(own_a, -1)
    away_b, act_b, centers_b, inverses_b = block(0, (mixed_b, left_b, right_b, opp_b), hidden_b)
    come_b = shift(away_b, -1)
    part = struct((half, share), bf16)
    mine_like = struct((half, share), f32)
    keep_a, mine_a = call(first_parts_kernel, [part, mine_like], [VMEM] * 3)(act_a, near_in, got_a)
    keep_b, own_b, mine_b = call(second_parts_kernel, [part, message, mine_like], [VMEM] * 3)(
        act_b, near_in, away_b
    )
    got_b = shift(own_b, 1)
    total_a = shift(middle(come_a, keep_a), 1)
    total_b = shift(middle(come_b, keep_b), -1)
    grown = call(
        first_tiles_kernel,
        [canvas_like],
        [SMEM] * 2 + [VMEM] * 11,
        [pltpu.VMEM((half, share), f32)],
    )(
        offsets, tile_counts, mine_a, got_a, total_a, come_a, away_a, mixed_a, centers_a, inverses_a,
        ln_gain, taps, taken,
    )[0]
    return call(
        last_tiles_kernel,
        jax.ShapeDtypeStruct(canvas.shape, f32),
        [SMEM] * 3 + [VMEM] * 11,
        [
            pltpu.VMEM((half, share), f32),
            pltpu.VMEM((lanes, PAD_ROWS, PAD_COLS, 128), f32),
            pltpu.VMEM(canvas.shape, f32),
            pltpu.SemaphoreType.DMA((4,)),
        ],
        out_specs=HBM,
    )(
        offsets, tile_counts, screen_size, mine_b, got_b, total_b, come_b, away_b, mixed_b, centers_b, inverses_b,
        ln_gain, taps, grown,
    )


def solution(mesh):
    return jax.shard_map(
        shards,
        mesh=mesh,
        in_specs=(
            P("img", None, "ch"),
            P("img", None),
            P(),
            P("img", None),
            P("img", None, None, "ch"),
            P(None, "ch"),
            P("ch"),
            P(),
            P(),
            P(None, "ch"),
            P("ch"),
            P("ch", None),
            P(),
        ),
        out_specs=P("img", None, "ch"),
        check_vma=False,
    )
```

```python
import jax
import jax.numpy as jnp
from jax import lax
from jax.experimental import pallas as pl
from jax.experimental.pallas import tpu as pltpu
from jax.sharding import PartitionSpec as P

TS = 4
SIDE = 32
PAD_ROWS = 38
PAD_COLS = 48
LEFT = 8

slope_coef = 0.7978845608
cubic_coef = 0.044715
norm_eps = 1e-06

VMEM = pl.BlockSpec(memory_space=pltpu.VMEM)
SMEM = pl.BlockSpec(memory_space=pltpu.SMEM)
HBM = pl.BlockSpec(memory_space=pltpu.HBM)


def call(kernel, out_shape, in_specs, scratch=(), limit=16, out_specs=None):
    run = pl.pallas_call(
        kernel,
        out_shape=out_shape,
        in_specs=in_specs,
        out_specs=out_specs or [VMEM] * len(out_shape),
        scratch_shapes=list(scratch),
        compiler_params=pltpu.CompilerParams(vmem_limit_bytes=limit << 20),
    )

    def held(*args):
        return run(
            *(
                pltpu.with_memory_space_constraint(a, pltpu.VMEM if spec is VMEM else pltpu.HBM)
                for spec, a in zip(in_specs, args, strict=True)
            )
        )

    return held


def inside_of(rows, row, height, width):
    column = lax.broadcasted_iota(jnp.int32, (rows, 128), 0)
    return (column < width) & (row < height)


def depthwise_kernel(
    offsets, screen, canvas, dwk, bias, w_out, mixed_a, mixed_b, near_out, taps, here, framed, kern_bf, bias_row, sems
):
    lanes = canvas.shape[2] // 128
    parts = 4
    deep = SIDE // parts
    height, width = screen[0, 0], screen[0, 1]
    small = [
        pltpu.make_async_copy(dwk, kern_bf, sems.at[parts]),
        pltpu.make_async_copy(bias, bias_row, sems.at[parts + 1]),
    ]
    rows_in = [
        pltpu.make_async_copy(
            canvas.at[pl.ds(g * deep, deep)], here.at[pl.ds(g * deep, deep)], sems.at[g]
        )
        for g in range(parts)
    ]
    weights = pltpu.make_async_copy(w_out, near_out, sems.at[parts + 2])
    for fetch in (*small, *rows_in, weights):
        fetch.start()
    low = lax.broadcasted_iota(jnp.int32, (8, 128), 0) < 4
    blank = jnp.zeros((PAD_COLS, 128), jnp.float32)
    for b in range(lanes):
        for y in (0, 1, 2, SIDE + 3, SIDE + 4, SIDE + 5):
            framed[b, y] = blank
    for fetch in small:
        fetch.wait()
    for b in range(lanes):
        kern = kern_bf[:, b * 128 : (b + 1) * 128].astype(jnp.float32)
        for i in range(7):
            for j in range(4):
                first = jnp.broadcast_to(kern[7 * i + j][None], (8, 128))
                if j < 3:
                    second = jnp.broadcast_to(kern[7 * i + j + 4][None], (8, 128))
                else:
                    second = jnp.zeros((8, 128), jnp.float32)
                taps[b, i * 4 + j] = jnp.where(low, first, second)

    def fill(y, carry):
        seen = inside_of(SIDE, y, height, width)
        for b in range(lanes):
            framed[b, y + 3, 0:LEFT, :] = blank[:LEFT]
            framed[b, y + 3, LEFT + SIDE : PAD_COLS, :] = blank[: PAD_COLS - LEFT - SIDE]
            row = here[y, :, b * 128 : (b + 1) * 128].astype(jnp.float32)
            framed[b, y + 3, LEFT : LEFT + SIDE, :] = jnp.where(seen, row, 0.0)
        return carry

    for g in range(parts):
        rows_in[g].wait()
        lax.fori_loop(g * deep, (g + 1) * deep, fill, 0, unroll=4)
    count = mixed_a.shape[0] // 16
    for b in range(lanes):
        cut = slice(b * 128, (b + 1) * 128)
        start = jnp.broadcast_to(bias_row[cut][None], (8, 128))
        for mixed, base in ((mixed_a, 0), (mixed_b, count)):

            def tile(t, carry):
                r, q = offsets[0, base + t], offsets[1, base + t]
                sums = [None] * 4
                for p in range(10):
                    for j in range(4):
                        seen = framed[b, r + p, pl.ds(q + (LEFT - 3 + j), 8), :]
                        for y in range(max(0, p - 6), min(3, p) + 1):
                            term = seen * taps[b, (p - y) * 4 + j]
                            sums[y] = term if sums[y] is None else sums[y] + term
                folded = [s + pltpu.roll(s, 4, 0) + start for s in sums]
                pair = [jnp.where(low, folded[y], folded[y + 1]) for y in (0, 2)]
                rows = pl.ds(pl.multiple_of(t * 16, 16), 16)
                mixed[rows, cut] = jnp.concatenate(pair, 0).astype(jnp.bfloat16)
                return carry

            lax.fori_loop(0, count, tile, 0, unroll=2)
    weights.wait()


def two_parts(row):
    high = row.astype(jnp.bfloat16).astype(jnp.float32)
    return [high, row - high]


def scaled_rows(cells, scale, begin):
    share = cells.shape[3]
    flat = cells[...].astype(jnp.float32).reshape(cells.shape[0] * 16, share)
    return (scale[pl.ds(begin, share)][None] * flat).astype(jnp.bfloat16)


def channels_of(ahead, share):
    return pl.multiple_of(lax.rem(lax.axis_index("ch") + ahead, 4) * share, 128)


def cotangent_kernel(offsets, counts, own, earlier, taken):
    del earlier
    taken[...] = jnp.zeros_like(taken)

    def tile(t, carry):
        r, q = offsets[0, t], offsets[1, t]
        for y in range(4):
            cells = own[t, y].astype(jnp.float32)
            for b in range(own.shape[3] // 128):
                taken[b, r + 3 + y, pl.ds(q + LEFT, 4), :] += cells[:, b * 128 : (b + 1) * 128]
        return carry

    lax.fori_loop(0, counts[lax.axis_index("img")], tile, 0)


def hidden_kernel(
    own, left, right, scale, gain, bias, b_in, w_out, w_in,
    hidden_a, hidden_b, near_in, sides, flat, sem,
):
    fetch = pltpu.make_async_copy(w_in, near_in, sem)
    fetch.start()
    share = own.shape[3]
    begins = []
    for k, (cells, ahead) in enumerate(((own, 0), (left, 3), (right, 1))):
        begins.append(channels_of(ahead, share))
        flat[k] = scaled_rows(cells, scale, begins[k])
    step = 512
    half = hidden_a.shape[0]
    for n in range(0, hidden_a.shape[1], step):
        total = None
        for k, begin in enumerate(begins):
            product = lax.dot_general(
                flat[k],
                w_out[n : n + step, pl.ds(begin, share)],
                (((1,), (1,)), ((), ())),
                preferred_element_type=jnp.float32,
            )
            total = product if total is None else total + product
        hidden_a[:, n : n + step] = total[:half]
        hidden_b[:, n : n + step] = total[half:]
    width = gain.shape[0]
    lines = two_parts(gain[...][None]) + two_parts(bias[...][None])
    lines = jnp.concatenate(lines + [jnp.zeros((12, width), jnp.float32)], 0).astype(jnp.bfloat16)
    fetch.wait()
    both = jnp.dot(lines, near_in[...], preferred_element_type=jnp.float32)
    sides[0:1, :] = both[0:1] + both[1:2]
    sides[1:2, :] = both[2:3] + both[3:4] + b_in[...][None]


def join_kernel(mixed, cells, joined):
    half = mixed.shape[0]
    joined[:half, :] = mixed[...]
    last = cells[cells.shape[0] // 2 :].astype(jnp.float32)
    joined[half:, :] = last.reshape(half, mixed.shape[1]).astype(jnp.bfloat16)


def opposite_kernel(before, cot, scale, w_out, earlier, hidden, flat):
    del earlier
    rows, share = flat.shape
    begin = channels_of(2, share)
    if len(cot.shape) == 4:
        flat[...] = scaled_rows(cot, scale, begin)
    else:
        cells = cot[rows:, :].astype(jnp.float32)
        flat[...] = (scale[pl.ds(begin, share)][None] * cells).astype(jnp.bfloat16)
    step = 512
    for n in range(0, before.shape[1], step):
        hidden[:, n : n + step] = before[:, n : n + step] + lax.dot_general(
            flat[...],
            w_out[n : n + step, pl.ds(begin, share)],
            (((1,), (1,)), ((), ())),
            preferred_element_type=jnp.float32,
        )


def gelu_slope(v):
    square = v * v
    t = jnp.tanh(v * (slope_coef + slope_coef * cubic_coef * square))
    w = v * (0.5 * slope_coef + 1.5 * slope_coef * cubic_coef * square)
    return (0.5 + 0.5 * t) + w * (1.0 - t * t)


def as_rows(column):
    count = column.shape[0] // 128
    eye = lax.broadcasted_iota(jnp.int32, (128, 128), 0) == lax.broadcasted_iota(jnp.int32, (128, 128), 1)
    return jnp.concatenate(
        [
            jnp.sum(jnp.where(eye, column[g * 128 : (g + 1) * 128], 0.0), axis=0, keepdims=True)
            for g in range(count)
        ],
        0,
    )


def as_column(rows):
    eye = lax.broadcasted_iota(jnp.int32, (128, 128), 0) == lax.broadcasted_iota(jnp.int32, (128, 128), 1)
    return jnp.concatenate(
        [
            jnp.sum(jnp.where(eye, rows[g : g + 1], 0.0), axis=1, keepdims=True)
            for g in range(rows.shape[0])
        ],
        0,
    )


def part_of(act, w_in, ahead):
    share = w_in.shape[0] // 4
    return lax.dot_general(
        act[...],
        w_in[pl.ds(channels_of(ahead, share), share), :],
        (((1,), (1,)), ((), ())),
        preferred_element_type=jnp.float32,
    )


def block_kernel(
    own, left, right, opp, gain, bias, w_in, b_in, hidden, sides,
    *outs,
):
    *own_part, away, act, centers, inverses, full, scaled = outs
    rows, width = full.shape
    share = own.shape[1]
    for ref, ahead in ((own, 0), (left, 3), (right, 1), (opp, 2)):
        full[:, pl.ds(channels_of(ahead, share), share)] = ref[:rows, :]
    step = 64
    for m in range(0, rows, step):
        values = full[m : m + step, :].astype(jnp.float32)
        center = jnp.mean(values, axis=1, keepdims=True)
        apart = values - center
        inverse = lax.rsqrt(jnp.mean(apart * apart, axis=1, keepdims=True) + norm_eps)
        centers[m : m + step, :] = center
        inverses[m : m + step, :] = inverse
        scaled[m : m + step, :] = (apart * inverse * gain[...][None] + bias[...][None]).astype(
            jnp.bfloat16
        )
    step = 512
    first = jnp.zeros((rows, 128), jnp.float32)
    second = jnp.zeros((rows, 128), jnp.float32)
    for n in range(0, width, step):
        span = slice(n, n + step)
        product = jnp.dot(scaled[...], w_in[:, span], preferred_element_type=jnp.float32)
        pre = product + b_in[span][None]
        rounded = (hidden[:, span] * gelu_slope(pre)).astype(jnp.bfloat16)
        act[:, span] = rounded
        value = rounded.astype(jnp.float32)
        one = value * sides[0:1, span]
        two = value * (pre - sides[1:2, span])
        for k in range(0, step, 128):
            first = first + one[:, k : k + 128]
            second = second + two[:, k : k + 128]
    away[:rows, :] = part_of(act, w_in, 2).astype(jnp.bfloat16)
    packed = []
    for sums in (first, second):
        packed += two_parts(as_rows(jnp.sum(sums, axis=1, keepdims=True)))
    packed += [jnp.zeros((16 - 4 * (rows // 128), 128), jnp.float32)]
    away[rows : rows + 16, :] = jnp.zeros((16, share), jnp.bfloat16)
    away[rows : rows + 16, :128] = jnp.concatenate(packed, 0).astype(jnp.bfloat16)
    for own_out in own_part:
        own_out[:rows, :] = part_of(act, w_in, 3).astype(jnp.bfloat16)
        own_out[rows:, :] = away[rows:, :]


def first_parts_kernel(act, w_in, earlier, keep, mine):
    del earlier
    keep[...] = part_of(act, w_in, 1).astype(jnp.bfloat16)
    mine[...] = part_of(act, w_in, 0)


def second_parts_kernel(act, w_in, away, keep, own, mine):
    rows = act.shape[0]
    own[:rows, :] = part_of(act, w_in, 1).astype(jnp.bfloat16)
    own[rows:, :] = away[rows:, :]
    keep[...] = part_of(act, w_in, 3).astype(jnp.bfloat16)
    mine[...] = part_of(act, w_in, 0)


def middle_kernel(come, keep, go):
    rows = keep.shape[0]
    total = keep[...].astype(jnp.float32) + come[:rows, :].astype(jnp.float32)
    go[:rows, :] = total.astype(jnp.bfloat16)
    go[rows:, :] = come[rows:, :]


def add_tiles(
    base, offsets, counts, mine, got, total, come, away, mixed, centers, inverses, gain, taps, upstream, grown
):
    rows, share = mixed.shape
    width = gain.shape[0]
    packed = None
    for ref in (away, come, got, total):
        lines = ref[rows : rows + 16, :128].astype(jnp.float32)
        packed = lines if packed is None else packed + lines
    n = rows // 128
    first = as_column((packed[0:n] + packed[n : 2 * n]) * (1.0 / width))
    second = as_column((packed[2 * n : 3 * n] + packed[3 * n : 4 * n]) * (1.0 / width))
    weight = gain[pl.ds(channels_of(0, share), share)][None]
    step = 64
    for m in range(0, rows, step):
        span = slice(m, m + step)
        norm_grad = mine[span, :] + got[span, :].astype(jnp.float32) + total[span, :].astype(jnp.float32)
        inverse = inverses[span, :]
        normed = (mixed[span, :].astype(jnp.float32) - centers[span, :]) * inverse
        upstream[span, :] = inverse * (norm_grad * weight - first[span] - normed * second[span])

    low = lax.broadcasted_iota(jnp.int32, (8, 128), 0) < 4

    def tile(t, carry):
        r, q = offsets[0, base + t], offsets[1, base + t]
        doubled = []
        for b in range(share // 128):
            twice = []
            for h in range(2):
                pair = upstream[pl.ds(pl.multiple_of(t * 16 + 8 * h, 8), 8), b * 128 : (b + 1) * 128]
                turned = pltpu.roll(pair, 4, 0)
                twice += [jnp.where(low, pair, turned), jnp.where(low, turned, pair)]
            doubled.append(twice)
        for j in range(4):
            columns = pl.ds(q + (LEFT - 3 + j), 8)
            for b in range(share // 128):
                for y in range(10):
                    more = None
                    for k in range(max(0, y - 6), min(3, y) + 1):
                        term = doubled[b][k] * taps[b, (y - k) * 4 + j]
                        more = term if more is None else more + term
                    grown[b, r + y, columns, :] += more
        return carry

    listed = counts[lax.axis_index("img")] - base
    lax.fori_loop(0, jnp.clip(listed, 0, rows // 16), tile, 0)


def first_tiles_kernel(
    offsets, counts, mine, got, total, come, away, mixed, centers, inverses, gain, taps, before,
    grown, upstream,
):
    grown[...] = before[...]
    add_tiles(
        0, offsets, counts, mine, got, total, come, away, mixed, centers, inverses, gain, taps, upstream, grown
    )


def last_tiles_kernel(
    offsets, counts, screen, mine, got, total, come, away, mixed, centers, inverses, gain, taps, before,
    grad, upstream, grown, stage, sems,
):
    grown[...] = before[...]
    add_tiles(
        mixed.shape[0] // 16,
        offsets, counts, mine, got, total, come, away, mixed, centers, inverses, gain, taps, upstream, grown,
    )
    height, width = screen[0, 0], screen[0, 1]
    stores = []
    deep = SIDE // 4
    for g in range(4):

        def line(y, carry):
            seen = inside_of(SIDE, y, height, width)
            for b in range(mixed.shape[1] // 128):
                whole = grown[b, y + 3, LEFT : LEFT + SIDE, :]
                stage[y, :, b * 128 : (b + 1) * 128] = jnp.where(seen, whole, 0.0)
            return carry

        lax.fori_loop(g * deep, (g + 1) * deep, line, 0, unroll=4)
        part = pl.ds(g * deep, deep)
        store = pltpu.make_async_copy(stage.at[part], grad.at[part], sems.at[g])
        store.start()
        stores.append(store)
    for store in stores:
        store.wait()


def shift(x, by):
    n = lax.axis_size("ch")
    return lax.ppermute(x, "ch", [(i, (i + by) % n) for i in range(n)])


def shards(
    canvas,
    screen_size,
    tile_counts,
    tile_offsets,
    cotangent,
    dw_kernel,
    dw_bias,
    ln_gain,
    ln_bias,
    w_in,
    b_in,
    w_out,
    layer_scale,
):
    f32, bf16 = jnp.float32, jnp.bfloat16
    struct = pltpu.VMEM
    slots = tile_offsets.shape[0]
    share = canvas.shape[2]
    width = ln_gain.shape[0]
    hid = w_in.shape[1]
    rows = slots * TS * TS
    half = rows // 2
    lanes = share // 128
    offsets = tile_offsets.T
    left, right = shift(cotangent, 1), shift(cotangent, -1)
    mixed_a, mixed_b, near_out, taps = call(
        depthwise_kernel,
        [
            struct((half, share), bf16),
            struct((half, share), bf16),
            struct(w_out.shape, bf16),
            struct((lanes, 28, 8, 128), f32),
        ],
        [SMEM, SMEM, HBM, HBM, HBM, HBM],
        [
            pltpu.VMEM(canvas.shape, bf16),
            pltpu.VMEM((lanes, PAD_ROWS, PAD_COLS, 128), f32),
            pltpu.VMEM(dw_kernel.shape, bf16),
            pltpu.VMEM(dw_bias.shape, f32),
            pltpu.SemaphoreType.DMA((7,)),
        ],
    )(offsets, screen_size, canvas, dw_kernel, dw_bias, w_out)
    left_a, right_b = shift(mixed_a, 1), shift(mixed_b, -1)
    canvas_like = struct((lanes, PAD_ROWS, PAD_COLS, 128), f32)
    taken = call(cotangent_kernel, [canvas_like], [SMEM] * 2 + [VMEM] * 2)(
        offsets, tile_counts, cotangent, mixed_a
    )[0]
    left, taken = lax.optimization_barrier((left, taken))
    cot_a, right_a = shift(left[: slots // 2], 1), shift(mixed_a, -1)
    hidden_a, hidden_b, near_in, sides = call(
        hidden_kernel,
        [struct((half, hid), f32), struct((half, hid), f32), struct(w_in.shape, bf16), struct((8, hid), f32)],
        [VMEM] * 8 + [HBM],
        [pltpu.VMEM((3, rows, share), bf16), pltpu.SemaphoreType.DMA(())],
    )(cotangent, left, right, layer_scale, ln_gain, ln_bias, b_in, near_out, w_in)
    forward_a, forward_b, forward_cot, sides = lax.optimization_barrier(
        (left_a, right_b, right, sides)
    )
    opp_a = shift(forward_a, 1)
    beyond = shift(
        call(join_kernel, [struct((rows, share), bf16)], [VMEM] * 2)(forward_b, forward_cot)[0], -1
    )

    def with_opposite(hidden, cot, earlier):
        return call(
            opposite_kernel,
            [struct((half, hid), f32)],
            [VMEM] * 5,
            [pltpu.VMEM((half, share), bf16)],
        )(hidden, cot, layer_scale, near_out, earlier)[0]

    hidden_a, late_b = lax.optimization_barrier((with_opposite(hidden_a, cot_a, right_a), mixed_b))
    left_b = shift(late_b, 1)
    hidden_b = with_opposite(hidden_b, beyond, right_b)
    message = struct((half + 16, share), bf16)

    def block(own_parts, blocks, hidden):
        return call(
            block_kernel,
            [message] * (own_parts + 1)
            + [struct((half, hid), bf16), struct((half, 1), f32), struct((half, 1), f32)],
            [VMEM] * 10,
            [pltpu.VMEM((half, width), bf16), pltpu.VMEM((half, width), bf16)],
        )(*blocks, ln_gain, ln_bias, near_in, b_in, hidden, sides)

    def middle(come, keep):
        return call(middle_kernel, [message], [VMEM] * 2)(come, keep)[0]

    own_a, away_a, act_a, centers_a, inverses_a = block(1, (mixed_a, left_a, right_a, opp_a), hidden_a)
    come_a, got_a = shift(away_a, 1), shift(own_a, -1)
    away_b, act_b, centers_b, inverses_b = block(0, (mixed_b, left_b, right_b, beyond), hidden_b)
    come_b = shift(away_b, -1)
    part = struct((half, share), bf16)
    mine_like = struct((half, share), f32)
    keep_a, mine_a = call(first_parts_kernel, [part, mine_like], [VMEM] * 3)(act_a, near_in, got_a)
    keep_b, own_b, mine_b = call(second_parts_kernel, [part, message, mine_like], [VMEM] * 3)(
        act_b, near_in, away_b
    )
    got_b = shift(own_b, 1)
    total_a = shift(middle(come_a, keep_a), 1)
    total_b = shift(middle(come_b, keep_b), -1)
    grown = call(
        first_tiles_kernel,
        [canvas_like],
        [SMEM] * 2 + [VMEM] * 11,
        [pltpu.VMEM((half, share), f32)],
    )(
        offsets, tile_counts, mine_a, got_a, total_a, come_a, away_a, mixed_a, centers_a, inverses_a,
        ln_gain, taps, taken,
    )[0]
    return call(
        last_tiles_kernel,
        jax.ShapeDtypeStruct(canvas.shape, f32),
        [SMEM] * 3 + [VMEM] * 11,
        [
            pltpu.VMEM((half, share), f32),
            pltpu.VMEM((lanes, PAD_ROWS, PAD_COLS, 128), f32),
            pltpu.VMEM(canvas.shape, f32),
            pltpu.SemaphoreType.DMA((4,)),
        ],
        out_specs=HBM,
    )(
        offsets, tile_counts, screen_size, mine_b, got_b, total_b, come_b, away_b, mixed_b, centers_b, inverses_b,
        ln_gain, taps, grown,
    )


def solution(mesh):
    return jax.shard_map(
        shards,
        mesh=mesh,
        in_specs=(
            P("img", None, "ch"),
            P("img", None),
            P(),
            P("img", None),
            P("img", None, None, "ch"),
            P(None, "ch"),
            P("ch"),
            P(),
            P(),
            P(None, "ch"),
            P("ch"),
            P("ch", None),
            P(),
        ),
        out_specs=P("img", None, "ch"),
        check_vma=False,
    )
```

```python
import jax
import jax.numpy as jnp
from jax import lax
from jax.experimental import pallas as pl
from jax.experimental.pallas import tpu as pltpu
from jax.sharding import PartitionSpec as P

TS = 4
SIDE = 32
PAD_ROWS = 38
PAD_COLS = 48
LEFT = 8

slope_coef = 0.7978845608
cubic_coef = 0.044715
norm_eps = 1e-06

VMEM = pl.BlockSpec(memory_space=pltpu.VMEM)
SMEM = pl.BlockSpec(memory_space=pltpu.SMEM)
HBM = pl.BlockSpec(memory_space=pltpu.HBM)


def call(kernel, out_shape, in_specs, scratch=(), limit=16, out_specs=None):
    run = pl.pallas_call(
        kernel,
        out_shape=out_shape,
        in_specs=in_specs,
        out_specs=out_specs or [VMEM] * len(out_shape),
        scratch_shapes=list(scratch),
        compiler_params=pltpu.CompilerParams(vmem_limit_bytes=limit << 20),
    )

    def held(*args):
        return run(
            *(
                pltpu.with_memory_space_constraint(a, pltpu.VMEM if spec is VMEM else pltpu.HBM)
                for spec, a in zip(in_specs, args, strict=True)
            )
        )

    return held


def inside_of(rows, row, height, width):
    column = lax.broadcasted_iota(jnp.int32, (rows, 128), 0)
    return (column < width) & (row < height)


def depthwise_kernel(
    offsets, screen, canvas, dwk, bias, w_out, mixed_a, mixed_b, near_out, taps, here, framed, kern_bf, bias_row, sems
):
    lanes = canvas.shape[2] // 128
    parts = 4
    deep = SIDE // parts
    height, width = screen[0, 0], screen[0, 1]
    small = [
        pltpu.make_async_copy(dwk, kern_bf, sems.at[parts]),
        pltpu.make_async_copy(bias, bias_row, sems.at[parts + 1]),
    ]
    rows_in = [
        pltpu.make_async_copy(
            canvas.at[pl.ds(g * deep, deep)], here.at[pl.ds(g * deep, deep)], sems.at[g]
        )
        for g in range(parts)
    ]
    weights = pltpu.make_async_copy(w_out, near_out, sems.at[parts + 2])
    for fetch in (*small, *rows_in, weights):
        fetch.start()
    low = lax.broadcasted_iota(jnp.int32, (8, 128), 0) < 4
    blank = jnp.zeros((PAD_COLS, 128), jnp.float32)
    for b in range(lanes):
        for y in (0, 1, 2, SIDE + 3, SIDE + 4, SIDE + 5):
            framed[b, y] = blank
    for fetch in small:
        fetch.wait()
    for b in range(lanes):
        kern = kern_bf[:, b * 128 : (b + 1) * 128].astype(jnp.float32)
        for i in range(7):
            for j in range(4):
                first = jnp.broadcast_to(kern[7 * i + j][None], (8, 128))
                if j < 3:
                    second = jnp.broadcast_to(kern[7 * i + j + 4][None], (8, 128))
                else:
                    second = jnp.zeros((8, 128), jnp.float32)
                taps[b, i * 4 + j] = jnp.where(low, first, second)

    def fill(y, carry):
        seen = inside_of(SIDE, y, height, width)
        for b in range(lanes):
            framed[b, y + 3, 0:LEFT, :] = blank[:LEFT]
            framed[b, y + 3, LEFT + SIDE : PAD_COLS, :] = blank[: PAD_COLS - LEFT - SIDE]
            row = here[y, :, b * 128 : (b + 1) * 128].astype(jnp.float32)
            framed[b, y + 3, LEFT : LEFT + SIDE, :] = jnp.where(seen, row, 0.0)
        return carry

    for g in range(parts):
        rows_in[g].wait()
        lax.fori_loop(g * deep, (g + 1) * deep, fill, 0, unroll=4)
    count = mixed_a.shape[0] // 16
    for mixed, base in ((mixed_a, 0), (mixed_b, count)):

        def tile(t, carry):
            r, q = offsets[0, base + t], offsets[1, base + t]
            rows = pl.ds(pl.multiple_of(t * 16, 16), 16)
            for b in range(lanes):
                cut = slice(b * 128, (b + 1) * 128)
                start = jnp.broadcast_to(bias_row[cut][None], (8, 128))
                sums = [None] * 4
                for p in range(10):
                    for j in range(4):
                        seen = framed[b, r + p, pl.ds(q + (LEFT - 3 + j), 8), :]
                        for y in range(max(0, p - 6), min(3, p) + 1):
                            term = seen * taps[b, (p - y) * 4 + j]
                            sums[y] = term if sums[y] is None else sums[y] + term
                folded = [s + pltpu.roll(s, 4, 0) + start for s in sums]
                pair = [jnp.where(low, folded[y], folded[y + 1]) for y in (0, 2)]
                mixed[rows, cut] = jnp.concatenate(pair, 0).astype(jnp.bfloat16)
            return carry

        lax.fori_loop(0, count, tile, 0)
    weights.wait()


def two_parts(row):
    high = row.astype(jnp.bfloat16).astype(jnp.float32)
    return [high, row - high]


def scaled_rows(cells, scale, begin):
    share = cells.shape[3]
    flat = cells[...].astype(jnp.float32).reshape(cells.shape[0] * 16, share)
    return (scale[pl.ds(begin, share)][None] * flat).astype(jnp.bfloat16)


def channels_of(ahead, share):
    return pl.multiple_of(lax.rem(lax.axis_index("ch") + ahead, 4) * share, 128)


def cotangent_kernel(offsets, counts, own, earlier, taken):
    del earlier
    taken[...] = jnp.zeros_like(taken)

    def tile(t, carry):
        r, q = offsets[0, t], offsets[1, t]
        for y in range(4):
            cells = own[t, y].astype(jnp.float32)
            for b in range(own.shape[3] // 128):
                taken[b, r + 3 + y, pl.ds(q + LEFT, 4), :] += cells[:, b * 128 : (b + 1) * 128]
        return carry

    lax.fori_loop(0, counts[lax.axis_index("img")], tile, 0)


def hidden_kernel(
    own, left, right, scale, gain, bias, b_in, w_out, w_in,
    hidden_a, hidden_b, near_in, sides, flat, sem,
):
    fetch = pltpu.make_async_copy(w_in, near_in, sem)
    fetch.start()
    share = own.shape[3]
    begins = []
    for k, (cells, ahead) in enumerate(((own, 0), (left, 3), (right, 1))):
        begins.append(channels_of(ahead, share))
        flat[k] = scaled_rows(cells, scale, begins[k])
    step = 512
    half = hidden_a.shape[0]
    for n in range(0, hidden_a.shape[1], step):
        total = None
        for k, begin in enumerate(begins):
            product = lax.dot_general(
                flat[k],
                w_out[n : n + step, pl.ds(begin, share)],
                (((1,), (1,)), ((), ())),
                preferred_element_type=jnp.float32,
            )
            total = product if total is None else total + product
        hidden_a[:, n : n + step] = total[:half]
        hidden_b[:, n : n + step] = total[half:]
    width = gain.shape[0]
    lines = two_parts(gain[...][None]) + two_parts(bias[...][None])
    lines = jnp.concatenate(lines + [jnp.zeros((12, width), jnp.float32)], 0).astype(jnp.bfloat16)
    fetch.wait()
    both = jnp.dot(lines, near_in[...], preferred_element_type=jnp.float32)
    sides[0:1, :] = both[0:1] + both[1:2]
    sides[1:2, :] = both[2:3] + both[3:4] + b_in[...][None]


def opposite_kernel(before, cot, scale, w_out, hidden, flat):
    share = flat.shape[1]
    begin = channels_of(2, share)
    flat[...] = scaled_rows(cot, scale, begin)
    step = 512
    for n in range(0, before.shape[1], step):
        hidden[:, n : n + step] = before[:, n : n + step] + lax.dot_general(
            flat[...],
            w_out[n : n + step, pl.ds(begin, share)],
            (((1,), (1,)), ((), ())),
            preferred_element_type=jnp.float32,
        )


def gelu_slope(v):
    square = v * v
    t = jnp.tanh(v * (slope_coef + slope_coef * cubic_coef * square))
    w = v * (0.5 * slope_coef + 1.5 * slope_coef * cubic_coef * square)
    return (0.5 + 0.5 * t) + w * (1.0 - t * t)


def as_rows(column):
    count = column.shape[0] // 128
    eye = lax.broadcasted_iota(jnp.int32, (128, 128), 0) == lax.broadcasted_iota(jnp.int32, (128, 128), 1)
    return jnp.concatenate(
        [
            jnp.sum(jnp.where(eye, column[g * 128 : (g + 1) * 128], 0.0), axis=0, keepdims=True)
            for g in range(count)
        ],
        0,
    )


def as_column(rows):
    eye = lax.broadcasted_iota(jnp.int32, (128, 128), 0) == lax.broadcasted_iota(jnp.int32, (128, 128), 1)
    return jnp.concatenate(
        [
            jnp.sum(jnp.where(eye, rows[g : g + 1], 0.0), axis=1, keepdims=True)
            for g in range(rows.shape[0])
        ],
        0,
    )


def part_of(act, w_in, ahead):
    share = w_in.shape[0] // 4
    return lax.dot_general(
        act[...],
        w_in[pl.ds(channels_of(ahead, share), share), :],
        (((1,), (1,)), ((), ())),
        preferred_element_type=jnp.float32,
    )


def block_kernel(
    own, left, right, opp, gain, bias, w_in, b_in, hidden, sides,
    *outs,
):
    *own_part, away, act, centers, inverses, full, scaled = outs
    rows, width = full.shape
    share = own.shape[1]
    for ref, ahead in ((own, 0), (left, 3), (right, 1), (opp, 2)):
        full[:, pl.ds(channels_of(ahead, share), share)] = ref[...]
    step = 64
    for m in range(0, rows, step):
        values = full[m : m + step, :].astype(jnp.float32)
        center = jnp.mean(values, axis=1, keepdims=True)
        apart = values - center
        inverse = lax.rsqrt(jnp.mean(apart * apart, axis=1, keepdims=True) + norm_eps)
        centers[m : m + step, :] = center
        inverses[m : m + step, :] = inverse
        scaled[m : m + step, :] = (apart * inverse * gain[...][None] + bias[...][None]).astype(
            jnp.bfloat16
        )
    step = 512
    first = jnp.zeros((rows, 128), jnp.float32)
    second = jnp.zeros((rows, 128), jnp.float32)
    for n in range(0, width, step):
        span = slice(n, n + step)
        product = jnp.dot(scaled[...], w_in[:, span], preferred_element_type=jnp.float32)
        pre = product + b_in[span][None]
        rounded = (hidden[:, span] * gelu_slope(pre)).astype(jnp.bfloat16)
        act[:, span] = rounded
        value = rounded.astype(jnp.float32)
        one = value * sides[0:1, span]
        two = value * (pre - sides[1:2, span])
        for k in range(0, step, 128):
            first = first + one[:, k : k + 128]
            second = second + two[:, k : k + 128]
    away[:rows, :] = part_of(act, w_in, 2).astype(jnp.bfloat16)
    packed = []
    for sums in (first, second):
        packed += two_parts(as_rows(jnp.sum(sums, axis=1, keepdims=True)))
    packed += [jnp.zeros((16 - 4 * (rows // 128), 128), jnp.float32)]
    away[rows : rows + 16, :] = jnp.zeros((16, share), jnp.bfloat16)
    away[rows : rows + 16, :128] = jnp.concatenate(packed, 0).astype(jnp.bfloat16)
    for own_out in own_part:
        own_out[:rows, :] = part_of(act, w_in, 3).astype(jnp.bfloat16)
        own_out[rows:, :] = away[rows:, :]


def first_parts_kernel(act, w_in, earlier, keep, mine):
    del earlier
    keep[...] = part_of(act, w_in, 1).astype(jnp.bfloat16)
    mine[...] = part_of(act, w_in, 0)


def second_parts_kernel(act, w_in, away, keep, own, mine):
    rows = act.shape[0]
    own[:rows, :] = part_of(act, w_in, 1).astype(jnp.bfloat16)
    own[rows:, :] = away[rows:, :]
    keep[...] = part_of(act, w_in, 3).astype(jnp.bfloat16)
    mine[...] = part_of(act, w_in, 0)


def middle_kernel(come, keep, go):
    rows = keep.shape[0]
    total = keep[...].astype(jnp.float32) + come[:rows, :].astype(jnp.float32)
    go[:rows, :] = total.astype(jnp.bfloat16)
    go[rows:, :] = come[rows:, :]


def add_tiles(
    base, offsets, counts, mine, got, total, come, away, mixed, centers, inverses, gain, taps, upstream, grown
):
    rows, share = mixed.shape
    width = gain.shape[0]
    packed = None
    for ref in (away, come, got, total):
        lines = ref[rows : rows + 16, :128].astype(jnp.float32)
        packed = lines if packed is None else packed + lines
    n = rows // 128
    first = as_column((packed[0:n] + packed[n : 2 * n]) * (1.0 / width))
    second = as_column((packed[2 * n : 3 * n] + packed[3 * n : 4 * n]) * (1.0 / width))
    weight = gain[pl.ds(channels_of(0, share), share)][None]
    step = 64
    for m in range(0, rows, step):
        span = slice(m, m + step)
        norm_grad = mine[span, :] + got[span, :].astype(jnp.float32) + total[span, :].astype(jnp.float32)
        inverse = inverses[span, :]
        normed = (mixed[span, :].astype(jnp.float32) - centers[span, :]) * inverse
        upstream[span, :] = inverse * (norm_grad * weight - first[span] - normed * second[span])

    low = lax.broadcasted_iota(jnp.int32, (8, 128), 0) < 4

    def tile(t, carry):
        r, q = offsets[0, base + t], offsets[1, base + t]
        doubled = []
        for b in range(share // 128):
            twice = []
            for h in range(2):
                pair = upstream[pl.ds(pl.multiple_of(t * 16 + 8 * h, 8), 8), b * 128 : (b + 1) * 128]
                turned = pltpu.roll(pair, 4, 0)
                twice += [jnp.where(low, pair, turned), jnp.where(low, turned, pair)]
            doubled.append(twice)
        for j in range(4):
            columns = pl.ds(q + (LEFT - 3 + j), 8)
            for b in range(share // 128):
                for y in range(10):
                    more = None
                    for k in range(max(0, y - 6), min(3, y) + 1):
                        term = doubled[b][k] * taps[b, (y - k) * 4 + j]
                        more = term if more is None else more + term
                    grown[b, r + y, columns, :] += more
        return carry

    listed = counts[lax.axis_index("img")] - base
    lax.fori_loop(0, jnp.clip(listed, 0, rows // 16), tile, 0)


def first_tiles_kernel(
    offsets, counts, mine, got, total, come, away, mixed, centers, inverses, gain, taps, before,
    grown, upstream,
):
    grown[...] = before[...]
    add_tiles(
        0, offsets, counts, mine, got, total, come, away, mixed, centers, inverses, gain, taps, upstream, grown
    )


def last_tiles_kernel(
    offsets, counts, screen, mine, got, total, come, away, mixed, centers, inverses, gain, taps, before,
    grad, upstream, grown, stage, sems,
):
    grown[...] = before[...]
    add_tiles(
        mixed.shape[0] // 16,
        offsets, counts, mine, got, total, come, away, mixed, centers, inverses, gain, taps, upstream, grown,
    )
    height, width = screen[0, 0], screen[0, 1]
    stores = []
    deep = SIDE // 4
    for g in range(4):

        def line(y, carry):
            seen = inside_of(SIDE, y, height, width)
            for b in range(mixed.shape[1] // 128):
                whole = grown[b, y + 3, LEFT : LEFT + SIDE, :]
                stage[y, :, b * 128 : (b + 1) * 128] = jnp.where(seen, whole, 0.0)
            return carry

        lax.fori_loop(g * deep, (g + 1) * deep, line, 0, unroll=4)
        part = pl.ds(g * deep, deep)
        store = pltpu.make_async_copy(stage.at[part], grad.at[part], sems.at[g])
        store.start()
        stores.append(store)
    for store in stores:
        store.wait()


def shift(x, by):
    n = lax.axis_size("ch")
    return lax.ppermute(x, "ch", [(i, (i + by) % n) for i in range(n)])


def shards(
    canvas,
    screen_size,
    tile_counts,
    tile_offsets,
    cotangent,
    dw_kernel,
    dw_bias,
    ln_gain,
    ln_bias,
    w_in,
    b_in,
    w_out,
    layer_scale,
):
    f32, bf16 = jnp.float32, jnp.bfloat16
    struct = pltpu.VMEM
    slots = tile_offsets.shape[0]
    share = canvas.shape[2]
    width = ln_gain.shape[0]
    hid = w_in.shape[1]
    rows = slots * TS * TS
    half = rows // 2
    lanes = share // 128
    offsets = tile_offsets.T
    left, right = shift(cotangent, 1), shift(cotangent, -1)
    mixed_a, mixed_b, near_out, taps = call(
        depthwise_kernel,
        [
            struct((half, share), bf16),
            struct((half, share), bf16),
            struct(w_out.shape, bf16),
            struct((lanes, 28, 8, 128), f32),
        ],
        [SMEM, SMEM, HBM, HBM, HBM, HBM],
        [
            pltpu.VMEM(canvas.shape, bf16),
            pltpu.VMEM((lanes, PAD_ROWS, PAD_COLS, 128), f32),
            pltpu.VMEM(dw_kernel.shape, bf16),
            pltpu.VMEM(dw_bias.shape, f32),
            pltpu.SemaphoreType.DMA((7,)),
        ],
    )(offsets, screen_size, canvas, dw_kernel, dw_bias, w_out)
    left_a, right_b = shift(mixed_a, 1), shift(mixed_b, -1)
    canvas_like = struct((lanes, PAD_ROWS, PAD_COLS, 128), f32)
    taken = call(cotangent_kernel, [canvas_like], [SMEM] * 2 + [VMEM] * 2)(
        offsets, tile_counts, cotangent, mixed_a
    )[0]
    left, taken = lax.optimization_barrier((left, taken))
    cot_a, right_a = shift(left[: slots // 2], 1), shift(mixed_a, -1)
    hidden_a, hidden_b, near_in, sides = call(
        hidden_kernel,
        [struct((half, hid), f32), struct((half, hid), f32), struct(w_in.shape, bf16), struct((8, hid), f32)],
        [VMEM] * 8 + [HBM],
        [pltpu.VMEM((3, rows, share), bf16), pltpu.SemaphoreType.DMA(())],
    )(cotangent, left, right, layer_scale, ln_gain, ln_bias, b_in, near_out, w_in)
    forward_a, forward_b, forward_cot, sides = lax.optimization_barrier(
        (left_a, right_b, right, sides)
    )
    opp_a, opp_b = shift(forward_a, 1), shift(forward_b, -1)
    cot_b = shift(forward_cot[slots // 2 :], -1)

    def with_opposite(hidden, cot):
        return call(
            opposite_kernel,
            [struct((half, hid), f32)],
            [VMEM] * 4,
            [pltpu.VMEM((half, share), bf16)],
        )(hidden, cot, layer_scale, near_out)[0]

    hidden_a, late_b = lax.optimization_barrier((with_opposite(hidden_a, cot_a), mixed_b))
    left_b = shift(late_b, 1)
    hidden_b = with_opposite(hidden_b, cot_b)
    message = struct((half + 16, share), bf16)

    def block(own_parts, blocks, hidden):
        return call(
            block_kernel,
            [message] * (own_parts + 1)
            + [struct((half, hid), bf16), struct((half, 1), f32), struct((half, 1), f32)],
            [VMEM] * 10,
            [pltpu.VMEM((half, width), bf16), pltpu.VMEM((half, width), bf16)],
        )(*blocks, ln_gain, ln_bias, near_in, b_in, hidden, sides)

    def middle(come, keep):
        return call(middle_kernel, [message], [VMEM] * 2)(come, keep)[0]

    own_a, away_a, act_a, centers_a, inverses_a = block(1, (mixed_a, left_a, right_a, opp_a), hidden_a)
    come_a, got_a = shift(away_a, 1), shift(own_a, -1)
    away_b, act_b, centers_b, inverses_b = block(0, (mixed_b, left_b, right_b, opp_b), hidden_b)
    come_b = shift(away_b, -1)
    part = struct((half, share), bf16)
    mine_like = struct((half, share), f32)
    keep_a, mine_a = call(first_parts_kernel, [part, mine_like], [VMEM] * 3)(act_a, near_in, got_a)
    keep_b, own_b, mine_b = call(second_parts_kernel, [part, message, mine_like], [VMEM] * 3)(
        act_b, near_in, away_b
    )
    got_b = shift(own_b, 1)
    total_a = shift(middle(come_a, keep_a), 1)
    total_b = shift(middle(come_b, keep_b), -1)
    grown = call(
        first_tiles_kernel,
        [canvas_like],
        [SMEM] * 2 + [VMEM] * 11,
        [pltpu.VMEM((half, share), f32)],
    )(
        offsets, tile_counts, mine_a, got_a, total_a, come_a, away_a, mixed_a, centers_a, inverses_a,
        ln_gain, taps, taken,
    )[0]
    return call(
        last_tiles_kernel,
        jax.ShapeDtypeStruct(canvas.shape, f32),
        [SMEM] * 3 + [VMEM] * 11,
        [
            pltpu.VMEM((half, share), f32),
            pltpu.VMEM((lanes, PAD_ROWS, PAD_COLS, 128), f32),
            pltpu.VMEM(canvas.shape, f32),
            pltpu.SemaphoreType.DMA((4,)),
        ],
        out_specs=HBM,
    )(
        offsets, tile_counts, screen_size, mine_b, got_b, total_b, come_b, away_b, mixed_b, centers_b, inverses_b,
        ln_gain, taps, grown,
    )


def solution(mesh):
    return jax.shard_map(
        shards,
        mesh=mesh,
        in_specs=(
            P("img", None, "ch"),
            P("img", None),
            P(),
            P("img", None),
            P("img", None, None, "ch"),
            P(None, "ch"),
            P("ch"),
            P(),
            P(),
            P(None, "ch"),
            P("ch"),
            P("ch", None),
            P(),
        ),
        out_specs=P("img", None, "ch"),
        check_vma=False,
    )
```

```python
import jax
import jax.numpy as jnp
from jax import lax
from jax.experimental import pallas as pl
from jax.experimental.pallas import tpu as pltpu
from jax.sharding import PartitionSpec as P

TS = 4
SIDE = 32
PAD_ROWS = 38
PAD_COLS = 48
LEFT = 8

slope_coef = 0.7978845608
cubic_coef = 0.044715
norm_eps = 1e-06

VMEM = pl.BlockSpec(memory_space=pltpu.VMEM)
SMEM = pl.BlockSpec(memory_space=pltpu.SMEM)
HBM = pl.BlockSpec(memory_space=pltpu.HBM)


def call(kernel, out_shape, in_specs, scratch=(), limit=16, out_specs=None):
    run = pl.pallas_call(
        kernel,
        out_shape=out_shape,
        in_specs=in_specs,
        out_specs=out_specs or [VMEM] * len(out_shape),
        scratch_shapes=list(scratch),
        compiler_params=pltpu.CompilerParams(vmem_limit_bytes=limit << 20),
    )

    def held(*args):
        return run(
            *(
                pltpu.with_memory_space_constraint(a, pltpu.VMEM if spec is VMEM else pltpu.HBM)
                for spec, a in zip(in_specs, args, strict=True)
            )
        )

    return held


def inside_of(rows, row, height, width):
    column = lax.broadcasted_iota(jnp.int32, (rows, 128), 0)
    return (column < width) & (row < height)


def depthwise_kernel(
    offsets, screen, canvas, dwk, bias, w_out, mixed_a, mixed_b, near_out, taps, here, framed, kern_bf, bias_row, sems
):
    lanes = canvas.shape[2] // 128
    parts = 4
    deep = SIDE // parts
    height, width = screen[0, 0], screen[0, 1]
    small = [
        pltpu.make_async_copy(dwk, kern_bf, sems.at[parts]),
        pltpu.make_async_copy(bias, bias_row, sems.at[parts + 1]),
    ]
    rows_in = [
        pltpu.make_async_copy(
            canvas.at[pl.ds(g * deep, deep)], here.at[pl.ds(g * deep, deep)], sems.at[g]
        )
        for g in range(parts)
    ]
    weights = pltpu.make_async_copy(w_out, near_out, sems.at[parts + 2])
    for fetch in (*small, *rows_in, weights):
        fetch.start()
    low = lax.broadcasted_iota(jnp.int32, (8, 128), 0) < 4
    blank = jnp.zeros((PAD_COLS, 128), jnp.float32)
    for b in range(lanes):
        for y in (0, 1, 2, SIDE + 3, SIDE + 4, SIDE + 5):
            framed[b, y] = blank
    for fetch in small:
        fetch.wait()
    for b in range(lanes):
        kern = kern_bf[:, b * 128 : (b + 1) * 128].astype(jnp.float32)
        for i in range(7):
            for j in range(4):
                first = jnp.broadcast_to(kern[7 * i + j][None], (8, 128))
                if j < 3:
                    second = jnp.broadcast_to(kern[7 * i + j + 4][None], (8, 128))
                else:
                    second = jnp.zeros((8, 128), jnp.float32)
                taps[b, i * 4 + j] = jnp.where(low, first, second)

    def fill(y, carry):
        seen = inside_of(SIDE, y, height, width)
        for b in range(lanes):
            framed[b, y + 3, 0:LEFT, :] = blank[:LEFT]
            framed[b, y + 3, LEFT + SIDE : PAD_COLS, :] = blank[: PAD_COLS - LEFT - SIDE]
            row = here[y, :, b * 128 : (b + 1) * 128].astype(jnp.float32)
            framed[b, y + 3, LEFT : LEFT + SIDE, :] = jnp.where(seen, row, 0.0)
        return carry

    for g in range(parts):
        rows_in[g].wait()
        lax.fori_loop(g * deep, (g + 1) * deep, fill, 0, unroll=4)
    count = mixed_a.shape[0] // 16
    for mixed, base in ((mixed_a, 0), (mixed_b, count)):

        def tile(t, carry):
            r, q = offsets[0, base + t], offsets[1, base + t]
            rows = pl.ds(pl.multiple_of(t * 16, 16), 16)
            for b in range(lanes):
                cut = slice(b * 128, (b + 1) * 128)
                start = jnp.broadcast_to(bias_row[cut][None], (8, 128))
                sums = [None] * 4
                for p in range(10):
                    for j in range(4):
                        seen = framed[b, r + p, pl.ds(q + (LEFT - 3 + j), 8), :]
                        for y in range(max(0, p - 6), min(3, p) + 1):
                            term = seen * taps[b, (p - y) * 4 + j]
                            sums[y] = term if sums[y] is None else sums[y] + term
                folded = [s + pltpu.roll(s, 4, 0) + start for s in sums]
                pair = [jnp.where(low, folded[y], folded[y + 1]) for y in (0, 2)]
                mixed[rows, cut] = jnp.concatenate(pair, 0).astype(jnp.bfloat16)
            return carry

        lax.fori_loop(0, count, tile, 0)
    weights.wait()


def two_parts(row):
    high = row.astype(jnp.bfloat16).astype(jnp.float32)
    return [high, row - high]


def scaled_rows(cells, scale, begin):
    share = cells.shape[3]
    flat = cells[...].astype(jnp.float32).reshape(cells.shape[0] * 16, share)
    return (scale[pl.ds(begin, share)][None] * flat).astype(jnp.bfloat16)


def channels_of(ahead, share):
    return pl.multiple_of(lax.rem(lax.axis_index("ch") + ahead, 4) * share, 128)


def cotangent_kernel(offsets, counts, own, earlier, taken):
    del earlier
    taken[...] = jnp.zeros_like(taken)

    def tile(t, carry):
        r, q = offsets[0, t], offsets[1, t]
        for y in range(4):
            cells = own[t, y].astype(jnp.float32)
            for b in range(own.shape[3] // 128):
                taken[b, r + 3 + y, pl.ds(q + LEFT, 4), :] += cells[:, b * 128 : (b + 1) * 128]
        return carry

    lax.fori_loop(0, counts[lax.axis_index("img")], tile, 0)


def hidden_kernel(
    own, left, right, scale, gain, bias, b_in, w_out, w_in,
    hidden_a, hidden_b, near_in, sides, flat, sem,
):
    fetch = pltpu.make_async_copy(w_in, near_in, sem)
    fetch.start()
    share = own.shape[3]
    begins = []
    for k, (cells, ahead) in enumerate(((own, 0), (left, 3), (right, 1))):
        begins.append(channels_of(ahead, share))
        flat[k] = scaled_rows(cells, scale, begins[k])
    step = 512
    half = hidden_a.shape[0]
    for n in range(0, hidden_a.shape[1], step):
        total = None
        for k, begin in enumerate(begins):
            product = lax.dot_general(
                flat[k],
                w_out[n : n + step, pl.ds(begin, share)],
                (((1,), (1,)), ((), ())),
                preferred_element_type=jnp.float32,
            )
            total = product if total is None else total + product
        hidden_a[:, n : n + step] = total[:half]
        hidden_b[:, n : n + step] = total[half:]
    width = gain.shape[0]
    lines = two_parts(gain[...][None]) + two_parts(bias[...][None])
    lines = jnp.concatenate(lines + [jnp.zeros((12, width), jnp.float32)], 0).astype(jnp.bfloat16)
    fetch.wait()
    both = jnp.dot(lines, near_in[...], preferred_element_type=jnp.float32)
    sides[0:1, :] = both[0:1] + both[1:2]
    sides[1:2, :] = both[2:3] + both[3:4] + b_in[...][None]


def opposite_kernel(before, cot, scale, w_out, hidden, flat):
    share = flat.shape[1]
    begin = channels_of(2, share)
    flat[...] = scaled_rows(cot, scale, begin)
    step = 512
    for n in range(0, before.shape[1], step):
        hidden[:, n : n + step] = before[:, n : n + step] + lax.dot_general(
            flat[...],
            w_out[n : n + step, pl.ds(begin, share)],
            (((1,), (1,)), ((), ())),
            preferred_element_type=jnp.float32,
        )


def gelu_slope(v):
    square = v * v
    t = jnp.tanh(v * (slope_coef + slope_coef * cubic_coef * square))
    w = v * (0.5 * slope_coef + 1.5 * slope_coef * cubic_coef * square)
    return (0.5 + 0.5 * t) + w * (1.0 - t * t)


def as_rows(column):
    count = column.shape[0] // 128
    eye = lax.broadcasted_iota(jnp.int32, (128, 128), 0) == lax.broadcasted_iota(jnp.int32, (128, 128), 1)
    return jnp.concatenate(
        [
            jnp.sum(jnp.where(eye, column[g * 128 : (g + 1) * 128], 0.0), axis=0, keepdims=True)
            for g in range(count)
        ],
        0,
    )


def as_column(rows):
    eye = lax.broadcasted_iota(jnp.int32, (128, 128), 0) == lax.broadcasted_iota(jnp.int32, (128, 128), 1)
    return jnp.concatenate(
        [
            jnp.sum(jnp.where(eye, rows[g : g + 1], 0.0), axis=1, keepdims=True)
            for g in range(rows.shape[0])
        ],
        0,
    )


def part_of(act, w_in, ahead):
    share = w_in.shape[0] // 4
    return lax.dot_general(
        act[...],
        w_in[pl.ds(channels_of(ahead, share), share), :],
        (((1,), (1,)), ((), ())),
        preferred_element_type=jnp.float32,
    )


def block_kernel(
    own, left, right, opp, gain, bias, w_in, b_in, hidden, sides,
    *outs,
):
    *own_part, away, act, centers, inverses, full, scaled = outs
    rows, width = full.shape
    share = own.shape[1]
    for ref, ahead in ((own, 0), (left, 3), (right, 1), (opp, 2)):
        full[:, pl.ds(channels_of(ahead, share), share)] = ref[...]
    step = 64
    for m in range(0, rows, step):
        values = full[m : m + step, :].astype(jnp.float32)
        center = jnp.mean(values, axis=1, keepdims=True)
        apart = values - center
        inverse = lax.rsqrt(jnp.mean(apart * apart, axis=1, keepdims=True) + norm_eps)
        centers[m : m + step, :] = center
        inverses[m : m + step, :] = inverse
        scaled[m : m + step, :] = (apart * inverse * gain[...][None] + bias[...][None]).astype(
            jnp.bfloat16
        )
    step = 256
    first = jnp.zeros((rows, 128), jnp.float32)
    second = jnp.zeros((rows, 128), jnp.float32)
    for n in range(0, width, step):
        span = slice(n, n + step)
        product = jnp.dot(scaled[...], w_in[:, span], preferred_element_type=jnp.float32)
        pre = product + b_in[span][None]
        rounded = (hidden[:, span] * gelu_slope(pre)).astype(jnp.bfloat16)
        act[:, span] = rounded
        value = rounded.astype(jnp.float32)
        one = value * sides[0:1, span]
        two = value * (pre - sides[1:2, span])
        for k in range(0, step, 128):
            first = first + one[:, k : k + 128]
            second = second + two[:, k : k + 128]
    away[:rows, :] = part_of(act, w_in, 2).astype(jnp.bfloat16)
    packed = []
    for sums in (first, second):
        packed += two_parts(as_rows(jnp.sum(sums, axis=1, keepdims=True)))
    packed += [jnp.zeros((16 - 4 * (rows // 128), 128), jnp.float32)]
    away[rows : rows + 16, :] = jnp.zeros((16, share), jnp.bfloat16)
    away[rows : rows + 16, :128] = jnp.concatenate(packed, 0).astype(jnp.bfloat16)
    for own_out in own_part:
        own_out[:rows, :] = part_of(act, w_in, 3).astype(jnp.bfloat16)
        own_out[rows:, :] = away[rows:, :]


def first_parts_kernel(act, w_in, earlier, keep, mine):
    del earlier
    keep[...] = part_of(act, w_in, 1).astype(jnp.bfloat16)
    mine[...] = part_of(act, w_in, 0)


def second_parts_kernel(act, w_in, away, keep, own, mine):
    rows = act.shape[0]
    own[:rows, :] = part_of(act, w_in, 1).astype(jnp.bfloat16)
    own[rows:, :] = away[rows:, :]
    keep[...] = part_of(act, w_in, 3).astype(jnp.bfloat16)
    mine[...] = part_of(act, w_in, 0)


def middle_kernel(come, keep, go):
    rows = keep.shape[0]
    total = keep[...].astype(jnp.float32) + come[:rows, :].astype(jnp.float32)
    go[:rows, :] = total.astype(jnp.bfloat16)
    go[rows:, :] = come[rows:, :]


def add_tiles(
    base, offsets, counts, mine, got, total, come, away, mixed, centers, inverses, gain, taps, upstream, grown
):
    rows, share = mixed.shape
    width = gain.shape[0]
    packed = None
    for ref in (away, come, got, total):
        lines = ref[rows : rows + 16, :128].astype(jnp.float32)
        packed = lines if packed is None else packed + lines
    n = rows // 128
    first = as_column((packed[0:n] + packed[n : 2 * n]) * (1.0 / width))
    second = as_column((packed[2 * n : 3 * n] + packed[3 * n : 4 * n]) * (1.0 / width))
    weight = gain[pl.ds(channels_of(0, share), share)][None]
    step = 64
    for m in range(0, rows, step):
        span = slice(m, m + step)
        norm_grad = mine[span, :] + got[span, :].astype(jnp.float32) + total[span, :].astype(jnp.float32)
        inverse = inverses[span, :]
        normed = (mixed[span, :].astype(jnp.float32) - centers[span, :]) * inverse
        upstream[span, :] = inverse * (norm_grad * weight - first[span] - normed * second[span])

    low = lax.broadcasted_iota(jnp.int32, (8, 128), 0) < 4

    def tile(t, carry):
        r, q = offsets[0, base + t], offsets[1, base + t]
        doubled = []
        for b in range(share // 128):
            twice = []
            for h in range(2):
                pair = upstream[pl.ds(pl.multiple_of(t * 16 + 8 * h, 8), 8), b * 128 : (b + 1) * 128]
                turned = pltpu.roll(pair, 4, 0)
                twice += [jnp.where(low, pair, turned), jnp.where(low, turned, pair)]
            doubled.append(twice)
        for j in range(4):
            columns = pl.ds(q + (LEFT - 3 + j), 8)
            for b in range(share // 128):
                for y in range(10):
                    more = None
                    for k in range(max(0, y - 6), min(3, y) + 1):
                        term = doubled[b][k] * taps[b, (y - k) * 4 + j]
                        more = term if more is None else more + term
                    grown[b, r + y, columns, :] += more
        return carry

    listed = counts[lax.axis_index("img")] - base
    lax.fori_loop(0, jnp.clip(listed, 0, rows // 16), tile, 0)


def first_tiles_kernel(
    offsets, counts, mine, got, total, come, away, mixed, centers, inverses, gain, taps, before,
    grown, upstream,
):
    grown[...] = before[...]
    add_tiles(
        0, offsets, counts, mine, got, total, come, away, mixed, centers, inverses, gain, taps, upstream, grown
    )


def last_tiles_kernel(
    offsets, counts, screen, mine, got, total, come, away, mixed, centers, inverses, gain, taps, before,
    grad, upstream, grown, stage, sems,
):
    grown[...] = before[...]
    add_tiles(
        mixed.shape[0] // 16,
        offsets, counts, mine, got, total, come, away, mixed, centers, inverses, gain, taps, upstream, grown,
    )
    height, width = screen[0, 0], screen[0, 1]
    stores = []
    deep = SIDE // 4
    for g in range(4):

        def line(y, carry):
            seen = inside_of(SIDE, y, height, width)
            for b in range(mixed.shape[1] // 128):
                whole = grown[b, y + 3, LEFT : LEFT + SIDE, :]
                stage[y, :, b * 128 : (b + 1) * 128] = jnp.where(seen, whole, 0.0)
            return carry

        lax.fori_loop(g * deep, (g + 1) * deep, line, 0, unroll=4)
        part = pl.ds(g * deep, deep)
        store = pltpu.make_async_copy(stage.at[part], grad.at[part], sems.at[g])
        store.start()
        stores.append(store)
    for store in stores:
        store.wait()


def shift(x, by):
    n = lax.axis_size("ch")
    return lax.ppermute(x, "ch", [(i, (i + by) % n) for i in range(n)])


def shards(
    canvas,
    screen_size,
    tile_counts,
    tile_offsets,
    cotangent,
    dw_kernel,
    dw_bias,
    ln_gain,
    ln_bias,
    w_in,
    b_in,
    w_out,
    layer_scale,
):
    f32, bf16 = jnp.float32, jnp.bfloat16
    struct = pltpu.VMEM
    slots = tile_offsets.shape[0]
    share = canvas.shape[2]
    width = ln_gain.shape[0]
    hid = w_in.shape[1]
    rows = slots * TS * TS
    half = rows // 2
    lanes = share // 128
    offsets = tile_offsets.T
    left, right = shift(cotangent, 1), shift(cotangent, -1)
    mixed_a, mixed_b, near_out, taps = call(
        depthwise_kernel,
        [
            struct((half, share), bf16),
            struct((half, share), bf16),
            struct(w_out.shape, bf16),
            struct((lanes, 28, 8, 128), f32),
        ],
        [SMEM, SMEM, HBM, HBM, HBM, HBM],
        [
            pltpu.VMEM(canvas.shape, bf16),
            pltpu.VMEM((lanes, PAD_ROWS, PAD_COLS, 128), f32),
            pltpu.VMEM(dw_kernel.shape, bf16),
            pltpu.VMEM(dw_bias.shape, f32),
            pltpu.SemaphoreType.DMA((7,)),
        ],
    )(offsets, screen_size, canvas, dw_kernel, dw_bias, w_out)
    left_a, right_b = shift(mixed_a, 1), shift(mixed_b, -1)
    canvas_like = struct((lanes, PAD_ROWS, PAD_COLS, 128), f32)
    taken = call(cotangent_kernel, [canvas_like], [SMEM] * 2 + [VMEM] * 2)(
        offsets, tile_counts, cotangent, mixed_a
    )[0]
    left, taken = lax.optimization_barrier((left, taken))
    cot_a, right_a = shift(left[: slots // 2], 1), shift(mixed_a, -1)
    hidden_a, hidden_b, near_in, sides = call(
        hidden_kernel,
        [struct((half, hid), f32), struct((half, hid), f32), struct(w_in.shape, bf16), struct((8, hid), f32)],
        [VMEM] * 8 + [HBM],
        [pltpu.VMEM((3, rows, share), bf16), pltpu.SemaphoreType.DMA(())],
    )(cotangent, left, right, layer_scale, ln_gain, ln_bias, b_in, near_out, w_in)
    forward_a, forward_b, forward_cot, sides = lax.optimization_barrier(
        (left_a, right_b, right, sides)
    )
    opp_a, opp_b = shift(forward_a, 1), shift(forward_b, -1)
    cot_b = shift(forward_cot[slots // 2 :], -1)

    def with_opposite(hidden, cot):
        return call(
            opposite_kernel,
            [struct((half, hid), f32)],
            [VMEM] * 4,
            [pltpu.VMEM((half, share), bf16)],
        )(hidden, cot, layer_scale, near_out)[0]

    hidden_a, late_b = lax.optimization_barrier((with_opposite(hidden_a, cot_a), mixed_b))
    left_b = shift(late_b, 1)
    hidden_b = with_opposite(hidden_b, cot_b)
    message = struct((half + 16, share), bf16)

    def block(own_parts, blocks, hidden):
        return call(
            block_kernel,
            [message] * (own_parts + 1)
            + [struct((half, hid), bf16), struct((half, 1), f32), struct((half, 1), f32)],
            [VMEM] * 10,
            [pltpu.VMEM((half, width), bf16), pltpu.VMEM((half, width), bf16)],
        )(*blocks, ln_gain, ln_bias, near_in, b_in, hidden, sides)

    def middle(come, keep):
        return call(middle_kernel, [message], [VMEM] * 2)(come, keep)[0]

    own_a, away_a, act_a, centers_a, inverses_a = block(1, (mixed_a, left_a, right_a, opp_a), hidden_a)
    come_a, got_a = shift(away_a, 1), shift(own_a, -1)
    away_b, act_b, centers_b, inverses_b = block(0, (mixed_b, left_b, right_b, opp_b), hidden_b)
    come_b = shift(away_b, -1)
    part = struct((half, share), bf16)
    mine_like = struct((half, share), f32)
    keep_a, mine_a = call(first_parts_kernel, [part, mine_like], [VMEM] * 3)(act_a, near_in, got_a)
    keep_b, own_b, mine_b = call(second_parts_kernel, [part, message, mine_like], [VMEM] * 3)(
        act_b, near_in, away_b
    )
    got_b = shift(own_b, 1)
    total_a = shift(middle(come_a, keep_a), 1)
    total_b = shift(middle(come_b, keep_b), -1)
    grown = call(
        first_tiles_kernel,
        [canvas_like],
        [SMEM] * 2 + [VMEM] * 11,
        [pltpu.VMEM((half, share), f32)],
    )(
        offsets, tile_counts, mine_a, got_a, total_a, come_a, away_a, mixed_a, centers_a, inverses_a,
        ln_gain, taps, taken,
    )[0]
    return call(
        last_tiles_kernel,
        jax.ShapeDtypeStruct(canvas.shape, f32),
        [SMEM] * 3 + [VMEM] * 11,
        [
            pltpu.VMEM((half, share), f32),
            pltpu.VMEM((lanes, PAD_ROWS, PAD_COLS, 128), f32),
            pltpu.VMEM(canvas.shape, f32),
            pltpu.SemaphoreType.DMA((4,)),
        ],
        out_specs=HBM,
    )(
        offsets, tile_counts, screen_size, mine_b, got_b, total_b, come_b, away_b, mixed_b, centers_b, inverses_b,
        ln_gain, taps, grown,
    )


def solution(mesh):
    return jax.shard_map(
        shards,
        mesh=mesh,
        in_specs=(
            P("img", None, "ch"),
            P("img", None),
            P(),
            P("img", None),
            P("img", None, None, "ch"),
            P(None, "ch"),
            P("ch"),
            P(),
            P(),
            P(None, "ch"),
            P("ch"),
            P("ch", None),
            P(),
        ),
        out_specs=P("img", None, "ch"),
        check_vma=False,
    )
```
